128 devices in a mesh: gx: 16 (over z, x), gy: 8 (over y, core).
Axes of the slice: x: 4, y: 4, z: 4, core: 2. Of those that a mesh axis runs over, the one named last changes fastest.
Arguments:
- activations: bfloat16 [768, 14848], P('gx', 'gy'), may hold values from -6 to 6
- norm_gain: float32 [14848], P('gy'), may hold values from 0.5 to 1.5
- norm_bias: float32 [14848], P('gy'), may hold values from -3 to 3
- input_outliers: int32 [32], P('gy'), may hold values from 0 to 1855, as said below
- query_int: bfloat16 [14848, 14336], P('gy', 'gx'), may hold values from -127 to 127, as said below
- query_scale: float32 [14336], P('gx'), as said below
- keyvalue_int: bfloat16 [14848, 1024], P('gy'), may hold values from -127 to 127, as said below
- keyvalue_scale: float32 [1024], replicated, as said below
- query_float: float32 [32, 14336], P('gy', 'gx'), may hold values from -1 to 1
- keyvalue_float: float32 [32, 1024], P('gy'), may hold values from -1 to 1
- key_cache: bfloat16 [384, 2048, 512], P(('gx', 'gy')), may hold values from -80 to 80
- value_cache: bfloat16 [384, 2048, 512], P(('gx', 'gy')), may hold values from -6 to 6
- lengths: int32 [384], P(('gx', 'gy')), may hold values from 1 to 2048, as said below
- middle_outliers: int32 [64], replicated, may hold values from 0 to 895, as said below
- output_int: bfloat16 [14336, 14848], P('gx', 'gy'), may hold values from -127 to 127, as said below
- output_scale: float32 [14848], P('gy'), as said below
- output_float: float32 [64, 14848], P('gx', 'gy'), may hold values from -0.75 to 0.75
Outputs:
- attention_out: bfloat16 [768, 14848], P('gx', 'gy')
The draws below stay inside these ranges and needn't reach their ends.
Inputs may be any that keep to these rules, and one draw needn't show every extreme that they name: `input_outliers`: within each shard the 4 positions are distinct. `middle_outliers`: within each shard the 4 positions are distinct. `query_int`: Integers. `keyvalue_int`: Integers. `output_int`: Integers. `query_scale`: Positive. `keyvalue_scale`: Positive. `output_scale`: Positive. `lengths`: some request has exactly 2048 and some exactly 1.
All inputs are finite; a program needn't handle non-finite values.
Results may differ from the reference program's by a relative error of at most 0.012.
The reference program's roundings to bfloat16 on the way (of `regular`, `outlier_vals`, `queries`, `pairs` and `weights`) count: a program that leaves them out, or rounds other values in their place, can miss the bound.
Values may be sent and summed in bfloat16 or wider, within the bound.
No kernel may reach another device: no remote copies, remote signals or barrier semaphores. Data moves between devices by JAX's collectives and lax.ppermute only.
A program may use at most 128 MiB of HBM per device.

```python
import math
import jax
import jax.numpy as jnp
from jax import lax

D = 14848
HEAD = 64
KV = 8
GROUP = 28
OUTL = 4
NEW = 2
CACHE = 2048
HQ = 224
QW = 14336
KW = 512
REQS = 384
TOKENS = 768
N_GX = 16
N_GY = 8


def loguniform_draw(seed_key, extent, lowest, highest):
    return jnp.exp(jax.random.uniform(seed_key, extent, jnp.float32, math.log(lowest), math.log(highest)))


def integer_weights(seed_key, extent):
    return jax.random.randint(seed_key, extent, -127, 128).astype(jnp.float32).astype(jnp.bfloat16)


def shard_positions(seed_key, shards, within):
    keys_list = jax.random.split(seed_key, shards)

    def one_shard(shard_key):
        return jax.random.permutation(shard_key, within)[:OUTL]
    return jax.vmap(one_shard)(keys_list).reshape(-1).astype(jnp.int32)


def draw_input_outliers(key, part):
    key = jax.random.fold_in(key, 11)
    return shard_positions(key, N_GY, D // N_GY)


def draw_middle_outliers(key, part):
    key = jax.random.fold_in(key, 12)
    return shard_positions(key, N_GX, QW // N_GX)


def draw_query_int(key, part):
    key = jax.random.fold_in(key, 13)
    return integer_weights(key, (D, QW))


def draw_keyvalue_int(key, part):
    key = jax.random.fold_in(key, 14)
    return integer_weights(key, (D, 2 * KW))


def draw_output_int(key, part):
    key = jax.random.fold_in(key, 15)
    return integer_weights(key, (QW, D))


def draw_query_scale(key, part):
    key = jax.random.fold_in(key, 16)
    return loguniform_draw(key, (QW,), 0.5, 2.0) / (73.6 * math.sqrt(D))


def draw_keyvalue_scale(key, part):
    key = jax.random.fold_in(key, 17)
    return loguniform_draw(key, (2 * KW,), 0.5, 2.0) / (73.6 * math.sqrt(D))


def draw_output_scale(key, part):
    key = jax.random.fold_in(key, 18)
    return loguniform_draw(key, (D,), 0.5, 2.0) * 6.0 / (73.6 * math.sqrt(QW))


def draw_key_cache(key, part):
    key = jax.random.fold_in(key, 19)
    first_key = jax.random.fold_in(key, 0)
    return jnp.clip(jax.random.normal(first_key, (REQS, CACHE, KW), jnp.float32), -6.0, 6.0).astype(jnp.bfloat16)


def draw_lengths(key, part):
    key = jax.random.fold_in(key, 20)
    first_key, second_key, third_key, fourth_key = jax.random.split(key, 4)
    shorter = jax.random.randint(first_key, (REQS,), 1, CACHE // 4 + 1)
    longer = jax.random.randint(second_key, (REQS,), CACHE // 2, CACHE + 1)
    chosen = jax.random.randint(third_key, (REQS,), 0, 4) == 0
    filled = jnp.where(chosen, longer, shorter)
    places = jax.random.permutation(fourth_key, REQS)
    filled = filled.at[places[0]].set(CACHE).at[places[1]].set(1)
    return filled.astype(jnp.int32)


def block_scale(rng, shape, cuts, least, high):
    def one(dim, blocks):
        steps = jax.random.uniform(jax.random.fold_in(jax.random.fold_in(rng, 6), dim), (blocks,), jnp.float32, least / len(cuts), high / len(cuts))
        return jnp.repeat(jnp.exp(steps), shape[dim] // blocks).reshape((-1,) + (1,) * (len(shape) - dim - 1))

    factor_of = one(*cuts[0])
    for cut in cuts[1:]:
        factor_of = factor_of * one(*cut)
    return factor_of


def gaussian(own_key, shape, width, limit, cuts=(), kind=jnp.bfloat16):
    values = width * jax.random.normal(own_key, shape, jnp.float32)
    if cuts:
        values = values * block_scale(own_key, shape, cuts, -0.22, 0.18)
    return jnp.clip(values, -limit, limit).astype(kind)


def setup_inputs(seed: int = 0) -> dict:
    arg_keys = jax.random.split(jax.random.key(seed), 18)
    return {
        "activations": gaussian(arg_keys[0], (TOKENS, D), 1.0, 6.0, ((0, 16), (1, 8))),
        "norm_gain": jnp.clip(1.0 + 0.1 * jax.random.normal(arg_keys[1], (D,), jnp.float32), 0.5, 1.5),
        "norm_bias": gaussian(arg_keys[2], (D,), 0.5, 3.0, ((0, 8),), jnp.float32),
        "input_outliers": draw_input_outliers(jax.random.fold_in(arg_keys[17], 71), 0),
        "query_int": draw_query_int(jax.random.fold_in(arg_keys[17], 71), 0),
        "query_scale": draw_query_scale(jax.random.fold_in(arg_keys[17], 71), 0),
        "keyvalue_int": draw_keyvalue_int(jax.random.fold_in(arg_keys[17], 71), 0),
        "keyvalue_scale": draw_keyvalue_scale(jax.random.fold_in(arg_keys[17], 71), 0),
        "query_float": gaussian(arg_keys[8], (N_GY * OUTL, QW), (N_GY * OUTL) ** -0.5, 1.0, ((0, 8), (1, 16)), jnp.float32),
        "keyvalue_float": gaussian(arg_keys[9], (N_GY * OUTL, 2 * KW), (N_GY * OUTL) ** -0.5, 1.0, ((0, 8),), jnp.float32),
        "key_cache": draw_key_cache(jax.random.fold_in(arg_keys[17], 71), 0),
        "value_cache": gaussian(arg_keys[11], (REQS, CACHE, KW), 1.0, 6.0, ((0, 128),)),
        "lengths": draw_lengths(jax.random.fold_in(arg_keys[17], 71), 0),
        "middle_outliers": draw_middle_outliers(jax.random.fold_in(arg_keys[17], 71), 0),
        "output_int": draw_output_int(jax.random.fold_in(arg_keys[17], 71), 0),
        "output_scale": draw_output_scale(jax.random.fold_in(arg_keys[17], 71), 0),
        "output_float": gaussian(arg_keys[16], (N_GX * OUTL, D), (N_GX * OUTL) ** -0.5, 0.75, ((0, 16), (1, 8)), jnp.float32),
    }


epsilon = 1e-05
rope_base = 10000.0

def rotate(values, positions):
    dimension = values.shape[-1]
    halfway = dimension // 2
    frequency = jnp.exp(jnp.arange(halfway, dtype=jnp.float32) * (-2.0 * math.log(rope_base) / dimension))
    angles = positions.astype(jnp.float32)[:, :, None] * frequency[None, None, :]
    cosine = jnp.cos(angles)[:, :, None, :]
    sine_part = jnp.sin(angles)[:, :, None, :]
    leading = values[..., :halfway]
    trailing = values[..., halfway:]
    return jnp.concatenate([leading * cosine - trailing * sine_part, trailing * cosine + leading * sine_part], axis=-1)

def attend(queries, fresh_keys, fresh_values, cached_keys, cached_values, lengths):
    score_scale = 1.0 / math.sqrt(queries.shape[-1])
    window = cached_keys.shape[1]
    fresh = fresh_keys.shape[1]
    highest_prec = lax.Precision.HIGHEST
    query_wide = queries.astype(jnp.float32)
    cache_scores = jnp.einsum('rtkgd,rlkd->rkgtl', query_wide, cached_keys.astype(jnp.float32), precision=highest_prec) * score_scale
    fresh_scores = jnp.einsum('rtkgd,rukd->rkgtu', query_wide, fresh_keys.astype(jnp.float32), precision=highest_prec) * score_scale
    active = jnp.arange(window, dtype=jnp.int32)[None, :] < lengths[:, None]
    cache_scores = jnp.where(active[:, None, None, None, :], cache_scores, -jnp.inf)
    causal = jnp.arange(fresh, dtype=jnp.int32)[None, :] <= jnp.arange(fresh, dtype=jnp.int32)[:, None]
    fresh_scores = jnp.where(causal, fresh_scores, -jnp.inf)
    highest = jnp.maximum(lax.optimization_barrier(jnp.max(cache_scores, axis=-1)), lax.optimization_barrier(jnp.max(fresh_scores, axis=-1)))[..., None]
    cache_weights = jnp.exp(cache_scores - highest)
    fresh_weights = jnp.exp(fresh_scores - highest)
    denominator = lax.optimization_barrier(jnp.sum(cache_weights, axis=-1, keepdims=True)) + lax.optimization_barrier(jnp.sum(fresh_weights, axis=-1, keepdims=True))
    cache_probs = (cache_weights / denominator).astype(jnp.bfloat16)
    fresh_probs = (fresh_weights / denominator).astype(jnp.bfloat16)
    result = jnp.einsum('rkgtl,rlkd->rtkgd', cache_probs.astype(jnp.float32), cached_values.astype(jnp.float32), precision=highest_prec)
    result = result + jnp.einsum('rkgtu,rukd->rtkgd', fresh_probs.astype(jnp.float32), fresh_values.astype(jnp.float32), precision=highest_prec)
    return result.reshape(result.shape[0], result.shape[1], -1)

def reference(activations, norm_gain, norm_bias, input_outliers, query_int, query_scale, keyvalue_int, keyvalue_scale, query_float, keyvalue_float, key_cache, value_cache, lengths, middle_outliers, output_int, output_scale, output_float):
    highest_prec = lax.Precision.HIGHEST
    widened = activations.astype(jnp.float32)
    average = lax.optimization_barrier(jnp.sum(widened, axis=1)) / D
    variance = lax.optimization_barrier(jnp.sum(widened * widened, axis=1)) / D - average * average
    normed = (widened - average[:, None]) * lax.rsqrt(variance[:, None] + epsilon) * norm_gain + norm_bias
    rounded = normed.astype(jnp.bfloat16)
    input_cols = jnp.arange(N_GY * OUTL, dtype=jnp.int32) // OUTL * (D // N_GY) + input_outliers.astype(jnp.int32)
    is_outlier = jnp.any(jnp.arange(D, dtype=jnp.int32)[:, None] == input_cols[None, :], axis=1)
    regular = jnp.where(is_outlier[None, :], jnp.zeros_like(rounded), rounded)
    outlier_vals = jnp.take(rounded, input_cols, axis=1)

    def project(weights, scales, extra):
        main_part = jnp.dot(regular.astype(jnp.float32), weights.astype(jnp.float32), precision=highest_prec) * scales
        return main_part + jnp.dot(outlier_vals.astype(jnp.float32), extra, precision=highest_prec)
    queries = project(query_int, query_scale, query_float).astype(jnp.bfloat16)
    pairs = project(keyvalue_int, keyvalue_scale, keyvalue_float).astype(jnp.bfloat16)
    positions = lengths[:, None] + jnp.arange(NEW, dtype=jnp.int32)[None, :]
    query_rot = rotate(queries.astype(jnp.float32).reshape(REQS, NEW, HQ, HEAD), positions).astype(jnp.bfloat16)
    query_rot = query_rot.reshape(REQS, NEW, KV, GROUP, HEAD)
    pair_heads = pairs.reshape(REQS, NEW, 2, KV, HEAD)
    fresh_keys = rotate(pair_heads[:, :, 0].astype(jnp.float32), positions).astype(jnp.bfloat16)
    fresh_values = pair_heads[:, :, 1]

    def one_request(items):
        query_one, keys_one, values_one, cache_keys, cache_values, length_one = items
        return attend(query_one[None], keys_one[None], values_one[None], cache_keys[None], cache_values[None], length_one[None])[0]
    attended = lax.map(one_request, (query_rot, fresh_keys, fresh_values, key_cache.reshape(REQS, CACHE, KV, HEAD), value_cache.reshape(REQS, CACHE, KV, HEAD), lengths))
    attended = attended.reshape(TOKENS, QW)
    middle_cols = jnp.arange(N_GX * OUTL, dtype=jnp.int32) // OUTL * (QW // N_GX) + middle_outliers.astype(jnp.int32)
    is_middle = jnp.any(jnp.arange(QW, dtype=jnp.int32)[:, None] == middle_cols[None, :], axis=1)
    attended_round = attended.astype(jnp.bfloat16)
    middle_regular = jnp.where(is_middle[None, :], jnp.zeros_like(attended_round), attended_round)
    middle_outlier = jnp.take(attended, middle_cols, axis=1).astype(jnp.bfloat16)
    result = jnp.dot(middle_regular.astype(jnp.float32), output_int.astype(jnp.float32), precision=highest_prec) * output_scale
    result = result + jnp.dot(middle_outlier.astype(jnp.float32), output_float, precision=highest_prec)
    return result.astype(jnp.bfloat16)
```

```python
import functools
import math

import jax
import jax.numpy as jnp
from jax import lax
from jax.experimental import pallas as pl
from jax.experimental.pallas import tpu as pltpu
from jax.sharding import PartitionSpec as P

D = 14848
HEAD = 64
KV = 8
GROUP = 28
OUTL = 4
NEW = 2
N_Y = 4
LOCAL_HEADS = 14
CHUNK = 512

epsilon = 1e-05
rope_base = 10000.0
BF = jnp.bfloat16
F32 = jnp.float32
MIB = 1024 * 1024


def lanes_of(columns):
    return [(n, slice(128 * n, min(128 * n + 128, columns))) for n in range((columns + 127) // 128)]


def put(ref, rows, values):
    for n, lanes in lanes_of(values.shape[1]):
        ref[n, rows, 0 : lanes.stop - lanes.start] = values[:, lanes]


def whole(shape):
    return pl.BlockSpec(shape, lambda *_: (0,) * len(shape))


def query_kernel(
    place, x, stats, gain, bias, gain_out, bias_out, scale, extra, weight, pairs, keep, send, acc
):
    step = pl.program_id(0)
    rows = x.shape[0]
    average = stats[:, 0:1] / D
    variance = stats[:, 1:2] / D - average * average
    inverse = lax.rsqrt(variance + epsilon)
    regular = ((x[...].astype(F32) - average) * inverse * gain[...] + bias[...]).astype(BF)
    term = jnp.dot(regular, weight[...], preferred_element_type=F32) * scale[...]
    for k in range(OUTL):
        value = (stats[:, 2 + k : 3 + k] - average) * inverse * gain_out[:, k : k + 1]
        value = (value + bias_out[:, k : k + 1]).astype(BF).astype(F32)
        term = term + value * extra[k : k + 1, :]
    put(acc, pl.ds(pl.multiple_of(step * rows, rows), rows), term)

    @pl.when(step == pl.num_programs(0) - 1)
    def _():
        y = place[0]
        c = place[1]
        for out, core in ((keep, c), (send, 1 - c)):
            for d in range(N_Y):
                j = 2 * lax.rem(y + d, N_Y) + core
                for k in range(6):
                    for n, lanes in lanes_of(896):
                        out[d, 16 * k : 16 * k + 16, lanes] = acc[n, pl.ds(6 * j + k, 16, stride=48), :].astype(BF)
                out[d, 96:112, 0:512] = pairs[j].astype(BF)
                out[d, 96:112, 512:896] = jnp.zeros((16, 384), BF)


def add_kernel(keep, received, o0, o1, o2, o3):
    for d, out in enumerate((o0, o1, o2, o3)):
        out[...] = (keep[d].astype(F32) + received[d].astype(F32)).astype(BF)


def collect_kernel(a, b, c, d, query_out, pair_out, acc):
    total = (a[...].astype(F32) + b[...].astype(F32)) + (c[...].astype(F32) + d[...].astype(F32))
    put(acc, slice(0, 112), total)
    for i in range(16):
        for n, lanes in lanes_of(896):
            query_out[i, :, lanes] = acc[n, pl.ds(i, 6, stride=16), :].astype(BF)
    pair_out[...] = total[96:112, 0:512]


def rotate_lanes(values, cosine, sine):
    lane = lax.broadcasted_iota(jnp.int32, values.shape, 1)
    partner = jnp.where(
        lane % 64 < 32, pltpu.roll(values, 96, axis=1), pltpu.roll(values, 32, axis=1)
    )
    return values * cosine + partner * sine


def attend_kernel(
    lengths, queries, pairs, cosine, sine, keys, values, out,
    staged, rotated, fresh_key, fresh_value, block0, block1, result,
):
    r = pl.program_id(0)
    length = lengths[r]

    @pl.when(r == 0)
    def _():
        for i in range(16):
            put(staged, slice(8 * i, 8 * i + 6), queries[i].astype(F32))
        for k in range(6):
            for col in range(7):
                lanes = slice(128 * col, 128 * col + 128)
                part = staged[col, pl.ds(k, 16, stride=8), :]
                turned = rotate_lanes(part, cosine[k : k + 1, :], sine[k : k + 1, :])
                rotated[16 * k : 16 * k + 16, lanes] = turned.astype(BF).astype(F32) * 0.125
        fresh_key[...] = jnp.zeros_like(fresh_key)
        fresh_value[...] = jnp.zeros_like(fresh_value)
        rounded = pairs[...].astype(BF).astype(F32)
        for col in range(4):
            lanes = slice(128 * col, 128 * col + 128)
            fresh_key[0:6, lanes] = rotate_lanes(rounded[0:6, lanes], cosine[0:6, :], sine[0:6, :])
        fresh_value[0:6, :] = rounded[6:12, :]

    sub = lax.broadcasted_iota(jnp.int32, (8, 256), 0)
    lane = lax.broadcasted_iota(jnp.int32, (8, 256), 1)
    own = sub // 2 == lane // 64
    low = lax.broadcasted_iota(jnp.int32, (8, 128), 1) < 64
    for g, block in enumerate((block0, block1)):
        for t in range(NEW):
            start = pl.multiple_of((NEW * r + t) * 16 + 8 * g, 8)
            for col in range(7):
                part = rotated[pl.ds(start, 8), 128 * col : 128 * col + 128]
                other = pltpu.roll(part, 64, axis=1)
                for half in range(2):
                    both = jnp.where(low, part, other) if half == 0 else jnp.where(low, other, part)
                    both = jnp.concatenate([both, both], axis=1)
                    at = (2 * col + half) * 16 + t * 8
                    block[at : at + 8, :] = jnp.where(own, both, 0.0)

    rows = LOCAL_HEADS * 16
    nt = (((1,), (1,)), ((), ()))
    row = lax.broadcasted_iota(jnp.int32, (rows, 128), 0)
    column = lax.broadcasted_iota(jnp.int32, (rows, 128), 1)
    token = (row // 8) % 2
    visible = (column // 2 == r) & (column % 2 <= token)
    state = []
    grouped = []
    for g, block in enumerate((block0, block1)):
        side = slice(256 * g, 256 * g + 256)
        query = block[...].astype(BF)
        grouped.append(query)
        scores = lax.dot_general(query, fresh_key[:, side].astype(BF), nt, preferred_element_type=F32)
        scores = jnp.where(visible, scores, -jnp.inf)
        top = jnp.max(scores, axis=1, keepdims=True)
        prob = jnp.exp(scores - top)
        total = jnp.sum(prob, axis=1, keepdims=True)
        mixed = jnp.dot(prob.astype(BF), fresh_value[:, side].astype(BF), preferred_element_type=F32)
        state.append((top, total, mixed))

    place = lax.broadcasted_iota(jnp.int32, (rows, CHUNK), 1)

    def body(n, state):
        at = pl.multiple_of(n * CHUNK, CHUNK)
        active = place < length - at
        new = []
        for g in range(2):
            top, total, mixed = state[g]
            side = slice(256 * g, 256 * g + 256)
            key = keys[0, pl.ds(at, CHUNK), side]
            value = values[0, pl.ds(at, CHUNK), side]
            scores = lax.dot_general(grouped[g], key, nt, preferred_element_type=F32)
            scores = jnp.where(active, scores, -jnp.inf)
            higher = jnp.maximum(top, jnp.max(scores, axis=1, keepdims=True))
            shrink = jnp.exp(top - higher)
            prob = jnp.exp(scores - higher)
            total = total * shrink + jnp.sum(prob, axis=1, keepdims=True)
            mixed = mixed * shrink + jnp.dot(prob.astype(BF), value, preferred_element_type=F32)
            new.append((higher, total, mixed))
        return tuple(new)

    state = lax.fori_loop(0, (length + CHUNK - 1) // CHUNK, body, tuple(state))
    for g in range(2):
        top, total, mixed = state[g]
        block0[...] = mixed / total
        for t in range(NEW):
            start = pl.multiple_of((NEW * r + t) * 16 + 8 * g, 8)
            for col in range(7):
                folded = []
                for half in range(2):
                    at = (2 * col + half) * 16 + t * 8
                    part = jnp.where(own, block0[at : at + 8, :], 0.0)
                    part = part[:, 0:128] + part[:, 128:256]
                    folded.append(part + pltpu.roll(part, 64, axis=1))
                result[col, pl.ds(start, 8), :] = jnp.where(low, folded[0], folded[1])

    @pl.when(r == pl.num_programs(0) - 1)
    def _():
        for i in range(16):
            for n, lanes in lanes_of(896):
                out[i, :, lanes] = result[n, pl.ds(i, 6, stride=16), :].astype(BF)


def repack_kernel(block, out, staged):
    for i in range(16):
        put(staged, slice(8 * i, 8 * i + 6), block[i].astype(F32))
    for k in range(6):
        for n, lanes in lanes_of(896):
            out[16 * k : 16 * k + 16, lanes] = staged[n, pl.ds(k, 16, stride=8), :].astype(BF)


def output_kernel(place, b0, b1, b2, b3, s0, s1, s2, s3, chosen, plain, scale, extra, weight, out, left, acc):
    y = place[0]
    c = place[1]
    for blocks, core in (((b0, b1, b2, b3), c), ((s0, s1, s2, s3), 1 - c)):
        for d, block in enumerate(blocks):
            j = 2 * lax.rem(y + N_Y - d, N_Y) + core
            left[pl.ds(pl.multiple_of(96 * j, 96), 96), :] = block[...]
    step = 192
    for n in range(768 // step):
        rows = slice(n * step, n * step + step)
        part = left[rows, :]
        picked = jnp.dot(part, chosen[...], preferred_element_type=F32)
        term = jnp.dot(part * plain[...], weight[...], preferred_element_type=F32) * scale[...]
        for k in range(OUTL):
            term = term + picked[:, k : k + 1] * extra[k : k + 1, :]
        put(acc, rows, term)
    for i in range(16):
        for n, lanes in lanes_of(out.shape[2]):
            got = acc[n, pl.ds(i, 48, stride=16), :].astype(BF)
            out[i, :, lanes] = got[:, 0 : lanes.stop - lanes.start]


def total_kernel(parts, out):
    total = parts[0].astype(F32)
    for i in range(1, 16):
        total = total + parts[i].astype(F32)
    out[...] = total.astype(BF)


def params(mib=48):
    return pltpu.CompilerParams(vmem_limit_bytes=mib * MIB)


def over_y(shift):
    return [(2 * y + c, 2 * ((y + shift) % N_Y) + c) for y in range(N_Y) for c in range(2)]


SIBLING = [(j, j ^ 1) for j in range(2 * N_Y)]


def on_device(
    activations,
    norm_gain,
    norm_bias,
    input_outliers,
    query_int,
    query_scale,
    keyvalue_int,
    keyvalue_scale,
    query_float,
    keyvalue_float,
    key_cache,
    value_cache,
    lengths,
    middle_outliers,
    output_int,
    output_scale,
    output_float,
):
    block_rows, features = activations.shape
    tokens = block_rows * 16
    columns = query_int.shape[1]
    out_columns = output_int.shape[1]
    me_x = lax.axis_index("gx")
    me_y = lax.axis_index("gy")
    place = jnp.stack([me_y // 2, me_y % 2]).astype(jnp.int32)

    gathered = lax.all_gather(activations, "gx", axis=0, tiled=True)

    widened = activations.astype(F32)
    sums = lax.psum(
        jnp.stack([jnp.sum(widened, axis=1), jnp.sum(widened * widened, axis=1)], axis=1), "gy"
    )
    picked = jnp.arange(features, dtype=jnp.int32)[:, None] == input_outliers[None, :]
    raw = jnp.dot(activations, picked.astype(BF), preferred_element_type=F32)
    stats = lax.all_gather(jnp.concatenate([sums, raw], axis=1), "gx", axis=0, tiled=True)

    is_outlier = jnp.any(picked, axis=1)
    gain_regular = jnp.where(is_outlier, 0.0, norm_gain)
    bias_regular = jnp.where(is_outlier, 0.0, norm_bias)
    gain_out = jnp.sum(jnp.where(picked, norm_gain[:, None], 0.0), axis=0)
    bias_out = jnp.sum(jnp.where(picked, norm_bias[:, None], 0.0), axis=0)

    average = sums[:, 0:1] / D
    inverse = lax.rsqrt(sums[:, 1:2] / D - average * average + epsilon)
    own_regular = ((widened - average) * inverse * gain_regular + bias_regular).astype(BF)
    own_outlier = ((raw - average) * inverse * gain_out + bias_out).astype(BF)
    pairs = jnp.dot(own_regular, keyvalue_int, preferred_element_type=F32) * keyvalue_scale
    pairs = pairs + jnp.dot(own_outlier.astype(F32), keyvalue_float, precision=lax.Precision.HIGHEST)
    pairs = pairs.reshape(8, 6, 2, 512).transpose(0, 2, 1, 3).reshape(8, 12, 512)
    pairs = jnp.pad(pairs, ((0, 0), (0, 4), (0, 0)))

    part_rows = tokens // 4
    smem = pl.BlockSpec(memory_space=pltpu.SMEM)
    keep, send = pl.pallas_call(
        query_kernel,
        grid=(4,),
        in_specs=[
            smem,
            pl.BlockSpec((part_rows, features), lambda n: (n, 0)),
            pl.BlockSpec((part_rows, 6), lambda n: (n, 0)),
            whole((1, features)),
            whole((1, features)),
            whole((1, OUTL)),
            whole((1, OUTL)),
            whole((1, columns)),
            whole((OUTL, columns)),
            whole((features, columns)),
            whole((8, 16, 512)),
        ],
        out_specs=[whole((N_Y, 112, columns))] * 2,
        out_shape=[jax.ShapeDtypeStruct((N_Y, 112, columns), BF)] * 2,
        scratch_shapes=[pltpu.VMEM((7, tokens, 128), F32)],
        compiler_params=params(),
        name="query_projection",
    )(
        place, gathered, stats, gain_regular[None], bias_regular[None], gain_out[None], bias_out[None],
        query_scale[None], query_float, query_int, pairs,
    )
    received = lax.ppermute(send, "gy", SIBLING)
    piece = jax.ShapeDtypeStruct((112, columns), BF)
    mine, to1, to2, to3 = pl.pallas_call(
        add_kernel, out_shape=[piece] * 4, compiler_params=params(), name="add_cores"
    )(keep, received)
    from1 = lax.ppermute(to1, "gy", over_y(1))
    from3 = lax.ppermute(to3, "gy", over_y(3))
    from2 = lax.ppermute(to2, "gy", over_y(2))
    summed, pair_sums = pl.pallas_call(
        collect_kernel,
        out_shape=[
            jax.ShapeDtypeStruct((16, 6, columns), BF),
            jax.ShapeDtypeStruct((16, 512), F32),
        ],
        scratch_shapes=[pltpu.VMEM((7, 112, 128), F32)],
        compiler_params=params(),
        name="collect",
    )(mine, from1, from2, from3)
    queries = lax.all_to_all(summed, "gx", split_axis=0, concat_axis=0, tiled=True)

    positions = (lengths[:, None] + jnp.arange(NEW, dtype=jnp.int32)[None, :]).reshape(6, 1)
    frequency = jnp.exp(jnp.arange(32, dtype=F32) * (-2.0 * math.log(rope_base) / HEAD))
    angles = positions.astype(F32) * frequency[None, :]
    cosine = jnp.tile(jnp.cos(angles), (1, 4))
    sine = jnp.sin(angles)
    sine = jnp.concatenate([-sine, sine, -sine, sine], axis=1)
    cosine = jnp.pad(cosine, ((0, 2), (0, 0)))
    sine = jnp.pad(sine, ((0, 2), (0, 0)))

    window = key_cache.shape[1]
    attended = pl.pallas_call(
        attend_kernel,
        grid=(3,),
        in_specs=[
            smem,
            whole((16, 6, columns)),
            whole((16, 512)),
            whole((8, 128)),
            whole((8, 128)),
            pl.BlockSpec((1, window, 512), lambda n: (n, 0, 0)),
            pl.BlockSpec((1, window, 512), lambda n: (n, 0, 0)),
        ],
        out_specs=whole((16, 6, columns)),
        out_shape=jax.ShapeDtypeStruct((16, 6, columns), BF),
        scratch_shapes=[
            pltpu.VMEM((7, 128, 128), F32),
            pltpu.VMEM((96, columns), F32),
            pltpu.VMEM((128, 512), F32),
            pltpu.VMEM((128, 512), F32),
            pltpu.VMEM((224, 256), F32),
            pltpu.VMEM((224, 256), F32),
            pltpu.VMEM((7, 96, 128), F32),
        ],
        compiler_params=params(),
        name="attention",
    )(lengths, queries, pair_sums, cosine, sine, key_cache, value_cache)

    back = lax.all_to_all(attended, "gx", split_axis=0, concat_axis=0, tiled=True)
    mine = pl.pallas_call(
        repack_kernel,
        out_shape=jax.ShapeDtypeStruct((96, columns), BF),
        scratch_shapes=[pltpu.VMEM((7, 128, 128), F32)],
        compiler_params=params(),
        name="repack",
    )(back)
    blocks = [mine] + [lax.ppermute(mine, "gy", over_y(d)) for d in (1, 2, 3)]
    blocks = blocks + [lax.ppermute(b, "gy", SIBLING) for b in blocks]

    middle = lax.dynamic_slice(middle_outliers, (me_x * OUTL,), (OUTL,))
    chosen = jnp.arange(columns, dtype=jnp.int32)[:, None] == middle[None, :]
    plain = jnp.where(jnp.any(chosen, axis=1), 0.0, 1.0).astype(BF)[None]
    chosen = jnp.pad(chosen.astype(BF), ((0, 0), (0, 128 - OUTL)))
    vmem = pl.BlockSpec(memory_space=pltpu.VMEM)
    partial = pl.pallas_call(
        output_kernel,
        in_specs=[smem] + [vmem] * 13,
        out_specs=vmem,
        out_shape=jax.ShapeDtypeStruct((16, block_rows, out_columns), BF),
        scratch_shapes=[pltpu.VMEM((tokens, columns), BF), pltpu.VMEM((15, tokens, 128), F32)],
        compiler_params=params(),
        name="output_projection",
    )(place, *blocks, chosen, plain, output_scale[None], output_float, output_int)
    parts = lax.all_to_all(partial, "gx", split_axis=0, concat_axis=0, tiled=True)
    return pl.pallas_call(
        total_kernel,
        out_shape=jax.ShapeDtypeStruct((block_rows, out_columns), BF),
        compiler_params=params(),
        name="total",
    )(parts)


def solution(mesh):
    placed = (
        P("gx", "gy"),
        P("gy"),
        P("gy"),
        P("gy"),
        P("gy", "gx"),
        P("gx"),
        P("gy", None),
        P(),
        P("gy", "gx"),
        P("gy", None),
        P(("gx", "gy"), None, None),
        P(("gx", "gy"), None, None),
        P(("gx", "gy")),
        P(),
        P("gx", "gy"),
        P("gy"),
        P("gx", "gy"),
    )
    return jax.shard_map(
        on_device, mesh=mesh, in_specs=placed, out_specs=P("gx", "gy"), check_vma=False
    )
```

```python
import functools
import math

import jax
import jax.numpy as jnp
from jax import lax
from jax.experimental import pallas as pl
from jax.experimental.pallas import tpu as pltpu
from jax.sharding import PartitionSpec as P

D = 14848
HEAD = 64
KV = 8
GROUP = 28
OUTL = 4
NEW = 2
N_Y = 4
LOCAL_HEADS = 14
CHUNK = 512

epsilon = 1e-05
rope_base = 10000.0
BF = jnp.bfloat16
F32 = jnp.float32
MIB = 1024 * 1024
STEPS = (0, 1, 3, 2)
NT = (((1,), (1,)), ((), ()))


def lanes_of(columns):
    return [(n, slice(128 * n, min(128 * n + 128, columns))) for n in range((columns + 127) // 128)]


def put(ref, rows, values):
    for n, lanes in lanes_of(values.shape[1]):
        ref[n, rows, 0 : lanes.stop - lanes.start] = values[:, lanes]


def whole(shape):
    return pl.BlockSpec(shape, lambda *_: (0,) * len(shape))


def normalize_kernel(place, parts, x, gain, bias, picked, plain, own, keep, send):
    sums = jnp.sum(parts[...], axis=0)
    rows = x.shape[0]
    unit = lax.broadcasted_iota(jnp.int32, (rows, rows), 0) == lax.broadcasted_iota(jnp.int32, (rows, rows), 1)
    sums = lax.dot_general(
        unit.astype(F32), sums, NT, precision=lax.Precision.HIGHEST, preferred_element_type=F32
    )
    average = sums[:, 0:1] / D
    variance = sums[:, 1:2] / D - average * average
    normed = (x[...].astype(F32) - average) * lax.rsqrt(variance + epsilon) * gain[...] + bias[...]
    rounded = normed.astype(BF)
    outlier = jnp.dot(rounded, picked[...], preferred_element_type=F32)
    regular = rounded.astype(F32) * plain[...]
    features = x.shape[1]
    own[:, 0:features] = regular.astype(BF)
    own[:, features:] = outlier[:, 0:64].astype(BF)
    half = rows // 2
    first = place[1] == 0
    for out, flag in ((keep, first), (send, jnp.logical_not(first))):
        out[:, 0:features] = jnp.where(flag, regular[0:half], regular[half:]).astype(BF)
        out[:, features:] = jnp.where(flag, outlier[0:half, 0:64], outlier[half:, 0:64]).astype(BF)


def query_kernel(
    place, a0, a1, a2, a3, b0, b1, b2, b3, scale, extra, weight, pairs, keep, send, acc
):
    y = place[0]
    c = place[1]
    z = place[2]
    x = place[3]
    features = weight.shape[0]
    for d2, (near, far) in enumerate(((a0, b0), (a1, b1), (a2, b2), (a3, b3))):
        rows = jnp.concatenate([near[0], far[...]], axis=0)
        term = jnp.dot(rows[:, 0:features], weight[...], preferred_element_type=F32) * scale[...]
        value = rows[:, features:].astype(F32)
        for k in range(OUTL):
            term = term + value[:, k : k + 1] * extra[k : k + 1, :]
        for side in range(2):
            half = c if side == 0 else 1 - c
            for d1 in range(4):
                along_x = lax.rem(x + 4 - jnp.where(half == 0, STEPS[d1], d2), 4)
                along_z = lax.rem(z + 4 - jnp.where(half == 0, d2, STEPS[d1]), 4)
                at = pl.multiple_of((along_z * 4 + along_x) * 48 + half * 24, 8)
                row = side * 96 + d1 * 24
                put(acc, pl.ds(at, 24), term[row : row + 24, :])
    for out, core in ((keep, c), (send, 1 - c)):
        for d in range(N_Y):
            j = 2 * lax.rem(y + d, N_Y) + core
            for k in range(6):
                for n, lanes in lanes_of(896):
                    out[d, 16 * k : 16 * k + 16, lanes] = acc[n, pl.ds(6 * j + k, 16, stride=48), :].astype(BF)
            out[d, 96:112, 0:512] = pairs[j].astype(BF)
            out[d, 96:112, 512:896] = jnp.zeros((16, 384), BF)


def add_kernel(keep, received, o0, o1, o2, o3):
    for d, out in enumerate((o0, o1, o2, o3)):
        out[...] = (keep[d].astype(F32) + received[d].astype(F32)).astype(BF)


def collect_kernel(a, b, c, d, query_out, pair_out, acc):
    total = (a[...].astype(F32) + b[...].astype(F32)) + (c[...].astype(F32) + d[...].astype(F32))
    put(acc, slice(0, 112), total)
    for i in range(16):
        for n, lanes in lanes_of(896):
            query_out[i, :, lanes] = acc[n, pl.ds(i, 6, stride=16), :].astype(BF)
    pair_out[...] = total[96:112, 0:512]


def rotate_lanes(values, cosine, sine):
    lane = lax.broadcasted_iota(jnp.int32, values.shape, 1)
    partner = jnp.where(
        lane % 64 < 32, pltpu.roll(values, 96, axis=1), pltpu.roll(values, 32, axis=1)
    )
    return values * cosine + partner * sine


def attend_kernel(
    lengths, queries, pairs, cosine, sine, keys, values, out,
    staged, rotated, fresh_key, fresh_value, block0, block1, result,
):
    r = pl.program_id(0)
    length = lengths[r]

    @pl.when(r == 0)
    def _():
        for i in range(16):
            put(staged, slice(8 * i, 8 * i + 6), queries[i].astype(F32))
        for k in range(6):
            for col in range(7):
                lanes = slice(128 * col, 128 * col + 128)
                part = staged[col, pl.ds(k, 16, stride=8), :]
                turned = rotate_lanes(part, cosine[k : k + 1, :], sine[k : k + 1, :])
                rotated[16 * k : 16 * k + 16, lanes] = turned.astype(BF).astype(F32) * 0.125
        fresh_key[...] = jnp.zeros_like(fresh_key)
        fresh_value[...] = jnp.zeros_like(fresh_value)
        rounded = pairs[...].astype(BF).astype(F32)
        for col in range(4):
            lanes = slice(128 * col, 128 * col + 128)
            fresh_key[0:6, lanes] = rotate_lanes(rounded[0:6, lanes], cosine[0:6, :], sine[0:6, :])
        fresh_value[0:6, :] = rounded[6:12, :]

    sub = lax.broadcasted_iota(jnp.int32, (8, 256), 0)
    lane = lax.broadcasted_iota(jnp.int32, (8, 256), 1)
    own = sub // 2 == lane // 64
    low = lax.broadcasted_iota(jnp.int32, (8, 128), 1) < 64
    for g, block in enumerate((block0, block1)):
        for t in range(NEW):
            start = pl.multiple_of((NEW * r + t) * 16 + 8 * g, 8)
            for col in range(7):
                part = rotated[pl.ds(start, 8), 128 * col : 128 * col + 128]
                other = pltpu.roll(part, 64, axis=1)
                for half in range(2):
                    both = jnp.where(low, part, other) if half == 0 else jnp.where(low, other, part)
                    both = jnp.concatenate([both, both], axis=1)
                    at = (2 * col + half) * 16 + t * 8
                    block[at : at + 8, :] = jnp.where(own, both, 0.0)

    rows = LOCAL_HEADS * 16
    row = lax.broadcasted_iota(jnp.int32, (rows, 128), 0)
    column = lax.broadcasted_iota(jnp.int32, (rows, 128), 1)
    token = (row // 8) % 2
    visible = (column // 2 == r) & (column % 2 <= token)
    state = []
    grouped = []
    for g, block in enumerate((block0, block1)):
        side = slice(256 * g, 256 * g + 256)
        query = block[...].astype(BF)
        grouped.append(query)
        scores = lax.dot_general(query, fresh_key[:, side].astype(BF), NT, preferred_element_type=F32)
        scores = jnp.where(visible, scores, -jnp.inf)
        top = jnp.max(scores, axis=1, keepdims=True)
        prob = jnp.exp(scores - top)
        total = jnp.sum(prob, axis=1, keepdims=True)
        mixed = jnp.dot(prob.astype(BF), fresh_value[:, side].astype(BF), preferred_element_type=F32)
        state.append((top, total, mixed))

    place = lax.broadcasted_iota(jnp.int32, (rows, CHUNK), 1)

    def body(n, state):
        at = pl.multiple_of(n * CHUNK, CHUNK)
        active = place < length - at
        new = []
        for g in range(2):
            top, total, mixed = state[g]
            side = slice(256 * g, 256 * g + 256)
            key = keys[0, pl.ds(at, CHUNK), side]
            value = values[0, pl.ds(at, CHUNK), side]
            scores = lax.dot_general(grouped[g], key, NT, preferred_element_type=F32)
            scores = jnp.where(active, scores, -jnp.inf)
            higher = jnp.maximum(top, jnp.max(scores, axis=1, keepdims=True))
            shrink = jnp.exp(top - higher)
            prob = jnp.exp(scores - higher)
            total = total * shrink + jnp.sum(prob, axis=1, keepdims=True)
            mixed = mixed * shrink + jnp.dot(prob.astype(BF), value, preferred_element_type=F32)
            new.append((higher, total, mixed))
        return tuple(new)

    state = lax.fori_loop(0, (length + CHUNK - 1) // CHUNK, body, tuple(state))
    for g in range(2):
        top, total, mixed = state[g]
        block0[...] = mixed / total
        for t in range(NEW):
            start = pl.multiple_of((NEW * r + t) * 16 + 8 * g, 8)
            for col in range(7):
                folded = []
                for half in range(2):
                    at = (2 * col + half) * 16 + t * 8
                    part = jnp.where(own, block0[at : at + 8, :], 0.0)
                    part = part[:, 0:128] + part[:, 128:256]
                    folded.append(part + pltpu.roll(part, 64, axis=1))
                result[col, pl.ds(start, 8), :] = jnp.where(low, folded[0], folded[1])

    @pl.when(r == pl.num_programs(0) - 1)
    def _():
        for i in range(16):
            for n, lanes in lanes_of(896):
                out[i, :, lanes] = result[n, pl.ds(i, 6, stride=16), :].astype(BF)


def repack_kernel(block, out, staged):
    for i in range(16):
        put(staged, slice(8 * i, 8 * i + 6), block[i].astype(F32))
    for k in range(6):
        for n, lanes in lanes_of(896):
            out[16 * k : 16 * k + 16, lanes] = staged[n, pl.ds(k, 16, stride=8), :].astype(BF)


def output_kernel(place, b0, b1, b2, b3, s0, s1, s2, s3, chosen, plain, scale, extra, weight, out, left, acc):
    y = place[0]
    c = place[1]
    for blocks, core in (((b0, b1, b2, b3), c), ((s0, s1, s2, s3), 1 - c)):
        for d, block in enumerate(blocks):
            j = 2 * lax.rem(y + N_Y - d, N_Y) + core
            left[pl.ds(pl.multiple_of(96 * j, 96), 96), :] = block[...]
    step = 192
    for n in range(768 // step):
        rows = slice(n * step, n * step + step)
        part = left[rows, :]
        picked = jnp.dot(part, chosen[...], preferred_element_type=F32)
        term = lax.dot_general(part * plain[...], weight[...], NT, preferred_element_type=F32) * scale[...]
        for k in range(OUTL):
            term = term + picked[:, k : k + 1] * extra[k : k + 1, :]
        put(acc, rows, term)
    for i in range(16):
        for n, lanes in lanes_of(out.shape[2]):
            got = acc[n, pl.ds(i, 48, stride=16), :].astype(BF)
            out[i, :, lanes] = got[:, 0 : lanes.stop - lanes.start]


def total_kernel(parts, out):
    total = parts[0].astype(F32)
    for i in range(1, 16):
        total = total + parts[i].astype(F32)
    out[...] = total.astype(BF)


def params(mib=48):
    return pltpu.CompilerParams(vmem_limit_bytes=mib * MIB)


def over_y(shift):
    return [(2 * y + c, 2 * ((y + shift) % N_Y) + c) for y in range(N_Y) for c in range(2)]


def shift_plane(first, shift):
    pairs = []
    for z in range(4):
        for x in range(4):
            for j in range(2 * N_Y):
                if (j % 2 == 0) == first:
                    to = z * 4 + (x + shift) % 4
                else:
                    to = (z + shift) % 4 * 4 + x
                pairs.append(((z * 4 + x) * 2 * N_Y + j, to * 2 * N_Y + j))
    return pairs


SIBLING = [(j, j ^ 1) for j in range(2 * N_Y)]


def on_device(
    activations,
    norm_gain,
    norm_bias,
    input_outliers,
    query_int,
    query_scale,
    keyvalue_int,
    keyvalue_scale,
    query_float,
    keyvalue_float,
    key_cache,
    value_cache,
    lengths,
    middle_outliers,
    output_int,
    output_scale,
    output_float,
):
    block_rows, features = activations.shape
    tokens = block_rows * 16
    columns = query_int.shape[1]
    out_columns = output_int.shape[1]
    me_x = lax.axis_index("gx")
    me_y = lax.axis_index("gy")
    place = jnp.stack([me_y // 2, me_y % 2, me_x // 4, me_x % 4]).astype(jnp.int32)
    smem = pl.BlockSpec(memory_space=pltpu.SMEM)
    vmem = pl.BlockSpec(memory_space=pltpu.VMEM)

    widened = activations.astype(F32)
    sums = jnp.stack([jnp.sum(widened, axis=1), jnp.sum(widened * widened, axis=1)])
    sums = lax.all_to_all(
        jnp.broadcast_to(sums[None], (2 * N_Y, 2, block_rows)), "gy", split_axis=0, concat_axis=0, tiled=True
    )
    picked = jnp.arange(features, dtype=jnp.int32)[:, None] == input_outliers[None, :]
    regular = jnp.where(jnp.any(picked, axis=1), 0.0, 1.0)[None]
    padded = features + 64
    own, kept, sent = pl.pallas_call(
        normalize_kernel,
        in_specs=[smem] + [vmem] * 6,
        out_specs=[vmem] * 3,
        out_shape=[
            jax.ShapeDtypeStruct((block_rows, padded), BF),
            jax.ShapeDtypeStruct((block_rows // 2, padded), BF),
            jax.ShapeDtypeStruct((block_rows // 2, padded), BF),
        ],
        compiler_params=params(),
        name="normalize",
    )(
        place, sums, activations, norm_gain[None], norm_bias[None],
        jnp.pad(picked.astype(BF), ((0, 0), (0, 128 - OUTL))), regular,
    )
    plane = ("gx", "gy")
    both = jnp.stack([kept, lax.ppermute(sent, "gy", SIBLING)])
    both = jnp.concatenate(
        [both] + [lax.ppermute(both, plane, shift_plane(True, d)) for d in (1, 3, 2)], axis=1
    )
    arrived = [both] + [lax.ppermute(both, plane, shift_plane(False, d)) for d in (1, 3, 2)]
    others = [lax.ppermute(block[1], "gy", SIBLING) for block in arrived]
    order = (0, 1, 3, 2)
    arrived = [arrived[n] for n in order]
    others = [others[n] for n in order]

    pairs = jnp.dot(own[:, 0:features], keyvalue_int, preferred_element_type=F32) * keyvalue_scale
    own_outlier = own[:, features : features + OUTL].astype(F32)
    pairs = pairs + jnp.dot(own_outlier, keyvalue_float, precision=lax.Precision.HIGHEST)
    pairs = pairs.reshape(8, 6, 2, 512).transpose(0, 2, 1, 3).reshape(8, 12, 512)
    pairs = jnp.pad(pairs, ((0, 0), (0, 4), (0, 0)))

    keep, send = pl.pallas_call(
        query_kernel,
        grid=(1,),
        in_specs=[smem] + [whole((1, 96, padded))] * 4 + [vmem] * 8,
        out_specs=[vmem] * 2,
        out_shape=[jax.ShapeDtypeStruct((N_Y, 112, columns), BF)] * 2,
        scratch_shapes=[pltpu.VMEM((7, tokens, 128), F32)],
        compiler_params=params(),
        name="query_projection",
    )(place, *arrived, *others, query_scale[None], query_float, query_int, pairs)
    received = lax.ppermute(send, "gy", SIBLING)
    piece = jax.ShapeDtypeStruct((112, columns), BF)
    mine, to1, to2, to3 = pl.pallas_call(
        add_kernel, out_shape=[piece] * 4, compiler_params=params(), name="add_cores"
    )(keep, received)
    from1 = lax.ppermute(to1, "gy", over_y(1))
    from3 = lax.ppermute(to3, "gy", over_y(3))
    from2 = lax.ppermute(to2, "gy", over_y(2))
    summed, pair_sums = pl.pallas_call(
        collect_kernel,
        out_shape=[
            jax.ShapeDtypeStruct((16, 6, columns), BF),
            jax.ShapeDtypeStruct((16, 512), F32),
        ],
        scratch_shapes=[pltpu.VMEM((7, 112, 128), F32)],
        compiler_params=params(),
        name="collect",
    )(mine, from1, from2, from3)
    queries = lax.all_to_all(summed, "gx", split_axis=0, concat_axis=0, tiled=True)

    positions = (lengths[:, None] + jnp.arange(NEW, dtype=jnp.int32)[None, :]).reshape(6, 1)
    frequency = jnp.exp(jnp.arange(32, dtype=F32) * (-2.0 * math.log(rope_base) / HEAD))
    angles = positions.astype(F32) * frequency[None, :]
    cosine = jnp.tile(jnp.cos(angles), (1, 4))
    sine = jnp.sin(angles)
    sine = jnp.concatenate([-sine, sine, -sine, sine], axis=1)
    cosine = jnp.pad(cosine, ((0, 2), (0, 0)))
    sine = jnp.pad(sine, ((0, 2), (0, 0)))

    window = key_cache.shape[1]
    attended = pl.pallas_call(
        attend_kernel,
        grid=(3,),
        in_specs=[
            smem,
            whole((16, 6, columns)),
            whole((16, 512)),
            whole((8, 128)),
            whole((8, 128)),
            pl.BlockSpec((1, window, 512), lambda n: (n, 0, 0)),
            pl.BlockSpec((1, window, 512), lambda n: (n, 0, 0)),
        ],
        out_specs=whole((16, 6, columns)),
        out_shape=jax.ShapeDtypeStruct((16, 6, columns), BF),
        scratch_shapes=[
            pltpu.VMEM((7, 128, 128), F32),
            pltpu.VMEM((96, columns), F32),
            pltpu.VMEM((128, 512), F32),
            pltpu.VMEM((128, 512), F32),
            pltpu.VMEM((224, 256), F32),
            pltpu.VMEM((224, 256), F32),
            pltpu.VMEM((7, 96, 128), F32),
        ],
        compiler_params=params(),
        name="attention",
    )(lengths, queries, pair_sums, cosine, sine, key_cache, value_cache)

    back = lax.all_to_all(attended, "gx", split_axis=0, concat_axis=0, tiled=True)
    mine = pl.pallas_call(
        repack_kernel,
        out_shape=jax.ShapeDtypeStruct((96, columns), BF),
        scratch_shapes=[pltpu.VMEM((7, 128, 128), F32)],
        compiler_params=params(),
        name="repack",
    )(back)
    blocks = [mine] + [lax.ppermute(mine, "gy", over_y(d)) for d in (1, 2, 3)]
    blocks = blocks + [lax.ppermute(b, "gy", SIBLING) for b in blocks]

    middle = lax.dynamic_slice(middle_outliers, (me_x * OUTL,), (OUTL,))
    chosen = jnp.arange(columns, dtype=jnp.int32)[:, None] == middle[None, :]
    plain = jnp.where(jnp.any(chosen, axis=1), 0.0, 1.0).astype(BF)[None]
    chosen = jnp.pad(chosen.astype(BF), ((0, 0), (0, 128 - OUTL)))
    partial = pl.pallas_call(
        output_kernel,
        in_specs=[smem] + [vmem] * 13,
        out_specs=vmem,
        out_shape=jax.ShapeDtypeStruct((16, block_rows, out_columns), BF),
        scratch_shapes=[pltpu.VMEM((tokens, columns), BF), pltpu.VMEM((15, tokens, 128), F32)],
        compiler_params=params(),
        name="output_projection",
    )(place, *blocks, chosen, plain, output_scale[None], output_float, output_int.T)
    parts = lax.all_to_all(partial, "gx", split_axis=0, concat_axis=0, tiled=True)
    return pl.pallas_call(
        total_kernel,
        out_shape=jax.ShapeDtypeStruct((block_rows, out_columns), BF),
        compiler_params=params(),
        name="total",
    )(parts)


def solution(mesh):
    placed = (
        P("gx", "gy"),
        P("gy"),
        P("gy"),
        P("gy"),
        P("gy", "gx"),
        P("gx"),
        P("gy", None),
        P(),
        P("gy", "gx"),
        P("gy", None),
        P(("gx", "gy"), None, None),
        P(("gx", "gy"), None, None),
        P(("gx", "gy")),
        P(),
        P("gx", "gy"),
        P("gy"),
        P("gx", "gy"),
    )
    return jax.shard_map(
        on_device, mesh=mesh, in_specs=placed, out_specs=P("gx", "gy"), check_vma=False
    )
```

```python
import functools
import math

import jax
import jax.numpy as jnp
from jax import lax
from jax.experimental import pallas as pl
from jax.experimental.pallas import tpu as pltpu
from jax.sharding import PartitionSpec as P

D = 14848
HEAD = 64
KV = 8
GROUP = 28
OUTL = 4
NEW = 2
N_Y = 4
LOCAL_HEADS = 14
CHUNK = 512

epsilon = 1e-05
rope_base = 10000.0
BF = jnp.bfloat16
F32 = jnp.float32
MIB = 1024 * 1024
STEPS = (0, 1, 3, 2)
NT = (((1,), (1,)), ((), ()))


def lanes_of(columns):
    return [(n, slice(128 * n, min(128 * n + 128, columns))) for n in range((columns + 127) // 128)]


def put(ref, rows, values):
    for n, lanes in lanes_of(values.shape[1]):
        ref[n, rows, 0 : lanes.stop - lanes.start] = values[:, lanes]


def whole(shape):
    return pl.BlockSpec(shape, lambda *_: (0,) * len(shape))


def normalize_kernel(place, parts, x, gain, bias, picked, plain, own, keep, send):
    sums = jnp.sum(parts[...], axis=0)
    rows = x.shape[0]
    unit = lax.broadcasted_iota(jnp.int32, (rows, rows), 0) == lax.broadcasted_iota(jnp.int32, (rows, rows), 1)
    sums = lax.dot_general(
        unit.astype(F32), sums, NT, precision=lax.Precision.HIGHEST, preferred_element_type=F32
    )
    average = sums[:, 0:1] / D
    variance = sums[:, 1:2] / D - average * average
    normed = (x[...].astype(F32) - average) * lax.rsqrt(variance + epsilon) * gain[...] + bias[...]
    rounded = normed.astype(BF)
    outlier = jnp.dot(rounded, picked[...], preferred_element_type=F32)
    regular = rounded.astype(F32) * plain[...]
    features = x.shape[1]
    own[:, 0:features] = regular.astype(BF)
    own[:, features:] = outlier[:, 0:64].astype(BF)
    half = rows // 2
    first = place[1] == 0
    for out, flag in ((keep, first), (send, jnp.logical_not(first))):
        out[:, 0:features] = jnp.where(flag, regular[0:half], regular[half:]).astype(BF)
        out[:, features:] = jnp.where(flag, outlier[0:half, 0:64], outlier[half:, 0:64]).astype(BF)


def pair_kernel(own, scale, extra, weight, out):
    features = weight.shape[0]
    term = jnp.dot(own[:, 0:features], weight[...], preferred_element_type=F32) * scale[...]
    value = own[:, features:].astype(F32)
    for k in range(OUTL):
        term = term + value[:, k : k + 1] * extra[k : k + 1, :]
    for j in range(2 * N_Y):
        rows = slice(6 * j, 6 * j + 6)
        out[j, 0:6, :] = term[rows, 0:512]
        out[j, 6:12, :] = term[rows, 512:1024]
        out[j, 12:16, :] = jnp.zeros((4, 512), F32)


def query_kernel(
    place, a0, a1, a2, a3, b0, b1, b2, b3, scale, extra, weight, pairs, keep, send, acc
):
    y = place[0]
    c = place[1]
    z = place[2]
    x = place[3]
    features = weight.shape[0]
    for d2, (near, far) in enumerate(((a0, b0), (a1, b1), (a2, b2), (a3, b3))):
        rows = jnp.concatenate([near[0], far[...]], axis=0)
        term = jnp.dot(rows[:, 0:features], weight[...], preferred_element_type=F32) * scale[...]
        value = rows[:, features:].astype(F32)
        for k in range(OUTL):
            term = term + value[:, k : k + 1] * extra[k : k + 1, :]
        for side in range(2):
            half = c if side == 0 else 1 - c
            for d1 in range(4):
                along_x = lax.rem(x + 4 - jnp.where(half == 0, STEPS[d1], d2), 4)
                along_z = lax.rem(z + 4 - jnp.where(half == 0, d2, STEPS[d1]), 4)
                at = pl.multiple_of((along_z * 4 + along_x) * 48 + half * 24, 8)
                row = side * 96 + d1 * 24
                put(acc, pl.ds(at, 24), term[row : row + 24, :])
    for out, core in ((keep, c), (send, 1 - c)):
        for d in range(N_Y):
            j = 2 * lax.rem(y + d, N_Y) + core
            for k in range(6):
                for n, lanes in lanes_of(896):
                    out[d, 16 * k : 16 * k + 16, lanes] = acc[n, pl.ds(6 * j + k, 16, stride=48), :].astype(BF)
            out[d, 96:112, 0:512] = pairs[j].astype(BF)
            out[d, 96:112, 512:896] = jnp.zeros((16, 384), BF)


def add_kernel(keep, received, o0, o1, o2, o3):
    for d, out in enumerate((o0, o1, o2, o3)):
        out[...] = (keep[d].astype(F32) + received[d].astype(F32)).astype(BF)


def collect_kernel(a, b, c, d, query_out, pair_out, acc):
    total = (a[...].astype(F32) + b[...].astype(F32)) + (c[...].astype(F32) + d[...].astype(F32))
    put(acc, slice(0, 112), total)
    for i in range(16):
        for n, lanes in lanes_of(896):
            query_out[i, :, lanes] = acc[n, pl.ds(i, 6, stride=16), :].astype(BF)
    pair_out[...] = total[96:112, 0:512]


def rotate_lanes(values, cosine, sine):
    lane = lax.broadcasted_iota(jnp.int32, values.shape, 1)
    partner = jnp.where(
        lane % 64 < 32, pltpu.roll(values, 96, axis=1), pltpu.roll(values, 32, axis=1)
    )
    return values * cosine + partner * sine


def attend_kernel(
    lengths, queries, pairs, cosine, sine, keys, values, out,
    staged, rotated, fresh_key, fresh_value, block0, block1, result,
):
    r = pl.program_id(0)
    length = lengths[r]

    @pl.when(r == 0)
    def _():
        for i in range(16):
            put(staged, slice(8 * i, 8 * i + 6), queries[i].astype(F32))
        for k in range(6):
            for col in range(7):
                lanes = slice(128 * col, 128 * col + 128)
                part = staged[col, pl.ds(k, 16, stride=8), :]
                turned = rotate_lanes(part, cosine[k : k + 1, :], sine[k : k + 1, :])
                rotated[16 * k : 16 * k + 16, lanes] = turned.astype(BF).astype(F32) * 0.125
        fresh_key[...] = jnp.zeros_like(fresh_key)
        fresh_value[...] = jnp.zeros_like(fresh_value)
        rounded = pairs[...].astype(BF).astype(F32)
        for col in range(4):
            lanes = slice(128 * col, 128 * col + 128)
            fresh_key[0:6, lanes] = rotate_lanes(rounded[0:6, lanes], cosine[0:6, :], sine[0:6, :])
        fresh_value[0:6, :] = rounded[6:12, :]

    sub = lax.broadcasted_iota(jnp.int32, (8, 256), 0)
    lane = lax.broadcasted_iota(jnp.int32, (8, 256), 1)
    own = sub // 2 == lane // 64
    low = lax.broadcasted_iota(jnp.int32, (8, 128), 1) < 64
    for g, block in enumerate((block0, block1)):
        for t in range(NEW):
            start = pl.multiple_of((NEW * r + t) * 16 + 8 * g, 8)
            for col in range(7):
                part = rotated[pl.ds(start, 8), 128 * col : 128 * col + 128]
                other = pltpu.roll(part, 64, axis=1)
                for half in range(2):
                    both = jnp.where(low, part, other) if half == 0 else jnp.where(low, other, part)
                    both = jnp.concatenate([both, both], axis=1)
                    at = (2 * col + half) * 16 + t * 8
                    block[at : at + 8, :] = jnp.where(own, both, 0.0)

    rows = LOCAL_HEADS * 16
    row = lax.broadcasted_iota(jnp.int32, (rows, 128), 0)
    column = lax.broadcasted_iota(jnp.int32, (rows, 128), 1)
    token = (row // 8) % 2
    visible = (column // 2 == r) & (column % 2 <= token)
    state = []
    grouped = []
    for g, block in enumerate((block0, block1)):
        side = slice(256 * g, 256 * g + 256)
        query = block[...].astype(BF)
        grouped.append(query)
        scores = lax.dot_general(query, fresh_key[:, side].astype(BF), NT, preferred_element_type=F32)
        scores = jnp.where(visible, scores, -jnp.inf)
        top = jnp.max(scores, axis=1, keepdims=True)
        prob = jnp.exp(scores - top)
        total = jnp.sum(prob, axis=1, keepdims=True)
        mixed = jnp.dot(prob.astype(BF), fresh_value[:, side].astype(BF), preferred_element_type=F32)
        state.append((top, total, mixed))

    place = lax.broadcasted_iota(jnp.int32, (rows, CHUNK), 1)

    def body(n, state):
        at = pl.multiple_of(n * CHUNK, CHUNK)
        active = place < length - at
        new = []
        for g in range(2):
            top, total, mixed = state[g]
            side = slice(256 * g, 256 * g + 256)
            key = keys[0, pl.ds(at, CHUNK), side]
            value = values[0, pl.ds(at, CHUNK), side]
            scores = lax.dot_general(grouped[g], key, NT, preferred_element_type=F32)
            scores = jnp.where(active, scores, -jnp.inf)
            higher = jnp.maximum(top, jnp.max(scores, axis=1, keepdims=True))
            shrink = jnp.exp(top - higher)
            prob = jnp.exp(scores - higher)
            total = total * shrink + jnp.sum(prob, axis=1, keepdims=True)
            mixed = mixed * shrink + jnp.dot(prob.astype(BF), value, preferred_element_type=F32)
            new.append((higher, total, mixed))
        return tuple(new)

    state = lax.fori_loop(0, (length + CHUNK - 1) // CHUNK, body, tuple(state))
    for g in range(2):
        top, total, mixed = state[g]
        block0[...] = mixed / total
        for t in range(NEW):
            start = pl.multiple_of((NEW * r + t) * 16 + 8 * g, 8)
            for col in range(7):
                folded = []
                for half in range(2):
                    at = (2 * col + half) * 16 + t * 8
                    part = jnp.where(own, block0[at : at + 8, :], 0.0)
                    part = part[:, 0:128] + part[:, 128:256]
                    folded.append(part + pltpu.roll(part, 64, axis=1))
                result[col, pl.ds(start, 8), :] = jnp.where(low, folded[0], folded[1])

    @pl.when(r == pl.num_programs(0) - 1)
    def _():
        for i in range(16):
            for n, lanes in lanes_of(896):
                out[i, :, lanes] = result[n, pl.ds(i, 6, stride=16), :].astype(BF)


def repack_kernel(block, out, staged):
    for i in range(16):
        put(staged, slice(8 * i, 8 * i + 6), block[i].astype(F32))
    for k in range(6):
        for n, lanes in lanes_of(896):
            out[16 * k : 16 * k + 16, lanes] = staged[n, pl.ds(k, 16, stride=8), :].astype(BF)


def output_kernel(place, b0, b1, b2, b3, s0, s1, s2, s3, chosen, plain, scale, extra, weight, out, left, acc):
    y = place[0]
    c = place[1]
    for blocks, core in (((b0, b1, b2, b3), c), ((s0, s1, s2, s3), 1 - c)):
        for d, block in enumerate(blocks):
            j = 2 * lax.rem(y + N_Y - d, N_Y) + core
            left[pl.ds(pl.multiple_of(96 * j, 96), 96), :] = block[...]
    step = 192
    for n in range(768 // step):
        rows = slice(n * step, n * step + step)
        part = left[rows, :]
        picked = jnp.dot(part, chosen[...], preferred_element_type=F32)
        term = lax.dot_general(part * plain[...], weight[...], NT, preferred_element_type=F32) * scale[...]
        for k in range(OUTL):
            term = term + picked[:, k : k + 1] * extra[k : k + 1, :]
        put(acc, rows, term)
    for i in range(16):
        for n, lanes in lanes_of(out.shape[2]):
            got = acc[n, pl.ds(i, 48, stride=16), :].astype(BF)
            out[i, :, lanes] = got[:, 0 : lanes.stop - lanes.start]


def total_kernel(parts, out):
    total = parts[0].astype(F32)
    for i in range(1, 16):
        total = total + parts[i].astype(F32)
    out[...] = total.astype(BF)


def params(mib=48):
    return pltpu.CompilerParams(vmem_limit_bytes=mib * MIB)


def over_y(shift):
    return [(2 * y + c, 2 * ((y + shift) % N_Y) + c) for y in range(N_Y) for c in range(2)]


def shift_plane(first, shift):
    pairs = []
    for z in range(4):
        for x in range(4):
            for j in range(2 * N_Y):
                if (j % 2 == 0) == first:
                    to = z * 4 + (x + shift) % 4
                else:
                    to = (z + shift) % 4 * 4 + x
                pairs.append(((z * 4 + x) * 2 * N_Y + j, to * 2 * N_Y + j))
    return pairs


SIBLING = [(j, j ^ 1) for j in range(2 * N_Y)]


def on_device(
    activations,
    norm_gain,
    norm_bias,
    input_outliers,
    query_int,
    query_scale,
    keyvalue_int,
    keyvalue_scale,
    query_float,
    keyvalue_float,
    key_cache,
    value_cache,
    lengths,
    middle_outliers,
    output_int,
    output_scale,
    output_float,
):
    block_rows, features = activations.shape
    tokens = block_rows * 16
    columns = query_int.shape[1]
    out_columns = output_int.shape[1]
    me_x = lax.axis_index("gx")
    me_y = lax.axis_index("gy")
    place = jnp.stack([me_y // 2, me_y % 2, me_x // 4, me_x % 4]).astype(jnp.int32)
    smem = pl.BlockSpec(memory_space=pltpu.SMEM)
    vmem = pl.BlockSpec(memory_space=pltpu.VMEM)

    widened = activations.astype(F32)
    sums = jnp.stack([jnp.sum(widened, axis=1), jnp.sum(widened * widened, axis=1)])
    sums = lax.all_to_all(
        jnp.broadcast_to(sums[None], (2 * N_Y, 2, block_rows)), "gy", split_axis=0, concat_axis=0, tiled=True
    )
    picked = jnp.arange(features, dtype=jnp.int32)[:, None] == input_outliers[None, :]
    regular = jnp.where(jnp.any(picked, axis=1), 0.0, 1.0)[None]
    padded = features + 64
    own, kept, sent = pl.pallas_call(
        normalize_kernel,
        in_specs=[smem] + [vmem] * 6,
        out_specs=[vmem] * 3,
        out_shape=[
            jax.ShapeDtypeStruct((block_rows, padded), BF),
            jax.ShapeDtypeStruct((block_rows // 2, padded), BF),
            jax.ShapeDtypeStruct((block_rows // 2, padded), BF),
        ],
        compiler_params=params(8),
        name="normalize",
    )(
        place, sums, activations, norm_gain[None], norm_bias[None],
        jnp.pad(picked.astype(BF), ((0, 0), (0, 128 - OUTL))), regular,
    )
    plane = ("gx", "gy")
    both = jnp.stack([kept, lax.ppermute(sent, "gy", SIBLING)])
    both = jnp.concatenate(
        [both] + [lax.ppermute(both, plane, shift_plane(True, d)) for d in (1, 3, 2)], axis=1
    )
    pairs = pl.pallas_call(
        pair_kernel,
        out_shape=jax.ShapeDtypeStruct((2 * N_Y, 16, 512), F32),
        compiler_params=params(16),
        name="pair_projection",
    )(own, keyvalue_scale[None], keyvalue_float, keyvalue_int)
    both, pairs = lax.optimization_barrier((both, pairs))
    arrived = [both] + [lax.ppermute(both, plane, shift_plane(False, d)) for d in (1, 3, 2)]
    others = [lax.ppermute(block[1], "gy", SIBLING) for block in arrived]
    order = (0, 1, 3, 2)
    arrived = [arrived[n] for n in order]
    others = [others[n] for n in order]

    keep, send = pl.pallas_call(
        query_kernel,
        grid=(1,),
        in_specs=[smem] + [whole((1, 96, padded))] * 4 + [vmem] * 8,
        out_specs=[vmem] * 2,
        out_shape=[jax.ShapeDtypeStruct((N_Y, 112, columns), BF)] * 2,
        scratch_shapes=[pltpu.VMEM((7, tokens, 128), F32)],
        compiler_params=params(24),
        name="query_projection",
    )(place, *arrived, *others, query_scale[None], query_float, query_int, pairs)
    received = lax.ppermute(send, "gy", SIBLING)
    piece = jax.ShapeDtypeStruct((112, columns), BF)
    mine, to1, to2, to3 = pl.pallas_call(
        add_kernel, out_shape=[piece] * 4, compiler_params=params(8), name="add_cores"
    )(keep, received)
    from1 = lax.ppermute(to1, "gy", over_y(1))
    from3 = lax.ppermute(to3, "gy", over_y(3))
    from2 = lax.ppermute(to2, "gy", over_y(2))
    summed, pair_sums = pl.pallas_call(
        collect_kernel,
        out_shape=[
            jax.ShapeDtypeStruct((16, 6, columns), BF),
            jax.ShapeDtypeStruct((16, 512), F32),
        ],
        scratch_shapes=[pltpu.VMEM((7, 112, 128), F32)],
        compiler_params=params(8),
        name="collect",
    )(mine, from1, from2, from3)
    queries = lax.all_to_all(summed, "gx", split_axis=0, concat_axis=0, tiled=True)

    positions = (lengths[:, None] + jnp.arange(NEW, dtype=jnp.int32)[None, :]).reshape(6, 1)
    frequency = jnp.exp(jnp.arange(32, dtype=F32) * (-2.0 * math.log(rope_base) / HEAD))
    angles = positions.astype(F32) * frequency[None, :]
    cosine = jnp.tile(jnp.cos(angles), (1, 4))
    sine = jnp.sin(angles)
    sine = jnp.concatenate([-sine, sine, -sine, sine], axis=1)
    cosine = jnp.pad(cosine, ((0, 2), (0, 0)))
    sine = jnp.pad(sine, ((0, 2), (0, 0)))

    window = key_cache.shape[1]
    attended = pl.pallas_call(
        attend_kernel,
        grid=(3,),
        in_specs=[
            smem,
            whole((16, 6, columns)),
            whole((16, 512)),
            whole((8, 128)),
            whole((8, 128)),
            pl.BlockSpec((1, window, 512), lambda n: (n, 0, 0)),
            pl.BlockSpec((1, window, 512), lambda n: (n, 0, 0)),
        ],
        out_specs=whole((16, 6, columns)),
        out_shape=jax.ShapeDtypeStruct((16, 6, columns), BF),
        scratch_shapes=[
            pltpu.VMEM((7, 128, 128), F32),
            pltpu.VMEM((96, columns), F32),
            pltpu.VMEM((128, 512), F32),
            pltpu.VMEM((128, 512), F32),
            pltpu.VMEM((224, 256), F32),
            pltpu.VMEM((224, 256), F32),
            pltpu.VMEM((7, 96, 128), F32),
        ],
        compiler_params=params(24),
        name="attention",
    )(lengths, queries, pair_sums, cosine, sine, key_cache, value_cache)

    back = lax.all_to_all(attended, "gx", split_axis=0, concat_axis=0, tiled=True)
    mine = pl.pallas_call(
        repack_kernel,
        out_shape=jax.ShapeDtypeStruct((96, columns), BF),
        scratch_shapes=[pltpu.VMEM((7, 128, 128), F32)],
        compiler_params=params(8),
        name="repack",
    )(back)
    blocks = [mine] + [lax.ppermute(mine, "gy", over_y(d)) for d in (1, 2, 3)]
    blocks = blocks + [lax.ppermute(b, "gy", SIBLING) for b in blocks]

    middle = lax.dynamic_slice(middle_outliers, (me_x * OUTL,), (OUTL,))
    chosen = jnp.arange(columns, dtype=jnp.int32)[:, None] == middle[None, :]
    plain = jnp.where(jnp.any(chosen, axis=1), 0.0, 1.0).astype(BF)[None]
    chosen = jnp.pad(chosen.astype(BF), ((0, 0), (0, 128 - OUTL)))
    partial = pl.pallas_call(
        output_kernel,
        in_specs=[smem] + [vmem] * 13,
        out_specs=vmem,
        out_shape=jax.ShapeDtypeStruct((16, block_rows, out_columns), BF),
        scratch_shapes=[pltpu.VMEM((tokens, columns), BF), pltpu.VMEM((15, tokens, 128), F32)],
        compiler_params=params(28),
        name="output_projection",
    )(place, *blocks, chosen, plain, output_scale[None], output_float, output_int.T)
    parts = lax.all_to_all(partial, "gx", split_axis=0, concat_axis=0, tiled=True)
    return pl.pallas_call(
        total_kernel,
        out_shape=jax.ShapeDtypeStruct((block_rows, out_columns), BF),
        compiler_params=params(16),
        name="total",
    )(parts)


def solution(mesh):
    placed = (
        P("gx", "gy"),
        P("gy"),
        P("gy"),
        P("gy"),
        P("gy", "gx"),
        P("gx"),
        P("gy", None),
        P(),
        P("gy", "gx"),
        P("gy", None),
        P(("gx", "gy"), None, None),
        P(("gx", "gy"), None, None),
        P(("gx", "gy")),
        P(),
        P("gx", "gy"),
        P("gy"),
        P("gx", "gy"),
    )
    return jax.shard_map(
        on_device, mesh=mesh, in_specs=placed, out_specs=P("gx", "gy"), check_vma=False
    )
```

```python
import functools
import math

import jax
import jax.numpy as jnp
from jax import lax
from jax.experimental import pallas as pl
from jax.experimental.pallas import tpu as pltpu
from jax.sharding import PartitionSpec as P

D = 14848
HEAD = 64
KV = 8
GROUP = 28
OUTL = 4
NEW = 2
N_Y = 4
LOCAL_HEADS = 14
CHUNK = 512

epsilon = 1e-05
rope_base = 10000.0
BF = jnp.bfloat16
F32 = jnp.float32
MIB = 1024 * 1024
STEPS = (0, 1, 3, 2)
NT = (((1,), (1,)), ((), ()))


def lanes_of(columns):
    return [(n, slice(128 * n, min(128 * n + 128, columns))) for n in range((columns + 127) // 128)]


def put(ref, rows, values):
    for n, lanes in lanes_of(values.shape[1]):
        ref[n, rows, 0 : lanes.stop - lanes.start] = values[:, lanes]


def whole(shape):
    return pl.BlockSpec(shape, lambda *_: (0,) * len(shape))


def normalize_kernel(place, parts, x, gain, bias, picked, plain, own, keep, send):
    sums = jnp.sum(parts[...], axis=0)
    rows = x.shape[0]
    unit = lax.broadcasted_iota(jnp.int32, (rows, rows), 0) == lax.broadcasted_iota(jnp.int32, (rows, rows), 1)
    sums = lax.dot_general(
        unit.astype(F32), sums, NT, precision=lax.Precision.HIGHEST, preferred_element_type=F32
    )
    average = sums[:, 0:1] / D
    variance = sums[:, 1:2] / D - average * average
    normed = (x[...].astype(F32) - average) * lax.rsqrt(variance + epsilon) * gain[...] + bias[...]
    rounded = normed.astype(BF)
    outlier = jnp.dot(rounded, picked[...], preferred_element_type=F32)
    regular = rounded.astype(F32) * plain[...]
    features = x.shape[1]
    own[:, 0:features] = regular.astype(BF)
    own[:, features:] = outlier[:, 0:64].astype(BF)
    half = rows // 2
    first = place[1] == 0
    for out, flag in ((keep, first), (send, jnp.logical_not(first))):
        out[:, 0:features] = jnp.where(flag, regular[0:half], regular[half:]).astype(BF)
        out[:, features:] = jnp.where(flag, outlier[0:half, 0:64], outlier[half:, 0:64]).astype(BF)


def pair_kernel(own, scale, extra, weight, out):
    features = weight.shape[0]
    term = jnp.dot(own[:, 0:features], weight[...], preferred_element_type=F32) * scale[...]
    value = own[:, features:].astype(F32)
    for k in range(OUTL):
        term = term + value[:, k : k + 1] * extra[k : k + 1, :]
    for j in range(2 * N_Y):
        rows = slice(6 * j, 6 * j + 6)
        out[j, 0:6, :] = term[rows, 0:512]
        out[j, 6:12, :] = term[rows, 512:1024]
        out[j, 12:16, :] = jnp.zeros((4, 512), F32)


def query_kernel(
    place, a0, a1, a2, a3, b0, b1, b2, b3, scale, extra, weight, pairs, keep, send, acc
):
    y = place[0]
    c = place[1]
    z = place[2]
    x = place[3]
    features = weight.shape[0]
    for d2, (near, far) in enumerate(((a0, b0), (a1, b1), (a2, b2), (a3, b3))):
        rows = jnp.concatenate([near[0], far[...]], axis=0)
        term = jnp.dot(rows[:, 0:features], weight[...], preferred_element_type=F32) * scale[...]
        value = rows[:, features:].astype(F32)
        for k in range(OUTL):
            term = term + value[:, k : k + 1] * extra[k : k + 1, :]
        for side in range(2):
            half = c if side == 0 else 1 - c
            for d1 in range(4):
                along_x = lax.rem(x + 4 - jnp.where(half == 0, STEPS[d1], d2), 4)
                along_z = lax.rem(z + 4 - jnp.where(half == 0, d2, STEPS[d1]), 4)
                at = pl.multiple_of((along_z * 4 + along_x) * 48 + half * 24, 8)
                row = side * 96 + d1 * 24
                put(acc, pl.ds(at, 24), term[row : row + 24, :])
    for out, core in ((keep, c), (send, 1 - c)):
        for d in range(N_Y):
            j = 2 * lax.rem(y + d, N_Y) + core
            for k in range(6):
                for n, lanes in lanes_of(896):
                    out[d, 16 * k : 16 * k + 16, lanes] = acc[n, pl.ds(6 * j + k, 16, stride=48), :].astype(BF)
            out[d, 96:112, 0:512] = pairs[j].astype(BF)
            out[d, 96:112, 512:896] = jnp.zeros((16, 384), BF)


def add_kernel(keep, received, o0, o1, o2, o3):
    for d, out in enumerate((o0, o1, o2, o3)):
        out[...] = (keep[d].astype(F32) + received[d].astype(F32)).astype(BF)


def collect_kernel(a, b, c, d, query_out, pair_out, acc):
    total = (a[...].astype(F32) + b[...].astype(F32)) + (c[...].astype(F32) + d[...].astype(F32))
    put(acc, slice(0, 112), total)
    for i in range(16):
        for n, lanes in lanes_of(896):
            query_out[i, :, lanes] = acc[n, pl.ds(i, 6, stride=16), :].astype(BF)
    pair_out[...] = total[96:112, 0:512]


def rotate_lanes(values, cosine, sine):
    lane = lax.broadcasted_iota(jnp.int32, values.shape, 1)
    partner = jnp.where(
        lane % 64 < 32, pltpu.roll(values, 96, axis=1), pltpu.roll(values, 32, axis=1)
    )
    return values * cosine + partner * sine


def attend_kernel(
    lengths, queries, pairs, cosine, sine, keys, values, out,
    staged, rotated, fresh_key, fresh_value, blocks, mixture, result, key_buf, value_buf, sems,
):
    requests = keys.shape[0]
    window = keys.shape[1]

    def fetch(r, n, which):
        source, target = ((keys, key_buf), (values, value_buf))[which]
        rows = pl.ds(pl.multiple_of(n * CHUNK, CHUNK), CHUNK)
        return pltpu.make_async_copy(source.at[r, rows], target.at[r, rows], sems.at[r, n, which])

    for r in range(requests):
        for n in range(window // CHUNK):

            @pl.when(lengths[r] > n * CHUNK)
            def _():
                fetch(r, n, 0).start()
                fetch(r, n, 1).start()

    for i in range(16):
        put(staged, slice(8 * i, 8 * i + 6), queries[i].astype(F32))
    for k in range(6):
        for col in range(7):
            lanes = slice(128 * col, 128 * col + 128)
            part = staged[col, pl.ds(k, 16, stride=8), :]
            turned = rotate_lanes(part, cosine[k : k + 1, :], sine[k : k + 1, :])
            rotated[16 * k : 16 * k + 16, lanes] = turned.astype(BF).astype(F32) * 0.125
    fresh_key[...] = jnp.zeros_like(fresh_key)
    fresh_value[...] = jnp.zeros_like(fresh_value)
    rounded = pairs[...].astype(BF).astype(F32)
    for col in range(4):
        lanes = slice(128 * col, 128 * col + 128)
        fresh_key[0:6, lanes] = rotate_lanes(rounded[0:6, lanes], cosine[0:6, :], sine[0:6, :])
    fresh_value[0:6, :] = rounded[6:12, :]

    sub = lax.broadcasted_iota(jnp.int32, (8, 256), 0)
    lane = lax.broadcasted_iota(jnp.int32, (8, 256), 1)
    own = sub // 2 == lane // 64
    low = lax.broadcasted_iota(jnp.int32, (8, 128), 1) < 64
    rows = LOCAL_HEADS * 16
    row = lax.broadcasted_iota(jnp.int32, (rows, 128), 0)
    column = lax.broadcasted_iota(jnp.int32, (rows, 128), 1)
    causal = column % 2 <= (row // 8) % 2
    place = lax.broadcasted_iota(jnp.int32, (rows, CHUNK), 1)

    starts = []
    for r in range(requests):
        state = []
        for g in range(2):
            for t in range(NEW):
                start = (NEW * r + t) * 16 + 8 * g
                for col in range(7):
                    part = rotated[start : start + 8, 128 * col : 128 * col + 128]
                    other = pltpu.roll(part, 64, axis=1)
                    for half in range(2):
                        both = jnp.where(low, part, other) if half == 0 else jnp.where(low, other, part)
                        both = jnp.concatenate([both, both], axis=1)
                        at = (2 * col + half) * 16 + t * 8
                        blocks[2 * r + g, at : at + 8, :] = jnp.where(own, both, 0.0)
            side = slice(256 * g, 256 * g + 256)
            query = blocks[2 * r + g].astype(BF)
            scores = lax.dot_general(query, fresh_key[:, side].astype(BF), NT, preferred_element_type=F32)
            scores = jnp.where(causal & (column // 2 == r), scores, -jnp.inf)
            top = jnp.max(scores, axis=1, keepdims=True)
            prob = jnp.exp(scores - top)
            total = jnp.sum(prob, axis=1, keepdims=True)
            mixture[2 * r + g] = jnp.dot(
                prob.astype(BF), fresh_value[:, side].astype(BF), preferred_element_type=F32
            )
            state.append((top, total))
        starts.append(tuple(state))

    for r in range(requests):
        length = lengths[r]

        def body(n, state):
            at = pl.multiple_of(n * CHUNK, CHUNK)
            active = place < length - at
            fetch(r, n, 0).wait()
            fetch(r, n, 1).wait()
            new = []
            for g in range(2):
                top, total = state[g]
                side = slice(256 * g, 256 * g + 256)
                key = key_buf[r, pl.ds(at, CHUNK), side]
                value = value_buf[r, pl.ds(at, CHUNK), side]
                query = blocks[2 * r + g].astype(BF)
                scores = lax.dot_general(query, key, NT, preferred_element_type=F32)
                scores = jnp.where(active, scores, -jnp.inf)
                higher = jnp.maximum(top, jnp.max(scores, axis=1, keepdims=True))
                shrink = jnp.exp(top - higher)
                prob = jnp.exp(scores - higher)
                total = total * shrink + jnp.sum(prob, axis=1, keepdims=True)
                mixture[2 * r + g] = mixture[2 * r + g] * shrink + jnp.dot(
                    prob.astype(BF), value, preferred_element_type=F32
                )
                new.append((higher, total))
            return tuple(new)

        state = lax.fori_loop(0, (length + CHUNK - 1) // CHUNK, body, starts[r])
        for g in range(2):
            blocks[2 * r + g] = mixture[2 * r + g] / state[g][1]
            for t in range(NEW):
                start = (NEW * r + t) * 16 + 8 * g
                for col in range(7):
                    folded = []
                    for half in range(2):
                        at = (2 * col + half) * 16 + t * 8
                        part = jnp.where(own, blocks[2 * r + g, at : at + 8, :], 0.0)
                        part = part[:, 0:128] + part[:, 128:256]
                        folded.append(part + pltpu.roll(part, 64, axis=1))
                    result[col, start : start + 8, :] = jnp.where(low, folded[0], folded[1])
    for i in range(16):
        for n, lanes in lanes_of(896):
            out[i, :, lanes] = result[n, pl.ds(i, 6, stride=16), :].astype(BF)


def repack_kernel(block, out, staged):
    for i in range(16):
        put(staged, slice(8 * i, 8 * i + 6), block[i].astype(F32))
    for k in range(6):
        for n, lanes in lanes_of(896):
            out[16 * k : 16 * k + 16, lanes] = staged[n, pl.ds(k, 16, stride=8), :].astype(BF)


def output_kernel(place, b0, b1, b2, b3, s0, s1, s2, s3, chosen, plain, scale, extra, weight, out, left, acc):
    y = place[0]
    c = place[1]
    for blocks, core in (((b0, b1, b2, b3), c), ((s0, s1, s2, s3), 1 - c)):
        for d, block in enumerate(blocks):
            j = 2 * lax.rem(y + N_Y - d, N_Y) + core
            left[pl.ds(pl.multiple_of(96 * j, 96), 96), :] = block[...]
    step = 192
    for n in range(768 // step):
        rows = slice(n * step, n * step + step)
        part = left[rows, :]
        picked = jnp.dot(part, chosen[...], preferred_element_type=F32)
        term = lax.dot_general(part * plain[...], weight[...], NT, preferred_element_type=F32) * scale[...]
        for k in range(OUTL):
            term = term + picked[:, k : k + 1] * extra[k : k + 1, :]
        put(acc, rows, term)
    for i in range(16):
        for n, lanes in lanes_of(out.shape[2]):
            got = acc[n, pl.ds(i, 48, stride=16), :].astype(BF)
            out[i, :, lanes] = got[:, 0 : lanes.stop - lanes.start]


def total_kernel(parts, out):
    total = parts[0].astype(F32)
    for i in range(1, 16):
        total = total + parts[i].astype(F32)
    out[...] = total.astype(BF)


def params(mib=48):
    return pltpu.CompilerParams(vmem_limit_bytes=mib * MIB)


def over_y(shift):
    return [(2 * y + c, 2 * ((y + shift) % N_Y) + c) for y in range(N_Y) for c in range(2)]


def shift_plane(first, shift):
    pairs = []
    for z in range(4):
        for x in range(4):
            for j in range(2 * N_Y):
                if (j % 2 == 0) == first:
                    to = z * 4 + (x + shift) % 4
                else:
                    to = (z + shift) % 4 * 4 + x
                pairs.append(((z * 4 + x) * 2 * N_Y + j, to * 2 * N_Y + j))
    return pairs


SIBLING = [(j, j ^ 1) for j in range(2 * N_Y)]


def on_device(
    activations,
    norm_gain,
    norm_bias,
    input_outliers,
    query_int,
    query_scale,
    keyvalue_int,
    keyvalue_scale,
    query_float,
    keyvalue_float,
    key_cache,
    value_cache,
    lengths,
    middle_outliers,
    output_int,
    output_scale,
    output_float,
):
    block_rows, features = activations.shape
    tokens = block_rows * 16
    columns = query_int.shape[1]
    out_columns = output_int.shape[1]
    me_x = lax.axis_index("gx")
    me_y = lax.axis_index("gy")
    place = jnp.stack([me_y // 2, me_y % 2, me_x // 4, me_x % 4]).astype(jnp.int32)
    smem = pl.BlockSpec(memory_space=pltpu.SMEM)
    vmem = pl.BlockSpec(memory_space=pltpu.VMEM)

    widened = activations.astype(F32)
    sums = jnp.stack([jnp.sum(widened, axis=1), jnp.sum(widened * widened, axis=1)])
    sums = lax.all_to_all(
        jnp.broadcast_to(sums[None], (2 * N_Y, 2, block_rows)), "gy", split_axis=0, concat_axis=0, tiled=True
    )
    picked = jnp.arange(features, dtype=jnp.int32)[:, None] == input_outliers[None, :]
    regular = jnp.where(jnp.any(picked, axis=1), 0.0, 1.0)[None]
    padded = features + 64
    own, kept, sent = pl.pallas_call(
        normalize_kernel,
        in_specs=[smem] + [vmem] * 6,
        out_specs=[vmem] * 3,
        out_shape=[
            jax.ShapeDtypeStruct((block_rows, padded), BF),
            jax.ShapeDtypeStruct((block_rows // 2, padded), BF),
            jax.ShapeDtypeStruct((block_rows // 2, padded), BF),
        ],
        compiler_params=params(8),
        name="normalize",
    )(
        place, sums, activations, norm_gain[None], norm_bias[None],
        jnp.pad(picked.astype(BF), ((0, 0), (0, 128 - OUTL))), regular,
    )
    plane = ("gx", "gy")
    both = jnp.stack([kept, lax.ppermute(sent, "gy", SIBLING)])
    both = jnp.concatenate(
        [both] + [lax.ppermute(both, plane, shift_plane(True, d)) for d in (1, 3, 2)], axis=1
    )
    pairs = pl.pallas_call(
        pair_kernel,
        out_shape=jax.ShapeDtypeStruct((2 * N_Y, 16, 512), F32),
        compiler_params=params(16),
        name="pair_projection",
    )(own, keyvalue_scale[None], keyvalue_float, keyvalue_int)
    both, pairs = lax.optimization_barrier((both, pairs))
    arrived = [both] + [lax.ppermute(both, plane, shift_plane(False, d)) for d in (1, 3, 2)]
    others = [lax.ppermute(block[1], "gy", SIBLING) for block in arrived]
    order = (0, 1, 3, 2)
    arrived = [arrived[n] for n in order]
    others = [others[n] for n in order]

    keep, send = pl.pallas_call(
        query_kernel,
        grid=(1,),
        in_specs=[smem] + [whole((1, 96, padded))] * 4 + [vmem] * 8,
        out_specs=[vmem] * 2,
        out_shape=[jax.ShapeDtypeStruct((N_Y, 112, columns), BF)] * 2,
        scratch_shapes=[pltpu.VMEM((7, tokens, 128), F32)],
        compiler_params=params(24),
        name="query_projection",
    )(place, *arrived, *others, query_scale[None], query_float, query_int, pairs)
    received = lax.ppermute(send, "gy", SIBLING)
    piece = jax.ShapeDtypeStruct((112, columns), BF)
    mine, to1, to2, to3 = pl.pallas_call(
        add_kernel, out_shape=[piece] * 4, compiler_params=params(8), name="add_cores"
    )(keep, received)
    from1 = lax.ppermute(to1, "gy", over_y(1))
    from3 = lax.ppermute(to3, "gy", over_y(3))
    from2 = lax.ppermute(to2, "gy", over_y(2))
    summed, pair_sums = pl.pallas_call(
        collect_kernel,
        out_shape=[
            jax.ShapeDtypeStruct((16, 6, columns), BF),
            jax.ShapeDtypeStruct((16, 512), F32),
        ],
        scratch_shapes=[pltpu.VMEM((7, 112, 128), F32)],
        compiler_params=params(8),
        name="collect",
    )(mine, from1, from2, from3)
    queries = lax.all_to_all(summed, "gx", split_axis=0, concat_axis=0, tiled=True)

    positions = (lengths[:, None] + jnp.arange(NEW, dtype=jnp.int32)[None, :]).reshape(6, 1)
    frequency = jnp.exp(jnp.arange(32, dtype=F32) * (-2.0 * math.log(rope_base) / HEAD))
    angles = positions.astype(F32) * frequency[None, :]
    cosine = jnp.tile(jnp.cos(angles), (1, 4))
    sine = jnp.sin(angles)
    sine = jnp.concatenate([-sine, sine, -sine, sine], axis=1)
    cosine = jnp.pad(cosine, ((0, 2), (0, 0)))
    sine = jnp.pad(sine, ((0, 2), (0, 0)))

    requests, window, cached = key_cache.shape
    hbm = pl.BlockSpec(memory_space=pltpu.HBM)
    attended = pl.pallas_call(
        attend_kernel,
        in_specs=[smem, vmem, vmem, vmem, vmem, hbm, hbm],
        out_specs=vmem,
        out_shape=jax.ShapeDtypeStruct((16, 6, columns), BF),
        scratch_shapes=[
            pltpu.VMEM((7, 128, 128), F32),
            pltpu.VMEM((96, columns), F32),
            pltpu.VMEM((128, cached), F32),
            pltpu.VMEM((128, cached), F32),
            pltpu.VMEM((6, 224, 256), F32),
            pltpu.VMEM((6, 224, 256), F32),
            pltpu.VMEM((7, 96, 128), F32),
            pltpu.VMEM((requests, window, cached), BF),
            pltpu.VMEM((requests, window, cached), BF),
            pltpu.SemaphoreType.DMA((requests, window // CHUNK, 2)),
        ],
        compiler_params=params(57),
        name="attention",
    )(lengths, queries, pair_sums, cosine, sine, key_cache, value_cache)

    back = lax.all_to_all(attended, "gx", split_axis=0, concat_axis=0, tiled=True)
    mine = pl.pallas_call(
        repack_kernel,
        out_shape=jax.ShapeDtypeStruct((96, columns), BF),
        scratch_shapes=[pltpu.VMEM((7, 128, 128), F32)],
        compiler_params=params(8),
        name="repack",
    )(back)
    blocks = [mine] + [lax.ppermute(mine, "gy", over_y(d)) for d in (1, 2, 3)]
    blocks = blocks + [lax.ppermute(b, "gy", SIBLING) for b in blocks]

    middle = lax.dynamic_slice(middle_outliers, (me_x * OUTL,), (OUTL,))
    chosen = jnp.arange(columns, dtype=jnp.int32)[:, None] == middle[None, :]
    plain = jnp.where(jnp.any(chosen, axis=1), 0.0, 1.0).astype(BF)[None]
    chosen = jnp.pad(chosen.astype(BF), ((0, 0), (0, 128 - OUTL)))
    partial = pl.pallas_call(
        output_kernel,
        in_specs=[smem] + [vmem] * 13,
        out_specs=vmem,
        out_shape=jax.ShapeDtypeStruct((16, block_rows, out_columns), BF),
        scratch_shapes=[pltpu.VMEM((tokens, columns), BF), pltpu.VMEM((15, tokens, 128), F32)],
        compiler_params=params(28),
        name="output_projection",
    )(place, *blocks, chosen, plain, output_scale[None], output_float, output_int.T)
    parts = lax.all_to_all(partial, "gx", split_axis=0, concat_axis=0, tiled=True)
    return pl.pallas_call(
        total_kernel,
        out_shape=jax.ShapeDtypeStruct((block_rows, out_columns), BF),
        compiler_params=params(16),
        name="total",
    )(parts)


def solution(mesh):
    placed = (
        P("gx", "gy"),
        P("gy"),
        P("gy"),
        P("gy"),
        P("gy", "gx"),
        P("gx"),
        P("gy", None),
        P(),
        P("gy", "gx"),
        P("gy", None),
        P(("gx", "gy"), None, None),
        P(("gx", "gy"), None, None),
        P(("gx", "gy")),
        P(),
        P("gx", "gy"),
        P("gy"),
        P("gx", "gy"),
    )
    return jax.shard_map(
        on_device, mesh=mesh, in_specs=placed, out_specs=P("gx", "gy"), check_vma=False
    )
```

```python
import functools
import math

import jax
import jax.numpy as jnp
from jax import lax
from jax.experimental import pallas as pl
from jax.experimental.pallas import tpu as pltpu
from jax.sharding import PartitionSpec as P

D = 14848
HEAD = 64
KV = 8
GROUP = 28
OUTL = 4
NEW = 2
N_Y = 4
LOCAL_HEADS = 14
CHUNK = 512

epsilon = 1e-05
rope_base = 10000.0
BF = jnp.bfloat16
F32 = jnp.float32
MIB = 1024 * 1024
STEPS = (0, 1, 3, 2)
NT = (((1,), (1,)), ((), ()))


def lanes_of(columns):
    return [(n, slice(128 * n, min(128 * n + 128, columns))) for n in range((columns + 127) // 128)]


def put(ref, rows, values):
    for n, lanes in lanes_of(values.shape[1]):
        ref[n, rows, 0 : lanes.stop - lanes.start] = values[:, lanes]


def whole(shape):
    return pl.BlockSpec(shape, lambda *_: (0,) * len(shape))


def prepare_kernel(place, x, picked, own, keep, send):
    outlier = jnp.dot(x[...], picked[...], preferred_element_type=F32)
    values = x[...].astype(F32)
    rows, features = x.shape
    own[:, 0:features] = x[...]
    own[:, features:] = outlier[:, 0:64].astype(BF)
    half = rows // 2
    first = place[1] == 0
    for out, flag in ((keep, first), (send, jnp.logical_not(first))):
        out[:, 0:features] = jnp.where(flag, values[0:half], values[half:]).astype(BF)
        out[:, features:] = jnp.where(flag, outlier[0:half, 0:64], outlier[half:, 0:64]).astype(BF)


def diagonal(size):
    return lax.broadcasted_iota(jnp.int32, (size, size), 0) == lax.broadcasted_iota(
        jnp.int32, (size, size), 1
    )


def sums_kernel(both, out):
    features = both.shape[2] - 64
    rows = both.shape[1]
    first = jnp.zeros((rows, 1), F32)
    second = jnp.zeros((rows, 1), F32)
    for part in range(2):
        values = both[part, :, 0:features].astype(F32)
        first = first + jnp.sum(values, axis=1, keepdims=True)
        second = second + jnp.sum(values * values, axis=1, keepdims=True)
    unit = diagonal(rows)
    first = jnp.sum(jnp.where(unit, first, 0.0), axis=0, keepdims=True)
    second = jnp.sum(jnp.where(unit, second, 0.0), axis=0, keepdims=True)
    for n in range(16):
        out[n, 0:1, :] = first
        out[n, 1:2, :] = second


def moments(sums):
    unit = diagonal(sums.shape[1])
    average = jnp.sum(jnp.where(unit, sums[0:1, :], 0.0), axis=1, keepdims=True) / D
    squares = jnp.sum(jnp.where(unit, sums[1:2, :], 0.0), axis=1, keepdims=True) / D
    return average, lax.rsqrt(squares - average * average + epsilon)


def normalize(rows, average, inverse, gain, bias, gain_out, bias_out, features):
    regular = ((rows[:, 0:features].astype(F32) - average) * inverse * gain + bias).astype(BF)
    outlier = (rows[:, features : features + OUTL].astype(F32) - average) * inverse * gain_out + bias_out
    return regular, outlier.astype(BF).astype(F32)


def pair_kernel(place, own, mine, other, gain, bias, gain_out, bias_out, scale, extra, weight, out):
    c = place[1]
    z = place[2]
    x = place[3]
    features = weight.shape[0]
    half = own.shape[0] // 2
    first = c == 0
    mine_at = mine[jnp.where(first, z, x)]
    other_at = other[jnp.where(first, x, z)]
    average0, inverse0 = moments(jnp.where(first, mine_at, other_at))
    average1, inverse1 = moments(jnp.where(first, other_at, mine_at))
    average = jnp.concatenate([average0[0:half], average1[0:half]], axis=0)
    inverse = jnp.concatenate([inverse0[0:half], inverse1[0:half]], axis=0)
    regular, outlier = normalize(
        own[...], average, inverse, gain[...], bias[...], gain_out[...], bias_out[...], features
    )
    term = jnp.dot(regular, weight[...], preferred_element_type=F32) * scale[...]
    for k in range(OUTL):
        term = term + outlier[:, k : k + 1] * extra[k : k + 1, :]
    for j in range(2 * N_Y):
        rows = slice(6 * j, 6 * j + 6)
        out[j, 0:6, :] = term[rows, 0:512]
        out[j, 6:12, :] = term[rows, 512:1024]
        out[j, 12:16, :] = jnp.zeros((4, 512), F32)


def query_kernel(
    place, a0, a1, a2, a3, b0, b1, b2, b3, mine, other, gain, bias, gain_out, bias_out,
    scale, extra, weight, pairs, keep, send, acc,
):
    y = place[0]
    c = place[1]
    z = place[2]
    x = place[3]
    features = weight.shape[0]
    for d2, (near, far) in enumerate(((a0, b0), (a1, b1), (a2, b2), (a3, b3))):
        regulars = []
        outliers = []
        for side, rows in enumerate((near[0], far[...])):
            sums = (mine, other)[side][lax.rem(jnp.where((c == 0) == (side == 0), z, x) + 4 - d2, 4)]
            average, inverse = moments(sums)
            regular, outlier = normalize(
                rows, average, inverse, gain[...], bias[...], gain_out[...], bias_out[...], features
            )
            regulars.append(regular)
            outliers.append(outlier)
        rows = jnp.concatenate(regulars, axis=0)
        value = jnp.concatenate(outliers, axis=0)
        term = jnp.dot(rows, weight[...], preferred_element_type=F32) * scale[...]
        for k in range(OUTL):
            term = term + value[:, k : k + 1] * extra[k : k + 1, :]
        for side in range(2):
            half = c if side == 0 else 1 - c
            for d1 in range(4):
                along_x = lax.rem(x + 4 - jnp.where(half == 0, STEPS[d1], d2), 4)
                along_z = lax.rem(z + 4 - jnp.where(half == 0, d2, STEPS[d1]), 4)
                at = pl.multiple_of((along_z * 4 + along_x) * 48 + half * 24, 8)
                row = side * 96 + d1 * 24
                put(acc, pl.ds(at, 24), term[row : row + 24, :])
    for out, core in ((keep, c), (send, 1 - c)):
        for d in range(N_Y):
            j = 2 * lax.rem(y + d, N_Y) + core
            for k in range(6):
                for n, lanes in lanes_of(896):
                    out[d, 16 * k : 16 * k + 16, lanes] = acc[n, pl.ds(6 * j + k, 16, stride=48), :].astype(BF)
            out[d, 96:112, 0:512] = pairs[j].astype(BF)
            out[d, 96:112, 512:896] = jnp.zeros((16, 384), BF)


def add_kernel(keep, received, o0, o1, o2, o3):
    for d, out in enumerate((o0, o1, o2, o3)):
        out[...] = (keep[d].astype(F32) + received[d].astype(F32)).astype(BF)


def collect_kernel(a, b, c, d, query_out, pair_out, acc):
    total = (a[...].astype(F32) + b[...].astype(F32)) + (c[...].astype(F32) + d[...].astype(F32))
    put(acc, slice(0, 112), total)
    for i in range(16):
        for n, lanes in lanes_of(896):
            query_out[i, :, lanes] = acc[n, pl.ds(i, 6, stride=16), :].astype(BF)
    pair_out[...] = total[96:112, 0:512]


def rotate_lanes(values, cosine, sine):
    lane = lax.broadcasted_iota(jnp.int32, values.shape, 1)
    partner = jnp.where(
        lane % 64 < 32, pltpu.roll(values, 96, axis=1), pltpu.roll(values, 32, axis=1)
    )
    return values * cosine + partner * sine


def attend_kernel(
    lengths, queries, pairs, cosine, sine, keys, values, out,
    staged, rotated, fresh_key, fresh_value, blocks, mixture, result, key_buf, value_buf, sems,
):
    requests = keys.shape[0]
    window = keys.shape[1]

    def fetch(r, n, which):
        source, target = ((keys, key_buf), (values, value_buf))[which]
        rows = pl.ds(pl.multiple_of(n * CHUNK, CHUNK), CHUNK)
        return pltpu.make_async_copy(source.at[r, rows], target.at[r, rows], sems.at[r, n, which])

    for r in range(requests):
        for n in range(window // CHUNK):

            @pl.when(lengths[r] > n * CHUNK)
            def _():
                fetch(r, n, 0).start()
                fetch(r, n, 1).start()

    for i in range(16):
        put(staged, slice(8 * i, 8 * i + 6), queries[i].astype(F32))
    for k in range(6):
        for col in range(7):
            lanes = slice(128 * col, 128 * col + 128)
            part = staged[col, pl.ds(k, 16, stride=8), :]
            turned = rotate_lanes(part, cosine[k : k + 1, :], sine[k : k + 1, :])
            rotated[16 * k : 16 * k + 16, lanes] = turned.astype(BF).astype(F32) * 0.125
    fresh_key[...] = jnp.zeros_like(fresh_key)
    fresh_value[...] = jnp.zeros_like(fresh_value)
    rounded = pairs[...].astype(BF).astype(F32)
    for col in range(4):
        lanes = slice(128 * col, 128 * col + 128)
        fresh_key[0:6, lanes] = rotate_lanes(rounded[0:6, lanes], cosine[0:6, :], sine[0:6, :])
    fresh_value[0:6, :] = rounded[6:12, :]

    sub = lax.broadcasted_iota(jnp.int32, (8, 256), 0)
    lane = lax.broadcasted_iota(jnp.int32, (8, 256), 1)
    own = sub // 2 == lane // 64
    low = lax.broadcasted_iota(jnp.int32, (8, 128), 1) < 64
    rows = LOCAL_HEADS * 16
    row = lax.broadcasted_iota(jnp.int32, (rows, 128), 0)
    column = lax.broadcasted_iota(jnp.int32, (rows, 128), 1)
    causal = column % 2 <= (row // 8) % 2
    place = lax.broadcasted_iota(jnp.int32, (rows, CHUNK), 1)

    starts = []
    for r in range(requests):
        state = []
        for g in range(2):
            for t in range(NEW):
                start = (NEW * r + t) * 16 + 8 * g
                for col in range(7):
                    part = rotated[start : start + 8, 128 * col : 128 * col + 128]
                    other = pltpu.roll(part, 64, axis=1)
                    for half in range(2):
                        both = jnp.where(low, part, other) if half == 0 else jnp.where(low, other, part)
                        both = jnp.concatenate([both, both], axis=1)
                        at = (2 * col + half) * 16 + t * 8
                        blocks[2 * r + g, at : at + 8, :] = jnp.where(own, both, 0.0)
            side = slice(256 * g, 256 * g + 256)
            query = blocks[2 * r + g].astype(BF)
            scores = lax.dot_general(query, fresh_key[:, side].astype(BF), NT, preferred_element_type=F32)
            scores = jnp.where(causal & (column // 2 == r), scores, -jnp.inf)
            top = jnp.max(scores, axis=1, keepdims=True)
            prob = jnp.exp(scores - top)
            total = jnp.sum(prob, axis=1, keepdims=True)
            mixture[2 * r + g] = jnp.dot(
                prob.astype(BF), fresh_value[:, side].astype(BF), preferred_element_type=F32
            )
            state.append((top, total))
        starts.append(tuple(state))

    for r in range(requests):
        length = lengths[r]

        def body(n, state):
            at = pl.multiple_of(n * CHUNK, CHUNK)
            active = place < length - at
            fetch(r, n, 0).wait()
            fetch(r, n, 1).wait()
            new = []
            for g in range(2):
                top, total = state[g]
                side = slice(256 * g, 256 * g + 256)
                key = key_buf[r, pl.ds(at, CHUNK), side]
                value = value_buf[r, pl.ds(at, CHUNK), side]
                query = blocks[2 * r + g].astype(BF)
                scores = lax.dot_general(query, key, NT, preferred_element_type=F32)
                scores = jnp.where(active, scores, -jnp.inf)
                higher = jnp.maximum(top, jnp.max(scores, axis=1, keepdims=True))
                shrink = jnp.exp(top - higher)
                prob = jnp.exp(scores - higher)
                total = total * shrink + jnp.sum(prob, axis=1, keepdims=True)
                mixture[2 * r + g] = mixture[2 * r + g] * shrink + jnp.dot(
                    prob.astype(BF), value, preferred_element_type=F32
                )
                new.append((higher, total))
            return tuple(new)

        state = lax.fori_loop(0, (length + CHUNK - 1) // CHUNK, body, starts[r])
        for g in range(2):
            blocks[2 * r + g] = mixture[2 * r + g] / state[g][1]
            for t in range(NEW):
                start = (NEW * r + t) * 16 + 8 * g
                for col in range(7):
                    folded = []
                    for half in range(2):
                        at = (2 * col + half) * 16 + t * 8
                        part = jnp.where(own, blocks[2 * r + g, at : at + 8, :], 0.0)
                        part = part[:, 0:128] + part[:, 128:256]
                        folded.append(part + pltpu.roll(part, 64, axis=1))
                    result[col, start : start + 8, :] = jnp.where(low, folded[0], folded[1])
    for i in range(16):
        for n, lanes in lanes_of(896):
            out[i, :, lanes] = result[n, pl.ds(i, 6, stride=16), :].astype(BF)


def repack_kernel(block, out, staged):
    for i in range(16):
        put(staged, slice(8 * i, 8 * i + 6), block[i].astype(F32))
    for k in range(6):
        for n, lanes in lanes_of(896):
            out[16 * k : 16 * k + 16, lanes] = staged[n, pl.ds(k, 16, stride=8), :].astype(BF)


def output_kernel(place, b0, b1, b2, b3, s0, s1, s2, s3, chosen, plain, scale, extra, weight, out, left, acc):
    y = place[0]
    c = place[1]
    for blocks, core in (((b0, b1, b2, b3), c), ((s0, s1, s2, s3), 1 - c)):
        for d, block in enumerate(blocks):
            j = 2 * lax.rem(y + N_Y - d, N_Y) + core
            left[pl.ds(pl.multiple_of(96 * j, 96), 96), :] = block[...]
    step = 192
    for n in range(768 // step):
        rows = slice(n * step, n * step + step)
        part = left[rows, :]
        picked = jnp.dot(part, chosen[...], preferred_element_type=F32)
        term = lax.dot_general(part * plain[...], weight[...], NT, preferred_element_type=F32) * scale[...]
        for k in range(OUTL):
            term = term + picked[:, k : k + 1] * extra[k : k + 1, :]
        put(acc, rows, term)
    for i in range(16):
        for n, lanes in lanes_of(out.shape[2]):
            got = acc[n, pl.ds(i, 48, stride=16), :].astype(BF)
            out[i, :, lanes] = got[:, 0 : lanes.stop - lanes.start]


def total_kernel(parts, out):
    total = parts[0].astype(F32)
    for i in range(1, 16):
        total = total + parts[i].astype(F32)
    out[...] = total.astype(BF)


def params(mib=48):
    return pltpu.CompilerParams(vmem_limit_bytes=mib * MIB)


def over_y(shift):
    return [(2 * y + c, 2 * ((y + shift) % N_Y) + c) for y in range(N_Y) for c in range(2)]


def shift_plane(first, shift):
    pairs = []
    for z in range(4):
        for x in range(4):
            for j in range(2 * N_Y):
                if (j % 2 == 0) == first:
                    to = z * 4 + (x + shift) % 4
                else:
                    to = (z + shift) % 4 * 4 + x
                pairs.append(((z * 4 + x) * 2 * N_Y + j, to * 2 * N_Y + j))
    return pairs


def sheets():
    groups = []
    for first in (True, False):
        for fixed in range(4):
            group = []
            for moving in range(4):
                z, x = (moving, fixed) if first else (fixed, moving)
                for y in range(N_Y):
                    group.append((z * 4 + x) * 2 * N_Y + 2 * y + (0 if first else 1))
            groups.append(group)
    return groups


SIBLING = [(j, j ^ 1) for j in range(2 * N_Y)]


def on_device(
    activations,
    norm_gain,
    norm_bias,
    input_outliers,
    query_int,
    query_scale,
    keyvalue_int,
    keyvalue_scale,
    query_float,
    keyvalue_float,
    key_cache,
    value_cache,
    lengths,
    middle_outliers,
    output_int,
    output_scale,
    output_float,
):
    block_rows, features = activations.shape
    tokens = block_rows * 16
    columns = query_int.shape[1]
    out_columns = output_int.shape[1]
    me_x = lax.axis_index("gx")
    me_y = lax.axis_index("gy")
    place = jnp.stack([me_y // 2, me_y % 2, me_x // 4, me_x % 4]).astype(jnp.int32)
    smem = pl.BlockSpec(memory_space=pltpu.SMEM)
    vmem = pl.BlockSpec(memory_space=pltpu.VMEM)

    picked = jnp.arange(features, dtype=jnp.int32)[:, None] == input_outliers[None, :]
    is_outlier = jnp.any(picked, axis=1)
    gain = jnp.where(is_outlier, 0.0, norm_gain)[None]
    bias = jnp.where(is_outlier, 0.0, norm_bias)[None]
    gain_out = jnp.sum(jnp.where(picked, norm_gain[:, None], 0.0), axis=0)[None]
    bias_out = jnp.sum(jnp.where(picked, norm_bias[:, None], 0.0), axis=0)[None]
    padded = features + 64
    own, kept, sent = pl.pallas_call(
        prepare_kernel,
        in_specs=[smem] + [vmem] * 2,
        out_specs=[vmem] * 3,
        out_shape=[
            jax.ShapeDtypeStruct((block_rows, padded), BF),
            jax.ShapeDtypeStruct((block_rows // 2, padded), BF),
            jax.ShapeDtypeStruct((block_rows // 2, padded), BF),
        ],
        compiler_params=params(8),
        name="prepare",
    )(place, activations, jnp.pad(picked.astype(BF), ((0, 0), (0, 128 - OUTL))))
    plane = ("gx", "gy")
    both = jnp.stack([kept, lax.ppermute(sent, "gy", SIBLING)])
    both = jnp.concatenate(
        [both] + [lax.ppermute(both, plane, shift_plane(True, d)) for d in (1, 3, 2)], axis=1
    )
    arrived = [both] + [lax.ppermute(both, plane, shift_plane(False, d)) for d in (1, 3, 2)]
    sums = pl.pallas_call(
        sums_kernel,
        out_shape=jax.ShapeDtypeStruct((16, 2, 96), F32),
        compiler_params=params(8),
        name="row_sums",
    )(both)
    sums = lax.all_to_all(
        sums, plane, split_axis=0, concat_axis=0, tiled=True, axis_index_groups=sheets()
    )
    mine = jnp.sum(sums.reshape(4, N_Y, 2, 96), axis=1)
    other = lax.ppermute(mine, "gy", SIBLING)
    *arrived, mine, other = lax.optimization_barrier((*arrived, mine, other))
    pairs = pl.pallas_call(
        pair_kernel,
        in_specs=[smem] + [vmem] * 10,
        out_specs=vmem,
        out_shape=jax.ShapeDtypeStruct((2 * N_Y, 16, 512), F32),
        compiler_params=params(16),
        name="pair_projection",
    )(
        place, own, mine, other, gain, bias, gain_out, bias_out,
        keyvalue_scale[None], keyvalue_float, keyvalue_int,
    )
    others = [lax.ppermute(block[1], "gy", SIBLING) for block in arrived]
    order = (0, 1, 3, 2)
    arrived = [arrived[n] for n in order]
    others = [others[n] for n in order]

    keep, send = pl.pallas_call(
        query_kernel,
        grid=(1,),
        in_specs=[smem] + [whole((1, 96, padded))] * 4 + [vmem] * 14,
        out_specs=[vmem] * 2,
        out_shape=[jax.ShapeDtypeStruct((N_Y, 112, columns), BF)] * 2,
        scratch_shapes=[pltpu.VMEM((7, tokens, 128), F32)],
        compiler_params=params(24),
        name="query_projection",
    )(
        place, *arrived, *others, mine, other, gain, bias, gain_out, bias_out,
        query_scale[None], query_float, query_int, pairs,
    )
    received = lax.ppermute(send, "gy", SIBLING)
    piece = jax.ShapeDtypeStruct((112, columns), BF)
    mine, to1, to2, to3 = pl.pallas_call(
        add_kernel, out_shape=[piece] * 4, compiler_params=params(8), name="add_cores"
    )(keep, received)
    from1 = lax.ppermute(to1, "gy", over_y(1))
    from3 = lax.ppermute(to3, "gy", over_y(3))
    from2 = lax.ppermute(to2, "gy", over_y(2))
    summed, pair_sums = pl.pallas_call(
        collect_kernel,
        out_shape=[
            jax.ShapeDtypeStruct((16, 6, columns), BF),
            jax.ShapeDtypeStruct((16, 512), F32),
        ],
        scratch_shapes=[pltpu.VMEM((7, 112, 128), F32)],
        compiler_params=params(8),
        name="collect",
    )(mine, from1, from2, from3)
    queries = lax.all_to_all(summed, "gx", split_axis=0, concat_axis=0, tiled=True)

    positions = (lengths[:, None] + jnp.arange(NEW, dtype=jnp.int32)[None, :]).reshape(6, 1)
    frequency = jnp.exp(jnp.arange(32, dtype=F32) * (-2.0 * math.log(rope_base) / HEAD))
    angles = positions.astype(F32) * frequency[None, :]
    cosine = jnp.tile(jnp.cos(angles), (1, 4))
    sine = jnp.sin(angles)
    sine = jnp.concatenate([-sine, sine, -sine, sine], axis=1)
    cosine = jnp.pad(cosine, ((0, 2), (0, 0)))
    sine = jnp.pad(sine, ((0, 2), (0, 0)))

    requests, window, cached = key_cache.shape
    hbm = pl.BlockSpec(memory_space=pltpu.HBM)
    attended = pl.pallas_call(
        attend_kernel,
        in_specs=[smem, vmem, vmem, vmem, vmem, hbm, hbm],
        out_specs=vmem,
        out_shape=jax.ShapeDtypeStruct((16, 6, columns), BF),
        scratch_shapes=[
            pltpu.VMEM((7, 128, 128), F32),
            pltpu.VMEM((96, columns), F32),
            pltpu.VMEM((128, cached), F32),
            pltpu.VMEM((128, cached), F32),
            pltpu.VMEM((6, 224, 256), F32),
            pltpu.VMEM((6, 224, 256), F32),
            pltpu.VMEM((7, 96, 128), F32),
            pltpu.VMEM((requests, window, cached), BF),
            pltpu.VMEM((requests, window, cached), BF),
            pltpu.SemaphoreType.DMA((requests, window // CHUNK, 2)),
        ],
        compiler_params=params(57),
        name="attention",
    )(lengths, queries, pair_sums, cosine, sine, key_cache, value_cache)

    back = lax.all_to_all(attended, "gx", split_axis=0, concat_axis=0, tiled=True)
    mine = pl.pallas_call(
        repack_kernel,
        out_shape=jax.ShapeDtypeStruct((96, columns), BF),
        scratch_shapes=[pltpu.VMEM((7, 128, 128), F32)],
        compiler_params=params(8),
        name="repack",
    )(back)
    blocks = [mine] + [lax.ppermute(mine, "gy", over_y(d)) for d in (1, 2, 3)]
    blocks = blocks + [lax.ppermute(b, "gy", SIBLING) for b in blocks]

    middle = lax.dynamic_slice(middle_outliers, (me_x * OUTL,), (OUTL,))
    chosen = jnp.arange(columns, dtype=jnp.int32)[:, None] == middle[None, :]
    plain = jnp.where(jnp.any(chosen, axis=1), 0.0, 1.0).astype(BF)[None]
    chosen = jnp.pad(chosen.astype(BF), ((0, 0), (0, 128 - OUTL)))
    partial = pl.pallas_call(
        output_kernel,
        in_specs=[smem] + [vmem] * 13,
        out_specs=vmem,
        out_shape=jax.ShapeDtypeStruct((16, block_rows, out_columns), BF),
        scratch_shapes=[pltpu.VMEM((tokens, columns), BF), pltpu.VMEM((15, tokens, 128), F32)],
        compiler_params=params(28),
        name="output_projection",
    )(place, *blocks, chosen, plain, output_scale[None], output_float, output_int.T)
    parts = lax.all_to_all(partial, "gx", split_axis=0, concat_axis=0, tiled=True)
    return pl.pallas_call(
        total_kernel,
        out_shape=jax.ShapeDtypeStruct((block_rows, out_columns), BF),
        compiler_params=params(16),
        name="total",
    )(parts)


def solution(mesh):
    placed = (
        P("gx", "gy"),
        P("gy"),
        P("gy"),
        P("gy"),
        P("gy", "gx"),
        P("gx"),
        P("gy", None),
        P(),
        P("gy", "gx"),
        P("gy", None),
        P(("gx", "gy"), None, None),
        P(("gx", "gy"), None, None),
        P(("gx", "gy")),
        P(),
        P("gx", "gy"),
        P("gy"),
        P("gx", "gy"),
    )
    return jax.shard_map(
        on_device, mesh=mesh, in_specs=placed, out_specs=P("gx", "gy"), check_vma=False
    )
```

```python
import functools
import math

import jax
import jax.numpy as jnp
from jax import lax
from jax.experimental import pallas as pl
from jax.experimental.pallas import tpu as pltpu
from jax.sharding import PartitionSpec as P

D = 14848
HEAD = 64
KV = 8
GROUP = 28
OUTL = 4
NEW = 2
N_Y = 4
LOCAL_HEADS = 14
CHUNK = 512

epsilon = 1e-05
rope_base = 10000.0
BF = jnp.bfloat16
F32 = jnp.float32
MIB = 1024 * 1024
STEPS = (0, 1, 3, 2)
NT = (((1,), (1,)), ((), ()))


def lanes_of(columns):
    return [(n, slice(128 * n, min(128 * n + 128, columns))) for n in range((columns + 127) // 128)]


def put(ref, rows, values):
    for n, lanes in lanes_of(values.shape[1]):
        ref[n, rows, 0 : lanes.stop - lanes.start] = values[:, lanes]


def whole(shape):
    return pl.BlockSpec(shape, lambda *_: (0,) * len(shape))


def here():
    i = lax.axis_index("gx")
    j = lax.axis_index("gy")
    return lax.div(j, 2), lax.rem(j, 2), lax.div(i, 4), lax.rem(i, 4)


def prepare_kernel(positions, x, own, keep, send):
    rows, features = x.shape
    place = lax.broadcasted_iota(jnp.int32, (features, 128), 0)
    column = lax.broadcasted_iota(jnp.int32, (features, 128), 1)
    picked = (place == positions[0]) & (column == 0)
    for k in range(1, OUTL):
        picked = picked | ((place == positions[k]) & (column == k))
    picked = picked.astype(F32).astype(BF)
    outlier = jnp.dot(x[...], picked, preferred_element_type=F32)
    values = x[...].astype(F32)
    own[:, 0:features] = x[...]
    own[:, features:] = outlier[:, 0:64].astype(BF)
    half = rows // 2
    first = here()[1] == 0
    for out, flag in ((keep, first), (send, jnp.logical_not(first))):
        out[:, 0:features] = jnp.where(flag, values[0:half], values[half:]).astype(BF)
        out[:, features:] = jnp.where(flag, outlier[0:half, 0:64], outlier[half:, 0:64]).astype(BF)


def diagonal(size):
    return lax.broadcasted_iota(jnp.int32, (size, size), 0) == lax.broadcasted_iota(
        jnp.int32, (size, size), 1
    )


def sums_kernel(both, out):
    features = both.shape[2] - 64
    rows = both.shape[1]
    first = jnp.zeros((rows, 1), F32)
    second = jnp.zeros((rows, 1), F32)
    for part in range(2):
        values = both[part, :, 0:features].astype(F32)
        first = first + jnp.sum(values, axis=1, keepdims=True)
        second = second + jnp.sum(values * values, axis=1, keepdims=True)
    unit = diagonal(rows)
    first = jnp.sum(jnp.where(unit, first, 0.0), axis=0, keepdims=True)
    second = jnp.sum(jnp.where(unit, second, 0.0), axis=0, keepdims=True)
    for n in range(16):
        out[n, 0:1, :] = first
        out[n, 1:2, :] = second


def moments(sums):
    unit = diagonal(sums.shape[1])
    average = jnp.sum(jnp.where(unit, sums[0:1, :], 0.0), axis=1, keepdims=True) / D
    squares = jnp.sum(jnp.where(unit, sums[1:2, :], 0.0), axis=1, keepdims=True) / D
    return average, lax.rsqrt(squares - average * average + epsilon)


def normalize(rows, average, inverse, gain, bias, gain_out, bias_out, features):
    regular = ((rows[:, 0:features].astype(F32) - average) * inverse * gain + bias).astype(BF)
    outlier = (rows[:, features : features + OUTL].astype(F32) - average) * inverse * gain_out + bias_out
    return regular, outlier.astype(BF).astype(F32)


def pair_kernel(own, mine, other, gain, bias, gain_out, bias_out, scale, extra, weight, out):
    _, c, z, x = here()
    features = weight.shape[0]
    half = own.shape[0] // 2
    first = c == 0
    mine_at = mine[jnp.where(first, z, x)]
    other_at = other[jnp.where(first, x, z)]
    average0, inverse0 = moments(jnp.where(first, mine_at, other_at))
    average1, inverse1 = moments(jnp.where(first, other_at, mine_at))
    average = jnp.concatenate([average0[0:half], average1[0:half]], axis=0)
    inverse = jnp.concatenate([inverse0[0:half], inverse1[0:half]], axis=0)
    regular, outlier = normalize(
        own[...], average, inverse, gain[...], bias[...], gain_out[...], bias_out[...], features
    )
    term = jnp.dot(regular, weight[...], preferred_element_type=F32) * scale[...]
    for k in range(OUTL):
        term = term + outlier[:, k : k + 1] * extra[k : k + 1, :]
    for j in range(2 * N_Y):
        rows = slice(6 * j, 6 * j + 6)
        out[j, 0:6, :] = term[rows, 0:512]
        out[j, 6:12, :] = term[rows, 512:1024]
        out[j, 12:16, :] = jnp.zeros((4, 512), F32)


def query_kernel(
    a0, a1, a2, a3, b0, b1, b2, b3, mine, other, gain, bias, gain_out, bias_out,
    scale, extra, weight, pairs, keep, send, acc,
):
    y, c, z, x = here()
    features = weight.shape[0]
    for d2, (near, far) in enumerate(((a0, b0), (a1, b1), (a2, b2), (a3, b3))):
        regulars = []
        outliers = []
        for side, rows in enumerate((near[0], far[...])):
            sums = (mine, other)[side][lax.rem(jnp.where((c == 0) == (side == 0), z, x) + 4 - d2, 4)]
            average, inverse = moments(sums)
            regular, outlier = normalize(
                rows, average, inverse, gain[...], bias[...], gain_out[...], bias_out[...], features
            )
            regulars.append(regular)
            outliers.append(outlier)
        rows = jnp.concatenate(regulars, axis=0)
        value = jnp.concatenate(outliers, axis=0)
        term = jnp.dot(rows, weight[...], preferred_element_type=F32) * scale[...]
        for k in range(OUTL):
            term = term + value[:, k : k + 1] * extra[k : k + 1, :]
        for side in range(2):
            half = c if side == 0 else 1 - c
            for d1 in range(4):
                along_x = lax.rem(x + 4 - jnp.where(half == 0, STEPS[d1], d2), 4)
                along_z = lax.rem(z + 4 - jnp.where(half == 0, d2, STEPS[d1]), 4)
                at = pl.multiple_of((along_z * 4 + along_x) * 48 + half * 24, 8)
                row = side * 96 + d1 * 24
                put(acc, pl.ds(at, 24), term[row : row + 24, :])
    for out, core in ((keep, c), (send, 1 - c)):
        for d in range(N_Y):
            j = 2 * lax.rem(y + d, N_Y) + core
            for k in range(6):
                for n, lanes in lanes_of(896):
                    out[d, 16 * k : 16 * k + 16, lanes] = acc[n, pl.ds(6 * j + k, 16, stride=48), :].astype(BF)
            out[d, 96:112, 0:512] = pairs[j].astype(BF)
            out[d, 96:112, 512:896] = jnp.zeros((16, 384), BF)


def add_kernel(keep, received, o0, o1, o2, o3):
    for d, out in enumerate((o0, o1, o2, o3)):
        out[...] = (keep[d].astype(F32) + received[d].astype(F32)).astype(BF)


def collect_kernel(a, b, c, d, query_out, pair_out, acc):
    total = (a[...].astype(F32) + b[...].astype(F32)) + (c[...].astype(F32) + d[...].astype(F32))
    put(acc, slice(0, 112), total)
    for i in range(16):
        for n, lanes in lanes_of(896):
            query_out[i, :, lanes] = acc[n, pl.ds(i, 6, stride=16), :].astype(BF)
    pair_out[...] = total[96:112, 0:512]


def rotate_lanes(values, cosine, sine):
    lane = lax.broadcasted_iota(jnp.int32, values.shape, 1)
    partner = jnp.where(
        lane % 64 < 32, pltpu.roll(values, 96, axis=1), pltpu.roll(values, 32, axis=1)
    )
    return values * cosine + partner * sine


def attend_kernel(
    lengths, queries, pairs, cosine, sine, keys, values, out,
    staged, rotated, fresh_key, fresh_value, blocks, mixture, result, key_buf, value_buf, sems,
):
    requests = keys.shape[0]
    window = keys.shape[1]

    def fetch(r, n, which):
        source, target = ((keys, key_buf), (values, value_buf))[which]
        rows = pl.ds(pl.multiple_of(n * CHUNK, CHUNK), CHUNK)
        return pltpu.make_async_copy(source.at[r, rows], target.at[r, rows], sems.at[r, n, which])

    for r in range(requests):
        for n in range(window // CHUNK):

            @pl.when(lengths[r] > n * CHUNK)
            def _():
                fetch(r, n, 0).start()
                fetch(r, n, 1).start()

    for i in range(16):
        put(staged, slice(8 * i, 8 * i + 6), queries[i].astype(F32))
    for k in range(6):
        for col in range(7):
            lanes = slice(128 * col, 128 * col + 128)
            part = staged[col, pl.ds(k, 16, stride=8), :]
            turned = rotate_lanes(part, cosine[k : k + 1, :], sine[k : k + 1, :])
            rotated[16 * k : 16 * k + 16, lanes] = turned.astype(BF).astype(F32) * 0.125
    fresh_key[...] = jnp.zeros_like(fresh_key)
    fresh_value[...] = jnp.zeros_like(fresh_value)
    rounded = pairs[...].astype(BF).astype(F32)
    for col in range(4):
        lanes = slice(128 * col, 128 * col + 128)
        fresh_key[0:6, lanes] = rotate_lanes(rounded[0:6, lanes], cosine[0:6, :], sine[0:6, :])
    fresh_value[0:6, :] = rounded[6:12, :]

    sub = lax.broadcasted_iota(jnp.int32, (8, 256), 0)
    lane = lax.broadcasted_iota(jnp.int32, (8, 256), 1)
    own = sub // 2 == lane // 64
    low = lax.broadcasted_iota(jnp.int32, (8, 128), 1) < 64
    rows = LOCAL_HEADS * 16
    row = lax.broadcasted_iota(jnp.int32, (rows, 128), 0)
    column = lax.broadcasted_iota(jnp.int32, (rows, 128), 1)
    causal = column % 2 <= (row // 8) % 2
    place = lax.broadcasted_iota(jnp.int32, (rows, CHUNK), 1)

    starts = []
    for r in range(requests):
        state = []
        for g in range(2):
            for t in range(NEW):
                start = (NEW * r + t) * 16 + 8 * g
                for col in range(7):
                    part = rotated[start : start + 8, 128 * col : 128 * col + 128]
                    other = pltpu.roll(part, 64, axis=1)
                    for half in range(2):
                        both = jnp.where(low, part, other) if half == 0 else jnp.where(low, other, part)
                        both = jnp.concatenate([both, both], axis=1)
                        at = (2 * col + half) * 16 + t * 8
                        blocks[2 * r + g, at : at + 8, :] = jnp.where(own, both, 0.0)
            side = slice(256 * g, 256 * g + 256)
            query = blocks[2 * r + g].astype(BF)
            scores = lax.dot_general(query, fresh_key[:, side].astype(BF), NT, preferred_element_type=F32)
            scores = jnp.where(causal & (column // 2 == r), scores, -jnp.inf)
            top = jnp.max(scores, axis=1, keepdims=True)
            prob = jnp.exp(scores - top)
            total = jnp.sum(prob, axis=1, keepdims=True)
            mixture[2 * r + g] = jnp.dot(
                prob.astype(BF), fresh_value[:, side].astype(BF), preferred_element_type=F32
            )
            state.append((top, total))
        starts.append(tuple(state))

    for r in range(requests):
        length = lengths[r]

        def body(n, state):
            at = pl.multiple_of(n * CHUNK, CHUNK)
            active = place < length - at
            fetch(r, n, 0).wait()
            fetch(r, n, 1).wait()
            new = []
            for g in range(2):
                top, total = state[g]
                side = slice(256 * g, 256 * g + 256)
                key = key_buf[r, pl.ds(at, CHUNK), side]
                value = value_buf[r, pl.ds(at, CHUNK), side]
                query = blocks[2 * r + g].astype(BF)
                scores = lax.dot_general(query, key, NT, preferred_element_type=F32)
                scores = jnp.where(active, scores, -jnp.inf)
                higher = jnp.maximum(top, jnp.max(scores, axis=1, keepdims=True))
                shrink = jnp.exp(top - higher)
                prob = jnp.exp(scores - higher)
                total = total * shrink + jnp.sum(prob, axis=1, keepdims=True)
                mixture[2 * r + g] = mixture[2 * r + g] * shrink + jnp.dot(
                    prob.astype(BF), value, preferred_element_type=F32
                )
                new.append((higher, total))
            return tuple(new)

        state = lax.fori_loop(0, (length + CHUNK - 1) // CHUNK, body, starts[r])
        for g in range(2):
            blocks[2 * r + g] = mixture[2 * r + g] / state[g][1]
            for t in range(NEW):
                start = (NEW * r + t) * 16 + 8 * g
                for col in range(7):
                    folded = []
                    for half in range(2):
                        at = (2 * col + half) * 16 + t * 8
                        part = jnp.where(own, blocks[2 * r + g, at : at + 8, :], 0.0)
                        part = part[:, 0:128] + part[:, 128:256]
                        folded.append(part + pltpu.roll(part, 64, axis=1))
                    result[col, start : start + 8, :] = jnp.where(low, folded[0], folded[1])
    for i in range(16):
        for n, lanes in lanes_of(896):
            out[i, :, lanes] = result[n, pl.ds(i, 6, stride=16), :].astype(BF)


def repack_kernel(block, out, staged):
    for i in range(16):
        put(staged, slice(8 * i, 8 * i + 6), block[i].astype(F32))
    for k in range(6):
        for n, lanes in lanes_of(896):
            out[16 * k : 16 * k + 16, lanes] = staged[n, pl.ds(k, 16, stride=8), :].astype(BF)


def output_kernel(b0, b1, b2, b3, s0, s1, s2, s3, chosen, plain, scale, extra, weight, out, left, acc):
    y, c, _, _ = here()
    for blocks, core in (((b0, b1, b2, b3), c), ((s0, s1, s2, s3), 1 - c)):
        for d, block in enumerate(blocks):
            j = 2 * lax.rem(y + N_Y - d, N_Y) + core
            left[pl.ds(pl.multiple_of(96 * j, 96), 96), :] = block[...]
    step = 192
    for n in range(768 // step):
        rows = slice(n * step, n * step + step)
        part = left[rows, :]
        picked = jnp.dot(part, chosen[...], preferred_element_type=F32)
        term = lax.dot_general(part * plain[...], weight[...], NT, preferred_element_type=F32) * scale[...]
        for k in range(OUTL):
            term = term + picked[:, k : k + 1] * extra[k : k + 1, :]
        put(acc, rows, term)
    for i in range(16):
        for n, lanes in lanes_of(out.shape[2]):
            got = acc[n, pl.ds(i, 48, stride=16), :].astype(BF)
            out[i, :, lanes] = got[:, 0 : lanes.stop - lanes.start]


def total_kernel(parts, out):
    total = parts[0].astype(F32)
    for i in range(1, 16):
        total = total + parts[i].astype(F32)
    out[...] = total.astype(BF)


def params(mib=48):
    return pltpu.CompilerParams(vmem_limit_bytes=mib * MIB)


def over_y(shift):
    return [(2 * y + c, 2 * ((y + shift) % N_Y) + c) for y in range(N_Y) for c in range(2)]


def shift_plane(first, shift):
    pairs = []
    for z in range(4):
        for x in range(4):
            for j in range(2 * N_Y):
                if (j % 2 == 0) == first:
                    to = z * 4 + (x + shift) % 4
                else:
                    to = (z + shift) % 4 * 4 + x
                pairs.append(((z * 4 + x) * 2 * N_Y + j, to * 2 * N_Y + j))
    return pairs


def sheets():
    groups = []
    for first in (True, False):
        for fixed in range(4):
            group = []
            for moving in range(4):
                z, x = (moving, fixed) if first else (fixed, moving)
                for y in range(N_Y):
                    group.append((z * 4 + x) * 2 * N_Y + 2 * y + (0 if first else 1))
            groups.append(group)
    return groups


SIBLING = [(j, j ^ 1) for j in range(2 * N_Y)]


def on_device(
    activations,
    norm_gain,
    norm_bias,
    input_outliers,
    query_int,
    query_scale,
    keyvalue_int,
    keyvalue_scale,
    query_float,
    keyvalue_float,
    key_cache,
    value_cache,
    lengths,
    middle_outliers,
    output_int,
    output_scale,
    output_float,
):
    block_rows, features = activations.shape
    tokens = block_rows * 16
    columns = query_int.shape[1]
    out_columns = output_int.shape[1]
    me_x = lax.axis_index("gx")
    smem = pl.BlockSpec(memory_space=pltpu.SMEM)
    vmem = pl.BlockSpec(memory_space=pltpu.VMEM)

    picked = jnp.arange(features, dtype=jnp.int32)[:, None] == input_outliers[None, :]
    is_outlier = jnp.any(picked, axis=1)
    gain = jnp.where(is_outlier, 0.0, norm_gain)[None]
    bias = jnp.where(is_outlier, 0.0, norm_bias)[None]
    gain_out = jnp.sum(jnp.where(picked, norm_gain[:, None], 0.0), axis=0)[None]
    bias_out = jnp.sum(jnp.where(picked, norm_bias[:, None], 0.0), axis=0)[None]
    padded = features + 64
    own, kept, sent = pl.pallas_call(
        prepare_kernel,
        in_specs=[smem, vmem],
        out_specs=[vmem] * 3,
        out_shape=[
            jax.ShapeDtypeStruct((block_rows, padded), BF),
            jax.ShapeDtypeStruct((block_rows // 2, padded), BF),
            jax.ShapeDtypeStruct((block_rows // 2, padded), BF),
        ],
        compiler_params=params(8),
        name="prepare",
    )(input_outliers, activations)
    plane = ("gx", "gy")
    both = jnp.stack([kept, lax.ppermute(sent, "gy", SIBLING)])
    both = jnp.concatenate(
        [both] + [lax.ppermute(both, plane, shift_plane(True, d)) for d in (1, 3, 2)], axis=1
    )
    arrived = [both] + [lax.ppermute(both, plane, shift_plane(False, d)) for d in (1, 3, 2)]
    sums = pl.pallas_call(
        sums_kernel,
        out_shape=jax.ShapeDtypeStruct((16, 2, 96), F32),
        compiler_params=params(8),
        name="row_sums",
    )(both)
    sums = lax.all_to_all(
        sums, plane, split_axis=0, concat_axis=0, tiled=True, axis_index_groups=sheets()
    )
    mine = jnp.sum(sums.reshape(4, N_Y, 2, 96), axis=1)
    other = lax.ppermute(mine, "gy", SIBLING)
    *arrived, mine, other = lax.optimization_barrier((*arrived, mine, other))
    pairs = pl.pallas_call(
        pair_kernel,
        in_specs=[vmem] * 10,
        out_specs=vmem,
        out_shape=jax.ShapeDtypeStruct((2 * N_Y, 16, 512), F32),
        compiler_params=params(16),
        name="pair_projection",
    )(
        own, mine, other, gain, bias, gain_out, bias_out,
        keyvalue_scale[None], keyvalue_float, keyvalue_int,
    )
    others = [lax.ppermute(block[1], "gy", SIBLING) for block in arrived]
    order = (0, 1, 3, 2)
    arrived = [arrived[n] for n in order]
    others = [others[n] for n in order]

    keep, send = pl.pallas_call(
        query_kernel,
        grid=(1,),
        in_specs=[whole((1, 96, padded))] * 4 + [vmem] * 14,
        out_specs=[vmem] * 2,
        out_shape=[jax.ShapeDtypeStruct((N_Y, 112, columns), BF)] * 2,
        scratch_shapes=[pltpu.VMEM((7, tokens, 128), F32)],
        compiler_params=params(24),
        name="query_projection",
    )(
        *arrived, *others, mine, other, gain, bias, gain_out, bias_out,
        query_scale[None], query_float, query_int, pairs,
    )
    received = lax.ppermute(send, "gy", SIBLING)
    piece = jax.ShapeDtypeStruct((112, columns), BF)
    mine, to1, to2, to3 = pl.pallas_call(
        add_kernel, out_shape=[piece] * 4, compiler_params=params(8), name="add_cores"
    )(keep, received)
    from1 = lax.ppermute(to1, "gy", over_y(1))
    from3 = lax.ppermute(to3, "gy", over_y(3))
    from2 = lax.ppermute(to2, "gy", over_y(2))
    summed, pair_sums = pl.pallas_call(
        collect_kernel,
        out_shape=[
            jax.ShapeDtypeStruct((16, 6, columns), BF),
            jax.ShapeDtypeStruct((16, 512), F32),
        ],
        scratch_shapes=[pltpu.VMEM((7, 112, 128), F32)],
        compiler_params=params(8),
        name="collect",
    )(mine, from1, from2, from3)
    queries = lax.all_to_all(summed, "gx", split_axis=0, concat_axis=0, tiled=True)

    positions = (lengths[:, None] + jnp.arange(NEW, dtype=jnp.int32)[None, :]).reshape(6, 1)
    frequency = jnp.exp(jnp.arange(32, dtype=F32) * (-2.0 * math.log(rope_base) / HEAD))
    angles = positions.astype(F32) * frequency[None, :]
    cosine = jnp.tile(jnp.cos(angles), (1, 4))
    sine = jnp.sin(angles)
    sine = jnp.concatenate([-sine, sine, -sine, sine], axis=1)
    cosine = jnp.pad(cosine, ((0, 2), (0, 0)))
    sine = jnp.pad(sine, ((0, 2), (0, 0)))

    requests, window, cached = key_cache.shape
    hbm = pl.BlockSpec(memory_space=pltpu.HBM)
    attended = pl.pallas_call(
        attend_kernel,
        in_specs=[smem, vmem, vmem, vmem, vmem, hbm, hbm],
        out_specs=vmem,
        out_shape=jax.ShapeDtypeStruct((16, 6, columns), BF),
        scratch_shapes=[
            pltpu.VMEM((7, 128, 128), F32),
            pltpu.VMEM((96, columns), F32),
            pltpu.VMEM((128, cached), F32),
            pltpu.VMEM((128, cached), F32),
            pltpu.VMEM((6, 224, 256), F32),
            pltpu.VMEM((6, 224, 256), F32),
            pltpu.VMEM((7, 96, 128), F32),
            pltpu.VMEM((requests, window, cached), BF),
            pltpu.VMEM((requests, window, cached), BF),
            pltpu.SemaphoreType.DMA((requests, window // CHUNK, 2)),
        ],
        compiler_params=params(57),
        name="attention",
    )(lengths, queries, pair_sums, cosine, sine, key_cache, value_cache)

    back = lax.all_to_all(attended, "gx", split_axis=0, concat_axis=0, tiled=True)
    mine = pl.pallas_call(
        repack_kernel,
        out_shape=jax.ShapeDtypeStruct((96, columns), BF),
        scratch_shapes=[pltpu.VMEM((7, 128, 128), F32)],
        compiler_params=params(8),
        name="repack",
    )(back)
    blocks = [mine] + [lax.ppermute(mine, "gy", over_y(d)) for d in (1, 2, 3)]
    blocks = blocks + [lax.ppermute(b, "gy", SIBLING) for b in blocks]

    middle = lax.dynamic_slice(middle_outliers, (me_x * OUTL,), (OUTL,))
    chosen = jnp.arange(columns, dtype=jnp.int32)[:, None] == middle[None, :]
    plain = jnp.where(jnp.any(chosen, axis=1), 0.0, 1.0).astype(BF)[None]
    chosen = jnp.pad(chosen.astype(BF), ((0, 0), (0, 128 - OUTL)))
    partial = pl.pallas_call(
        output_kernel,
        in_specs=[vmem] * 13,
        out_specs=vmem,
        out_shape=jax.ShapeDtypeStruct((16, block_rows, out_columns), BF),
        scratch_shapes=[pltpu.VMEM((tokens, columns), BF), pltpu.VMEM((15, tokens, 128), F32)],
        compiler_params=params(28),
        name="output_projection",
    )(*blocks, chosen, plain, output_scale[None], output_float, output_int.T)
    parts = lax.all_to_all(partial, "gx", split_axis=0, concat_axis=0, tiled=True)
    return pl.pallas_call(
        total_kernel,
        out_shape=jax.ShapeDtypeStruct((block_rows, out_columns), BF),
        compiler_params=params(16),
        name="total",
    )(parts)


def solution(mesh):
    placed = (
        P("gx", "gy"),
        P("gy"),
        P("gy"),
        P("gy"),
        P("gy", "gx"),
        P("gx"),
        P("gy", None),
        P(),
        P("gy", "gx"),
        P("gy", None),
        P(("gx", "gy"), None, None),
        P(("gx", "gy"), None, None),
        P(("gx", "gy")),
        P(),
        P("gx", "gy"),
        P("gy"),
        P("gx", "gy"),
    )
    return jax.shard_map(
        on_device, mesh=mesh, in_specs=placed, out_specs=P("gx", "gy"), check_vma=False
    )
```

```python
import functools
import math

import jax
import jax.numpy as jnp
from jax import lax
from jax.experimental import pallas as pl
from jax.experimental.pallas import tpu as pltpu
from jax.sharding import PartitionSpec as P

D = 14848
HEAD = 64
KV = 8
GROUP = 28
OUTL = 4
NEW = 2
N_Y = 4
LOCAL_HEADS = 14
CHUNK = 512

epsilon = 1e-05
rope_base = 10000.0
BF = jnp.bfloat16
F32 = jnp.float32
MIB = 1024 * 1024
STEPS = (0, 1, 3, 2)
NT = (((1,), (1,)), ((), ()))


def lanes_of(columns):
    return [(n, slice(128 * n, min(128 * n + 128, columns))) for n in range((columns + 127) // 128)]


def put(ref, rows, values):
    for n, lanes in lanes_of(values.shape[1]):
        ref[n, rows, 0 : lanes.stop - lanes.start] = values[:, lanes]


def whole(shape):
    return pl.BlockSpec(shape, lambda *_: (0,) * len(shape))


def here():
    i = lax.axis_index("gx")
    j = lax.axis_index("gy")
    return lax.div(j, 2), lax.rem(j, 2), lax.div(i, 4), lax.rem(i, 4)


def prepare_kernel(positions, x, own, keep, send):
    rows, features = x.shape
    place = lax.broadcasted_iota(jnp.int32, (features, 128), 0)
    column = lax.broadcasted_iota(jnp.int32, (features, 128), 1)
    picked = (place == positions[0]) & (column == 0)
    for k in range(1, OUTL):
        picked = picked | ((place == positions[k]) & (column == k))
    picked = picked.astype(F32).astype(BF)
    outlier = jnp.dot(x[...], picked, preferred_element_type=F32)
    values = x[...].astype(F32)
    own[:, 0:features] = x[...]
    own[:, features:] = outlier[:, 0:64].astype(BF)
    half = rows // 2
    first = here()[1] == 0
    for out, flag in ((keep, first), (send, jnp.logical_not(first))):
        out[:, 0:features] = jnp.where(flag, values[0:half], values[half:]).astype(BF)
        out[:, features:] = jnp.where(flag, outlier[0:half, 0:64], outlier[half:, 0:64]).astype(BF)


def diagonal(size):
    return lax.broadcasted_iota(jnp.int32, (size, size), 0) == lax.broadcasted_iota(
        jnp.int32, (size, size), 1
    )


def sums_kernel(both, out):
    features = both.shape[2] - 64
    rows = both.shape[1]
    first = jnp.zeros((rows, 1), F32)
    second = jnp.zeros((rows, 1), F32)
    for part in range(2):
        values = both[part, :, 0:features].astype(F32)
        first = first + jnp.sum(values, axis=1, keepdims=True)
        second = second + jnp.sum(values * values, axis=1, keepdims=True)
    unit = diagonal(rows)
    first = jnp.sum(jnp.where(unit, first, 0.0), axis=0, keepdims=True)
    second = jnp.sum(jnp.where(unit, second, 0.0), axis=0, keepdims=True)
    for n in range(16):
        out[n, 0:1, :] = first
        out[n, 1:2, :] = second


def moments(sums):
    unit = diagonal(sums.shape[1])
    average = jnp.sum(jnp.where(unit, sums[0:1, :], 0.0), axis=1, keepdims=True) / D
    squares = jnp.sum(jnp.where(unit, sums[1:2, :], 0.0), axis=1, keepdims=True) / D
    return average, lax.rsqrt(squares - average * average + epsilon)


def normalize(rows, average, inverse, gain, bias, gain_out, bias_out, features):
    regular = ((rows[:, 0:features].astype(F32) - average) * inverse * gain + bias).astype(BF)
    outlier = (rows[:, features : features + OUTL].astype(F32) - average) * inverse * gain_out + bias_out
    return regular, outlier.astype(BF).astype(F32)


def pair_kernel(own, mine, other, gain, bias, gain_out, bias_out, scale, extra, weight, out):
    _, c, z, x = here()
    features = weight.shape[0]
    half = own.shape[0] // 2
    first = c == 0
    mine_at = mine[jnp.where(first, z, x)]
    other_at = other[jnp.where(first, x, z)]
    average0, inverse0 = moments(jnp.where(first, mine_at, other_at))
    average1, inverse1 = moments(jnp.where(first, other_at, mine_at))
    average = jnp.concatenate([average0[0:half], average1[0:half]], axis=0)
    inverse = jnp.concatenate([inverse0[0:half], inverse1[0:half]], axis=0)
    regular, outlier = normalize(
        own[...], average, inverse, gain[...], bias[...], gain_out[...], bias_out[...], features
    )
    term = jnp.dot(regular, weight[...], preferred_element_type=F32) * scale[...]
    for k in range(OUTL):
        term = term + outlier[:, k : k + 1] * extra[k : k + 1, :]
    for j in range(2 * N_Y):
        rows = slice(6 * j, 6 * j + 6)
        out[j, 0:6, :] = term[rows, 0:512]
        out[j, 6:12, :] = term[rows, 512:1024]
        out[j, 12:16, :] = jnp.zeros((4, 512), F32)


def query_kernel(
    a0, a1, a2, a3, b0, b1, b2, b3, mine, other, gain, bias, gain_out, bias_out,
    scale, extra, weight, pairs, keep, send, acc,
):
    y, c, z, x = here()
    features = weight.shape[0]
    for d2, (near, far) in enumerate(((a0, b0), (a1, b1), (a2, b2), (a3, b3))):
        regulars = []
        outliers = []
        for side, rows in enumerate((near[0], far[...])):
            sums = (mine, other)[side][lax.rem(jnp.where((c == 0) == (side == 0), z, x) + 4 - d2, 4)]
            average, inverse = moments(sums)
            regular, outlier = normalize(
                rows, average, inverse, gain[...], bias[...], gain_out[...], bias_out[...], features
            )
            regulars.append(regular)
            outliers.append(outlier)
        rows = jnp.concatenate(regulars, axis=0)
        value = jnp.concatenate(outliers, axis=0)
        term = jnp.dot(rows, weight[...], preferred_element_type=F32) * scale[...]
        for k in range(OUTL):
            term = term + value[:, k : k + 1] * extra[k : k + 1, :]
        for side in range(2):
            half = c if side == 0 else 1 - c
            for d1 in range(4):
                along_x = lax.rem(x + 4 - jnp.where(half == 0, STEPS[d1], d2), 4)
                along_z = lax.rem(z + 4 - jnp.where(half == 0, d2, STEPS[d1]), 4)
                at = pl.multiple_of((along_z * 4 + along_x) * 48 + half * 24, 8)
                row = side * 96 + d1 * 24
                put(acc, pl.ds(at, 24), term[row : row + 24, :])
    for out, core in ((keep, c), (send, 1 - c)):
        for d in range(N_Y):
            j = 2 * lax.rem(y + d, N_Y) + core
            for k in range(6):
                for n, lanes in lanes_of(896):
                    out[d, 16 * k : 16 * k + 16, lanes] = acc[n, pl.ds(6 * j + k, 16, stride=48), :].astype(BF)
            out[d, 96:112, 0:512] = pairs[j].astype(BF)
            out[d, 96:112, 512:896] = jnp.zeros((16, 384), BF)


def add_kernel(keep, received, o0, o1, o2, o3):
    for d, out in enumerate((o0, o1, o2, o3)):
        out[...] = (keep[d].astype(F32) + received[d].astype(F32)).astype(BF)


def collect_kernel(a, b, c, d, query_out, pair_out, acc):
    total = (a[...].astype(F32) + b[...].astype(F32)) + (c[...].astype(F32) + d[...].astype(F32))
    put(acc, slice(0, 112), total)
    for i in range(16):
        for n, lanes in lanes_of(896):
            query_out[i, :, lanes] = acc[n, pl.ds(i, 6, stride=16), :].astype(BF)
    pair_out[...] = total[96:112, 0:512]


def rotate_lanes(values, cosine, sine):
    lane = lax.broadcasted_iota(jnp.int32, values.shape, 1)
    partner = jnp.where(
        lane % 64 < 32, pltpu.roll(values, 96, axis=1), pltpu.roll(values, 32, axis=1)
    )
    return values * cosine + partner * sine


def attend_kernel(
    lengths, queries, pairs, cosine, sine, keys, values, out,
    staged, rotated, fresh_key, fresh_value, blocks, mixture, result, key_buf, value_buf, sems,
):
    requests = keys.shape[0]
    window = keys.shape[1]

    def fetch(r, n, which):
        source, target = ((keys, key_buf), (values, value_buf))[which]
        rows = pl.ds(pl.multiple_of(n * CHUNK, CHUNK), CHUNK)
        return pltpu.make_async_copy(source.at[r, rows], target.at[r, rows], sems.at[r, n, which])

    for r in range(requests):
        for n in range(window // CHUNK):

            @pl.when(lengths[r] > n * CHUNK)
            def _():
                fetch(r, n, 0).start()
                fetch(r, n, 1).start()

    for i in range(16):
        put(staged, slice(8 * i, 8 * i + 6), queries[i].astype(F32))
    for k in range(6):
        for col in range(7):
            lanes = slice(128 * col, 128 * col + 128)
            part = staged[col, pl.ds(k, 16, stride=8), :]
            turned = rotate_lanes(part, cosine[k : k + 1, :], sine[k : k + 1, :])
            rotated[16 * k : 16 * k + 16, lanes] = turned.astype(BF).astype(F32) * 0.125
    fresh_key[...] = jnp.zeros_like(fresh_key)
    fresh_value[...] = jnp.zeros_like(fresh_value)
    rounded = pairs[...].astype(BF).astype(F32)
    for col in range(4):
        lanes = slice(128 * col, 128 * col + 128)
        fresh_key[0:6, lanes] = rotate_lanes(rounded[0:6, lanes], cosine[0:6, :], sine[0:6, :])
    fresh_value[0:6, :] = rounded[6:12, :]

    sub = lax.broadcasted_iota(jnp.int32, (8, 256), 0)
    lane = lax.broadcasted_iota(jnp.int32, (8, 256), 1)
    own = sub // 2 == lane // 64
    low = lax.broadcasted_iota(jnp.int32, (8, 128), 1) < 64
    rows = LOCAL_HEADS * 16
    row = lax.broadcasted_iota(jnp.int32, (rows, 128), 0)
    column = lax.broadcasted_iota(jnp.int32, (rows, 128), 1)
    causal = column % 2 <= (row // 8) % 2
    place = lax.broadcasted_iota(jnp.int32, (rows, CHUNK), 1)

    starts = []
    for r in range(requests):
        state = []
        for g in range(2):
            for t in range(NEW):
                start = (NEW * r + t) * 16 + 8 * g
                for col in range(7):
                    part = rotated[start : start + 8, 128 * col : 128 * col + 128]
                    other = pltpu.roll(part, 64, axis=1)
                    for half in range(2):
                        both = jnp.where(low, part, other) if half == 0 else jnp.where(low, other, part)
                        both = jnp.concatenate([both, both], axis=1)
                        at = (2 * col + half) * 16 + t * 8
                        blocks[2 * r + g, at : at + 8, :] = jnp.where(own, both, 0.0)
            side = slice(256 * g, 256 * g + 256)
            query = blocks[2 * r + g].astype(BF)
            scores = lax.dot_general(query, fresh_key[:, side].astype(BF), NT, preferred_element_type=F32)
            scores = jnp.where(causal & (column // 2 == r), scores, -jnp.inf)
            top = jnp.max(scores, axis=1, keepdims=True)
            prob = jnp.exp(scores - top)
            total = jnp.sum(prob, axis=1, keepdims=True)
            mixture[2 * r + g] = jnp.dot(
                prob.astype(BF), fresh_value[:, side].astype(BF), preferred_element_type=F32
            )
            state.append((top, total))
        starts.append(tuple(state))

    for r in range(requests):
        length = lengths[r]

        def body(n, state):
            at = pl.multiple_of(n * CHUNK, CHUNK)
            active = place < length - at
            fetch(r, n, 0).wait()
            fetch(r, n, 1).wait()
            new = []
            for g in range(2):
                top, total = state[g]
                side = slice(256 * g, 256 * g + 256)
                key = key_buf[r, pl.ds(at, CHUNK), side]
                value = value_buf[r, pl.ds(at, CHUNK), side]
                query = blocks[2 * r + g].astype(BF)
                scores = lax.dot_general(query, key, NT, preferred_element_type=F32)
                scores = jnp.where(active, scores, -jnp.inf)
                higher = jnp.maximum(top, jnp.max(scores, axis=1, keepdims=True))
                shrink = jnp.exp(top - higher)
                prob = jnp.exp(scores - higher)
                total = total * shrink + jnp.sum(prob, axis=1, keepdims=True)
                mixture[2 * r + g] = mixture[2 * r + g] * shrink + jnp.dot(
                    prob.astype(BF), value, preferred_element_type=F32
                )
                new.append((higher, total))
            return tuple(new)

        state = lax.fori_loop(0, (length + CHUNK - 1) // CHUNK, body, starts[r])
        for g in range(2):
            blocks[2 * r + g] = mixture[2 * r + g] / state[g][1]
            for t in range(NEW):
                start = (NEW * r + t) * 16 + 8 * g
                for col in range(7):
                    folded = []
                    for half in range(2):
                        at = (2 * col + half) * 16 + t * 8
                        part = jnp.where(own, blocks[2 * r + g, at : at + 8, :], 0.0)
                        part = part[:, 0:128] + part[:, 128:256]
                        folded.append(part + pltpu.roll(part, 64, axis=1))
                    result[col, start : start + 8, :] = jnp.where(low, folded[0], folded[1])
    for i in range(16):
        for n, lanes in lanes_of(896):
            out[i, :, lanes] = result[n, pl.ds(i, 6, stride=16), :].astype(BF)


def repack_kernel(block, out, staged):
    for i in range(16):
        put(staged, slice(8 * i, 8 * i + 6), block[i].astype(F32))
    for k in range(6):
        for n, lanes in lanes_of(896):
            out[16 * k : 16 * k + 16, lanes] = staged[n, pl.ds(k, 16, stride=8), :].astype(BF)


def output_kernel(
    sending, b0, b1, b2, b3, s0, s1, s2, s3, chosen, plain, scale, extra, weight, out, left, acc
):
    y, c, z, x = here()
    half = 1 - c if sending else c
    for blocks, core in (((b0, b1, b2, b3), c), ((s0, s1, s2, s3), 1 - c)):
        for d, block in enumerate(blocks):
            j = 2 * lax.rem(y + N_Y - d, N_Y) + core
            left[pl.ds(pl.multiple_of(96 * j, 96), 96), :] = block[...]
    step = 192
    for n in range(384 // step):
        part = left[pl.ds(pl.multiple_of(half * 384 + n * step, step), step), :]
        picked = jnp.dot(part, chosen[...], preferred_element_type=F32)
        term = lax.dot_general(part * plain[...], weight[...], NT, preferred_element_type=F32) * scale[...]
        for k in range(OUTL):
            term = term + picked[:, k : k + 1] * extra[k : k + 1, :]
        put(acc, slice(n * step, n * step + step), term)
    for d in range(4):
        owners = []
        for f in range(4):
            along_x = lax.rem(x + jnp.where(half == 0, f, d), 4)
            along_z = lax.rem(z + jnp.where(half == 0, d, f), 4)
            owners.append(along_z * 4 + along_x)
        for n, lanes in lanes_of(out.shape[2]):
            got = [acc[n, pl.ds(i, 24, stride=16), :] for i in owners]
            got = jnp.concatenate(got, axis=0).astype(BF)
            out[d, :, lanes] = got[:, 0 : lanes.stop - lanes.start]


def first_sum_kernel(mine, other, r1, r3, r2, o0, o1, o2, o3):
    for part, start in enumerate((mine, other)):
        total = start[0].astype(F32) + r1[part].astype(F32)
        total = total + (r3[part].astype(F32) + r2[part].astype(F32))
        for f, out in enumerate((o0, o1, o2, o3)):
            out[part] = total[24 * f : 24 * f + 24, :].astype(BF)


def last_sum_kernel(own, r1, r3, r2, keep, send):
    for part, out in enumerate((keep, send)):
        total = own[part].astype(F32) + r1[part].astype(F32)
        out[...] = (total + (r3[part].astype(F32) + r2[part].astype(F32))).astype(BF)


def join_kernel(mine, other, out):
    first = here()[1] == 0
    a = mine[...].astype(F32)
    b = other[...].astype(F32)
    joined = jnp.concatenate([jnp.where(first, a, b), jnp.where(first, b, a)], axis=0)
    out[...] = joined.astype(BF)


def params(mib=48):
    return pltpu.CompilerParams(vmem_limit_bytes=mib * MIB)


def over_y(shift):
    return [(2 * y + c, 2 * ((y + shift) % N_Y) + c) for y in range(N_Y) for c in range(2)]


def shift_plane(first, shift):
    pairs = []
    for z in range(4):
        for x in range(4):
            for j in range(2 * N_Y):
                if (j % 2 == 0) == first:
                    to = z * 4 + (x + shift) % 4
                else:
                    to = (z + shift) % 4 * 4 + x
                pairs.append(((z * 4 + x) * 2 * N_Y + j, to * 2 * N_Y + j))
    return pairs


def sheets():
    groups = []
    for first in (True, False):
        for fixed in range(4):
            group = []
            for moving in range(4):
                z, x = (moving, fixed) if first else (fixed, moving)
                for y in range(N_Y):
                    group.append((z * 4 + x) * 2 * N_Y + 2 * y + (0 if first else 1))
            groups.append(group)
    return groups


SIBLING = [(j, j ^ 1) for j in range(2 * N_Y)]


def on_device(
    activations,
    norm_gain,
    norm_bias,
    input_outliers,
    query_int,
    query_scale,
    keyvalue_int,
    keyvalue_scale,
    query_float,
    keyvalue_float,
    key_cache,
    value_cache,
    lengths,
    middle_outliers,
    output_int,
    output_scale,
    output_float,
):
    block_rows, features = activations.shape
    tokens = block_rows * 16
    columns = query_int.shape[1]
    out_columns = output_int.shape[1]
    me_x = lax.axis_index("gx")
    smem = pl.BlockSpec(memory_space=pltpu.SMEM)
    vmem = pl.BlockSpec(memory_space=pltpu.VMEM)

    picked = jnp.arange(features, dtype=jnp.int32)[:, None] == input_outliers[None, :]
    is_outlier = jnp.any(picked, axis=1)
    gain = jnp.where(is_outlier, 0.0, norm_gain)[None]
    bias = jnp.where(is_outlier, 0.0, norm_bias)[None]
    gain_out = jnp.sum(jnp.where(picked, norm_gain[:, None], 0.0), axis=0)[None]
    bias_out = jnp.sum(jnp.where(picked, norm_bias[:, None], 0.0), axis=0)[None]
    padded = features + 64
    own, kept, sent = pl.pallas_call(
        prepare_kernel,
        in_specs=[smem, vmem],
        out_specs=[vmem] * 3,
        out_shape=[
            jax.ShapeDtypeStruct((block_rows, padded), BF),
            jax.ShapeDtypeStruct((block_rows // 2, padded), BF),
            jax.ShapeDtypeStruct((block_rows // 2, padded), BF),
        ],
        compiler_params=params(8),
        name="prepare",
    )(input_outliers, activations)
    plane = ("gx", "gy")
    both = jnp.stack([kept, lax.ppermute(sent, "gy", SIBLING)])
    both = jnp.concatenate(
        [both] + [lax.ppermute(both, plane, shift_plane(True, d)) for d in (1, 3, 2)], axis=1
    )
    arrived = [both] + [lax.ppermute(both, plane, shift_plane(False, d)) for d in (1, 3, 2)]
    sums = pl.pallas_call(
        sums_kernel,
        out_shape=jax.ShapeDtypeStruct((16, 2, 96), F32),
        compiler_params=params(8),
        name="row_sums",
    )(both)
    sums = lax.all_to_all(
        sums, plane, split_axis=0, concat_axis=0, tiled=True, axis_index_groups=sheets()
    )
    mine = jnp.sum(sums.reshape(4, N_Y, 2, 96), axis=1)
    other = lax.ppermute(mine, "gy", SIBLING)
    *arrived, mine, other = lax.optimization_barrier((*arrived, mine, other))
    pairs = pl.pallas_call(
        pair_kernel,
        in_specs=[vmem] * 10,
        out_specs=vmem,
        out_shape=jax.ShapeDtypeStruct((2 * N_Y, 16, 512), F32),
        compiler_params=params(16),
        name="pair_projection",
    )(
        own, mine, other, gain, bias, gain_out, bias_out,
        keyvalue_scale[None], keyvalue_float, keyvalue_int,
    )
    others = [lax.ppermute(block[1], "gy", SIBLING) for block in arrived]
    order = (0, 1, 3, 2)
    arrived = [arrived[n] for n in order]
    others = [others[n] for n in order]

    keep, send = pl.pallas_call(
        query_kernel,
        grid=(1,),
        in_specs=[whole((1, 96, padded))] * 4 + [vmem] * 14,
        out_specs=[vmem] * 2,
        out_shape=[jax.ShapeDtypeStruct((N_Y, 112, columns), BF)] * 2,
        scratch_shapes=[pltpu.VMEM((7, tokens, 128), F32)],
        compiler_params=params(24),
        name="query_projection",
    )(
        *arrived, *others, mine, other, gain, bias, gain_out, bias_out,
        query_scale[None], query_float, query_int, pairs,
    )
    received = lax.ppermute(send, "gy", SIBLING)
    piece = jax.ShapeDtypeStruct((112, columns), BF)
    mine, to1, to2, to3 = pl.pallas_call(
        add_kernel, out_shape=[piece] * 4, compiler_params=params(8), name="add_cores"
    )(keep, received)
    from1 = lax.ppermute(to1, "gy", over_y(1))
    from3 = lax.ppermute(to3, "gy", over_y(3))
    from2 = lax.ppermute(to2, "gy", over_y(2))
    summed, pair_sums = pl.pallas_call(
        collect_kernel,
        out_shape=[
            jax.ShapeDtypeStruct((16, 6, columns), BF),
            jax.ShapeDtypeStruct((16, 512), F32),
        ],
        scratch_shapes=[pltpu.VMEM((7, 112, 128), F32)],
        compiler_params=params(8),
        name="collect",
    )(mine, from1, from2, from3)
    queries = lax.all_to_all(summed, "gx", split_axis=0, concat_axis=0, tiled=True)

    positions = (lengths[:, None] + jnp.arange(NEW, dtype=jnp.int32)[None, :]).reshape(6, 1)
    frequency = jnp.exp(jnp.arange(32, dtype=F32) * (-2.0 * math.log(rope_base) / HEAD))
    angles = positions.astype(F32) * frequency[None, :]
    cosine = jnp.tile(jnp.cos(angles), (1, 4))
    sine = jnp.sin(angles)
    sine = jnp.concatenate([-sine, sine, -sine, sine], axis=1)
    cosine = jnp.pad(cosine, ((0, 2), (0, 0)))
    sine = jnp.pad(sine, ((0, 2), (0, 0)))

    requests, window, cached = key_cache.shape
    hbm = pl.BlockSpec(memory_space=pltpu.HBM)
    attended = pl.pallas_call(
        attend_kernel,
        in_specs=[smem, vmem, vmem, vmem, vmem, hbm, hbm],
        out_specs=vmem,
        out_shape=jax.ShapeDtypeStruct((16, 6, columns), BF),
        scratch_shapes=[
            pltpu.VMEM((7, 128, 128), F32),
            pltpu.VMEM((96, columns), F32),
            pltpu.VMEM((128, cached), F32),
            pltpu.VMEM((128, cached), F32),
            pltpu.VMEM((6, 224, 256), F32),
            pltpu.VMEM((6, 224, 256), F32),
            pltpu.VMEM((7, 96, 128), F32),
            pltpu.VMEM((requests, window, cached), BF),
            pltpu.VMEM((requests, window, cached), BF),
            pltpu.SemaphoreType.DMA((requests, window // CHUNK, 2)),
        ],
        compiler_params=params(57),
        name="attention",
    )(lengths, queries, pair_sums, cosine, sine, key_cache, value_cache)

    back = lax.all_to_all(attended, "gx", split_axis=0, concat_axis=0, tiled=True)
    mine = pl.pallas_call(
        repack_kernel,
        out_shape=jax.ShapeDtypeStruct((96, columns), BF),
        scratch_shapes=[pltpu.VMEM((7, 128, 128), F32)],
        compiler_params=params(8),
        name="repack",
    )(back)
    blocks = [mine] + [lax.ppermute(mine, "gy", over_y(d)) for d in (1, 2, 3)]
    blocks = blocks + [lax.ppermute(b, "gy", SIBLING) for b in blocks]

    middle = lax.dynamic_slice(middle_outliers, (me_x * OUTL,), (OUTL,))
    chosen = jnp.arange(columns, dtype=jnp.int32)[:, None] == middle[None, :]
    plain = jnp.where(jnp.any(chosen, axis=1), 0.0, 1.0).astype(BF)[None]
    chosen = jnp.pad(chosen.astype(BF), ((0, 0), (0, 128 - OUTL)))
    half_rows = block_rows // 2

    def project(sending):
        return pl.pallas_call(
            functools.partial(output_kernel, sending),
            in_specs=[vmem] * 13,
            out_specs=vmem,
            out_shape=jax.ShapeDtypeStruct((4, 4 * half_rows, out_columns), BF),
            scratch_shapes=[
                pltpu.VMEM((tokens, columns), BF),
                pltpu.VMEM((15, tokens // 2, 128), F32),
            ],
            compiler_params=params(24),
            name="output_sent" if sending else "output_kept",
        )(*blocks, chosen, plain, output_scale[None], output_float, output_int.T)

    other = lax.ppermute(project(True), "gy", SIBLING)
    kept = project(False)
    steps = (1, 3, 2)
    got = [
        lax.ppermute(jnp.stack([kept[d], other[d]]), plane, shift_plane(False, d)) for d in steps
    ]
    quarter = jax.ShapeDtypeStruct((2, half_rows, out_columns), BF)
    sums = pl.pallas_call(
        first_sum_kernel,
        grid=(1,),
        in_specs=[whole((1, 4 * half_rows, out_columns))] * 2 + [vmem] * 3,
        out_specs=[vmem] * 4,
        out_shape=[quarter] * 4,
        compiler_params=params(16),
        name="first_sum",
    )(kept, other, *got)
    got = [lax.ppermute(sums[f], plane, shift_plane(True, f)) for f in steps]
    half = jax.ShapeDtypeStruct((half_rows, out_columns), BF)
    keep, send = pl.pallas_call(
        last_sum_kernel, out_shape=[half] * 2, compiler_params=params(8), name="last_sum"
    )(sums[0], *got)
    return pl.pallas_call(
        join_kernel,
        out_shape=jax.ShapeDtypeStruct((block_rows, out_columns), BF),
        compiler_params=params(8),
        name="join",
    )(keep, lax.ppermute(send, "gy", SIBLING))


def solution(mesh):
    placed = (
        P("gx", "gy"),
        P("gy"),
        P("gy"),
        P("gy"),
        P("gy", "gx"),
        P("gx"),
        P("gy", None),
        P(),
        P("gy", "gx"),
        P("gy", None),
        P(("gx", "gy"), None, None),
        P(("gx", "gy"), None, None),
        P(("gx", "gy")),
        P(),
        P("gx", "gy"),
        P("gy"),
        P("gx", "gy"),
    )
    return jax.shard_map(
        on_device, mesh=mesh, in_specs=placed, out_specs=P("gx", "gy"), check_vma=False
    )
```

```python
import functools
import math

import jax
import jax.numpy as jnp
from jax import lax
from jax.experimental import pallas as pl
from jax.experimental.pallas import tpu as pltpu
from jax.sharding import PartitionSpec as P

D = 14848
HEAD = 64
KV = 8
GROUP = 28
OUTL = 4
NEW = 2
N_Y = 4
LOCAL_HEADS = 14
CHUNK = 512

epsilon = 1e-05
rope_base = 10000.0
BF = jnp.bfloat16
F32 = jnp.float32
MIB = 1024 * 1024
STEPS = (0, 1, 3, 2)
NT = (((1,), (1,)), ((), ()))


def lanes_of(columns):
    return [(n, slice(128 * n, min(128 * n + 128, columns))) for n in range((columns + 127) // 128)]


def put(ref, rows, values):
    for n, lanes in lanes_of(values.shape[1]):
        ref[n, rows, 0 : lanes.stop - lanes.start] = values[:, lanes]


def whole(shape):
    return pl.BlockSpec(shape, lambda *_: (0,) * len(shape))


def here():
    i = lax.axis_index("gx")
    j = lax.axis_index("gy")
    return lax.div(j, 2), lax.rem(j, 2), lax.div(i, 4), lax.rem(i, 4)


def prepare_kernel(positions, x, own, keep, send):
    rows, features = x.shape
    place = lax.broadcasted_iota(jnp.int32, (features, 128), 0)
    column = lax.broadcasted_iota(jnp.int32, (features, 128), 1)
    picked = (place == positions[0]) & (column == 0)
    for k in range(1, OUTL):
        picked = picked | ((place == positions[k]) & (column == k))
    picked = picked.astype(F32).astype(BF)
    outlier = jnp.dot(x[...], picked, preferred_element_type=F32)
    values = x[...].astype(F32)
    own[:, 0:features] = x[...]
    own[:, features:] = outlier[:, 0:64].astype(BF)
    half = rows // 2
    first = here()[1] == 0
    for out, flag in ((keep, first), (send, jnp.logical_not(first))):
        out[:, 0:features] = jnp.where(flag, values[0:half], values[half:]).astype(BF)
        out[:, features:] = jnp.where(flag, outlier[0:half, 0:64], outlier[half:, 0:64]).astype(BF)


def diagonal(size):
    return lax.broadcasted_iota(jnp.int32, (size, size), 0) == lax.broadcasted_iota(
        jnp.int32, (size, size), 1
    )


def sums_kernel(both, out):
    features = both.shape[2] - 64
    rows = both.shape[1]
    first = jnp.zeros((rows, 1), F32)
    second = jnp.zeros((rows, 1), F32)
    for part in range(2):
        values = both[part, :, 0:features].astype(F32)
        first = first + jnp.sum(values, axis=1, keepdims=True)
        second = second + jnp.sum(values * values, axis=1, keepdims=True)
    unit = diagonal(rows)
    first = jnp.sum(jnp.where(unit, first, 0.0), axis=0, keepdims=True)
    second = jnp.sum(jnp.where(unit, second, 0.0), axis=0, keepdims=True)
    for n in range(16):
        out[n, 0:1, :] = first
        out[n, 1:2, :] = second


def moments(sums):
    unit = diagonal(sums.shape[1])
    average = jnp.sum(jnp.where(unit, sums[0:1, :], 0.0), axis=1, keepdims=True) / D
    squares = jnp.sum(jnp.where(unit, sums[1:2, :], 0.0), axis=1, keepdims=True) / D
    return average, lax.rsqrt(squares - average * average + epsilon)


def normalize(rows, average, inverse, gain, bias, gain_out, bias_out, features):
    regular = ((rows[:, 0:features].astype(F32) - average) * inverse * gain + bias).astype(BF)
    outlier = (rows[:, features : features + OUTL].astype(F32) - average) * inverse * gain_out + bias_out
    return regular, outlier.astype(BF).astype(F32)


def pair_kernel(own, mine, other, gain, bias, gain_out, bias_out, scale, extra, weight, out):
    _, c, z, x = here()
    features = weight.shape[0]
    half = own.shape[0] // 2
    first = c == 0
    mine_at = mine[jnp.where(first, z, x)]
    other_at = other[jnp.where(first, x, z)]
    average0, inverse0 = moments(jnp.where(first, mine_at, other_at))
    average1, inverse1 = moments(jnp.where(first, other_at, mine_at))
    average = jnp.concatenate([average0[0:half], average1[0:half]], axis=0)
    inverse = jnp.concatenate([inverse0[0:half], inverse1[0:half]], axis=0)
    regular, outlier = normalize(
        own[...], average, inverse, gain[...], bias[...], gain_out[...], bias_out[...], features
    )
    term = jnp.dot(regular, weight[...], preferred_element_type=F32) * scale[...]
    for k in range(OUTL):
        term = term + outlier[:, k : k + 1] * extra[k : k + 1, :]
    for j in range(2 * N_Y):
        rows = slice(6 * j, 6 * j + 6)
        out[j, 0:6, :] = term[rows, 0:512]
        out[j, 6:12, :] = term[rows, 512:1024]
        out[j, 12:16, :] = jnp.zeros((4, 512), F32)


def query_kernel(
    a0, a1, a2, a3, b0, b1, b2, b3, mine, other, gain, bias, gain_out, bias_out,
    scale, extra, weight, pairs, keep, send, acc,
):
    y, c, z, x = here()
    features = weight.shape[0]
    for d2, (near, far) in enumerate(((a0, b0), (a1, b1), (a2, b2), (a3, b3))):
        regulars = []
        outliers = []
        for side, rows in enumerate((near[0], far[...])):
            sums = (mine, other)[side][lax.rem(jnp.where((c == 0) == (side == 0), z, x) + 4 - d2, 4)]
            average, inverse = moments(sums)
            regular, outlier = normalize(
                rows, average, inverse, gain[...], bias[...], gain_out[...], bias_out[...], features
            )
            regulars.append(regular)
            outliers.append(outlier)
        rows = jnp.concatenate(regulars, axis=0)
        value = jnp.concatenate(outliers, axis=0)
        term = jnp.dot(rows, weight[...], preferred_element_type=F32) * scale[...]
        for k in range(OUTL):
            term = term + value[:, k : k + 1] * extra[k : k + 1, :]
        for side in range(2):
            half = c if side == 0 else 1 - c
            for d1 in range(4):
                along_x = lax.rem(x + 4 - jnp.where(half == 0, STEPS[d1], d2), 4)
                along_z = lax.rem(z + 4 - jnp.where(half == 0, d2, STEPS[d1]), 4)
                at = pl.multiple_of((along_z * 4 + along_x) * 48 + half * 24, 8)
                row = side * 96 + d1 * 24
                put(acc, pl.ds(at, 24), term[row : row + 24, :])
    for out, core in ((keep, c), (send, 1 - c)):
        for d in range(N_Y):
            j = 2 * lax.rem(y + d, N_Y) + core
            for k in range(6):
                for n, lanes in lanes_of(896):
                    out[d, 16 * k : 16 * k + 16, lanes] = acc[n, pl.ds(6 * j + k, 16, stride=48), :].astype(BF)
            out[d, 96:112, 0:512] = pairs[j].astype(BF)
            out[d, 96:112, 512:896] = jnp.zeros((16, 384), BF)


def add_kernel(keep, received, o0, o1, o2, o3):
    for d, out in enumerate((o0, o1, o2, o3)):
        out[...] = (keep[d].astype(F32) + received[d].astype(F32)).astype(BF)


def collect_kernel(a, b, c, d, query_out, pair_out, acc):
    total = (a[...].astype(F32) + b[...].astype(F32)) + (c[...].astype(F32) + d[...].astype(F32))
    put(acc, slice(0, 112), total)
    for i in range(16):
        for n, lanes in lanes_of(896):
            query_out[i, :, lanes] = acc[n, pl.ds(i, 6, stride=16), :].astype(BF)
    pair_out[...] = total[96:112, 0:512]


def rotate_lanes(values, cosine, sine):
    lane = lax.broadcasted_iota(jnp.int32, values.shape, 1)
    partner = jnp.where(
        lane % 64 < 32, pltpu.roll(values, 96, axis=1), pltpu.roll(values, 32, axis=1)
    )
    return values * cosine + partner * sine


def attend_kernel(
    lengths, queries, pairs, cosine, sine, keys, values, out,
    staged, rotated, fresh_key, fresh_value, blocks, mixture, result, key_buf, value_buf, sems,
):
    requests = keys.shape[0]
    window = keys.shape[1]

    def fetch(r, n, which):
        source, target = ((keys, key_buf), (values, value_buf))[which]
        rows = pl.ds(pl.multiple_of(n * CHUNK, CHUNK), CHUNK)
        return pltpu.make_async_copy(source.at[r, rows], target.at[r, rows], sems.at[r, n, which])

    for r in range(requests):
        for n in range(window // CHUNK):

            @pl.when(lengths[r] > n * CHUNK)
            def _():
                fetch(r, n, 0).start()
                fetch(r, n, 1).start()

    for i in range(16):
        put(staged, slice(8 * i, 8 * i + 6), queries[i].astype(F32))
    for k in range(6):
        for col in range(7):
            lanes = slice(128 * col, 128 * col + 128)
            part = staged[col, pl.ds(k, 16, stride=8), :]
            turned = rotate_lanes(part, cosine[k : k + 1, :], sine[k : k + 1, :])
            rotated[16 * k : 16 * k + 16, lanes] = turned.astype(BF).astype(F32) * 0.125
    fresh_key[...] = jnp.zeros_like(fresh_key)
    fresh_value[...] = jnp.zeros_like(fresh_value)
    rounded = pairs[...].astype(BF).astype(F32)
    for col in range(4):
        lanes = slice(128 * col, 128 * col + 128)
        fresh_key[0:6, lanes] = rotate_lanes(rounded[0:6, lanes], cosine[0:6, :], sine[0:6, :])
    fresh_value[0:6, :] = rounded[6:12, :]

    sub = lax.broadcasted_iota(jnp.int32, (8, 256), 0)
    lane = lax.broadcasted_iota(jnp.int32, (8, 256), 1)
    own = sub // 2 == lane // 64
    low = lax.broadcasted_iota(jnp.int32, (8, 128), 1) < 64
    rows = LOCAL_HEADS * 16
    row = lax.broadcasted_iota(jnp.int32, (rows, 128), 0)
    column = lax.broadcasted_iota(jnp.int32, (rows, 128), 1)
    causal = column % 2 <= (row // 8) % 2
    place = lax.broadcasted_iota(jnp.int32, (rows, CHUNK), 1)

    starts = []
    for r in range(requests):
        state = []
        for g in range(2):
            for t in range(NEW):
                start = (NEW * r + t) * 16 + 8 * g
                for col in range(7):
                    part = rotated[start : start + 8, 128 * col : 128 * col + 128]
                    other = pltpu.roll(part, 64, axis=1)
                    for half in range(2):
                        both = jnp.where(low, part, other) if half == 0 else jnp.where(low, other, part)
                        both = jnp.concatenate([both, both], axis=1)
                        at = (2 * col + half) * 16 + t * 8
                        blocks[2 * r + g, at : at + 8, :] = jnp.where(own, both, 0.0)
            side = slice(256 * g, 256 * g + 256)
            query = blocks[2 * r + g].astype(BF)
            scores = lax.dot_general(query, fresh_key[:, side].astype(BF), NT, preferred_element_type=F32)
            scores = jnp.where(causal & (column // 2 == r), scores, -jnp.inf)
            top = jnp.max(scores, axis=1, keepdims=True)
            prob = jnp.exp(scores - top)
            total = jnp.sum(prob, axis=1, keepdims=True)
            mixture[2 * r + g] = jnp.dot(
                prob.astype(BF), fresh_value[:, side].astype(BF), preferred_element_type=F32
            )
            state.append((top, total))
        starts.append(tuple(state))

    for r in range(requests):
        length = lengths[r]

        def body(n, state):
            at = pl.multiple_of(n * CHUNK, CHUNK)
            active = place < length - at
            fetch(r, n, 0).wait()
            fetch(r, n, 1).wait()
            new = []
            for g in range(2):
                top, total = state[g]
                side = slice(256 * g, 256 * g + 256)
                key = key_buf[r, pl.ds(at, CHUNK), side]
                value = value_buf[r, pl.ds(at, CHUNK), side]
                query = blocks[2 * r + g].astype(BF)
                scores = lax.dot_general(query, key, NT, preferred_element_type=F32)
                scores = jnp.where(active, scores, -jnp.inf)
                higher = jnp.maximum(top, jnp.max(scores, axis=1, keepdims=True))
                shrink = jnp.exp(top - higher)
                prob = jnp.exp(scores - higher)
                total = total * shrink + jnp.sum(prob, axis=1, keepdims=True)
                mixture[2 * r + g] = mixture[2 * r + g] * shrink + jnp.dot(
                    prob.astype(BF), value, preferred_element_type=F32
                )
                new.append((higher, total))
            return tuple(new)

        state = lax.fori_loop(0, (length + CHUNK - 1) // CHUNK, body, starts[r])
        for g in range(2):
            blocks[2 * r + g] = mixture[2 * r + g] / state[g][1]
            for t in range(NEW):
                start = (NEW * r + t) * 16 + 8 * g
                for col in range(7):
                    folded = []
                    for half in range(2):
                        at = (2 * col + half) * 16 + t * 8
                        part = jnp.where(own, blocks[2 * r + g, at : at + 8, :], 0.0)
                        part = part[:, 0:128] + part[:, 128:256]
                        folded.append(part + pltpu.roll(part, 64, axis=1))
                    result[col, start : start + 8, :] = jnp.where(low, folded[0], folded[1])
    for i in range(16):
        for n, lanes in lanes_of(896):
            out[i, :, lanes] = result[n, pl.ds(i, 6, stride=16), :].astype(BF)


def repack_kernel(block, out, staged):
    for i in range(16):
        put(staged, slice(8 * i, 8 * i + 6), block[i].astype(F32))
    for k in range(6):
        for n, lanes in lanes_of(896):
            out[16 * k : 16 * k + 16, lanes] = staged[n, pl.ds(k, 16, stride=8), :].astype(BF)


def output_kernel(
    sending, b0, b1, b2, b3, s0, s1, s2, s3, chosen, plain, factors, weight, out, left, acc
):
    y, c, z, x = here()
    half = 1 - c if sending else c
    for blocks, core in (((b0, b1, b2, b3), c), ((s0, s1, s2, s3), 1 - c)):
        for d, block in enumerate(blocks):
            j = 2 * lax.rem(y + N_Y - d, N_Y) + core
            left[pl.ds(pl.multiple_of(96 * j, 96), 96), :] = block[...]
    step = 192
    for n in range(384 // step):
        part = left[pl.ds(pl.multiple_of(half * 384 + n * step, step), step), :]
        picked = jnp.dot(part, chosen[...], preferred_element_type=F32)
        term = lax.dot_general(part * plain[...], weight[...], NT, preferred_element_type=F32)
        term = term * factors[0:1, :]
        for k in range(OUTL):
            term = term + picked[:, k : k + 1] * factors[k + 1 : k + 2, :]
        put(acc, slice(n * step, n * step + step), term)
    for d in range(4):
        owners = []
        for f in range(4):
            along_x = lax.rem(x + jnp.where(half == 0, f, d), 4)
            along_z = lax.rem(z + jnp.where(half == 0, d, f), 4)
            owners.append(along_z * 4 + along_x)
        for n, lanes in lanes_of(out.shape[2]):
            got = [acc[n, pl.ds(i, 24, stride=16), :] for i in owners]
            got = jnp.concatenate(got, axis=0).astype(BF)
            out[d, :, lanes] = got[:, 0 : lanes.stop - lanes.start]


def first_sum_kernel(mine, other, r1, r3, r2, o0, o1, o2, o3):
    for part, start in enumerate((mine, other)):
        total = start[0].astype(F32) + r1[part].astype(F32)
        total = total + (r3[part].astype(F32) + r2[part].astype(F32))
        for f, out in enumerate((o0, o1, o2, o3)):
            out[part] = total[24 * f : 24 * f + 24, :].astype(BF)


def last_sum_kernel(own, r1, r3, r2, keep, send):
    for part, out in enumerate((keep, send)):
        total = own[part].astype(F32) + r1[part].astype(F32)
        out[...] = (total + (r3[part].astype(F32) + r2[part].astype(F32))).astype(BF)


def join_kernel(mine, other, out):
    first = here()[1] == 0
    a = mine[...].astype(F32)
    b = other[...].astype(F32)
    joined = jnp.concatenate([jnp.where(first, a, b), jnp.where(first, b, a)], axis=0)
    out[...] = joined.astype(BF)


def params(mib=48):
    return pltpu.CompilerParams(vmem_limit_bytes=mib * MIB)


def over_y(shift):
    return [(2 * y + c, 2 * ((y + shift) % N_Y) + c) for y in range(N_Y) for c in range(2)]


def shift_plane(first, shift):
    pairs = []
    for z in range(4):
        for x in range(4):
            for j in range(2 * N_Y):
                if (j % 2 == 0) == first:
                    to = z * 4 + (x + shift) % 4
                else:
                    to = (z + shift) % 4 * 4 + x
                pairs.append(((z * 4 + x) * 2 * N_Y + j, to * 2 * N_Y + j))
    return pairs


def sheets():
    groups = []
    for first in (True, False):
        for fixed in range(4):
            group = []
            for moving in range(4):
                z, x = (moving, fixed) if first else (fixed, moving)
                for y in range(N_Y):
                    group.append((z * 4 + x) * 2 * N_Y + 2 * y + (0 if first else 1))
            groups.append(group)
    return groups


SIBLING = [(j, j ^ 1) for j in range(2 * N_Y)]


def on_device(
    activations,
    norm_gain,
    norm_bias,
    input_outliers,
    query_int,
    query_scale,
    keyvalue_int,
    keyvalue_scale,
    query_float,
    keyvalue_float,
    key_cache,
    value_cache,
    lengths,
    middle_outliers,
    output_int,
    output_scale,
    output_float,
):
    block_rows, features = activations.shape
    tokens = block_rows * 16
    columns = query_int.shape[1]
    out_columns = output_int.shape[1]
    me_x = lax.axis_index("gx")
    smem = pl.BlockSpec(memory_space=pltpu.SMEM)
    vmem = pl.BlockSpec(memory_space=pltpu.VMEM)

    picked = jnp.arange(features, dtype=jnp.int32)[:, None] == input_outliers[None, :]
    is_outlier = jnp.any(picked, axis=1)
    gain = jnp.where(is_outlier, 0.0, norm_gain)[None]
    bias = jnp.where(is_outlier, 0.0, norm_bias)[None]
    gain_out = jnp.sum(jnp.where(picked, norm_gain[:, None], 0.0), axis=0)[None]
    bias_out = jnp.sum(jnp.where(picked, norm_bias[:, None], 0.0), axis=0)[None]
    padded = features + 64
    own, kept, sent = pl.pallas_call(
        prepare_kernel,
        in_specs=[smem, vmem],
        out_specs=[vmem] * 3,
        out_shape=[
            jax.ShapeDtypeStruct((block_rows, padded), BF),
            jax.ShapeDtypeStruct((block_rows // 2, padded), BF),
            jax.ShapeDtypeStruct((block_rows // 2, padded), BF),
        ],
        compiler_params=params(8),
        name="prepare",
    )(input_outliers, activations)
    plane = ("gx", "gy")
    both = jnp.stack([kept, lax.ppermute(sent, "gy", SIBLING)])
    both = jnp.concatenate(
        [both] + [lax.ppermute(both, plane, shift_plane(True, d)) for d in (1, 3, 2)], axis=1
    )
    arrived = [both] + [lax.ppermute(both, plane, shift_plane(False, d)) for d in (1, 3, 2)]
    sums = pl.pallas_call(
        sums_kernel,
        out_shape=jax.ShapeDtypeStruct((16, 2, 96), F32),
        compiler_params=params(8),
        name="row_sums",
    )(both)
    sums = lax.all_to_all(
        sums, plane, split_axis=0, concat_axis=0, tiled=True, axis_index_groups=sheets()
    )
    mine = jnp.sum(sums.reshape(4, N_Y, 2, 96), axis=1)
    other = lax.ppermute(mine, "gy", SIBLING)
    *arrived, mine, other = lax.optimization_barrier((*arrived, mine, other))
    pairs = pl.pallas_call(
        pair_kernel,
        in_specs=[vmem] * 10,
        out_specs=vmem,
        out_shape=jax.ShapeDtypeStruct((2 * N_Y, 16, 512), F32),
        compiler_params=params(16),
        name="pair_projection",
    )(
        own, mine, other, gain, bias, gain_out, bias_out,
        keyvalue_scale[None], keyvalue_float, keyvalue_int,
    )
    others = [lax.ppermute(block[1], "gy", SIBLING) for block in arrived]
    order = (0, 1, 3, 2)
    arrived = [arrived[n] for n in order]
    others = [others[n] for n in order]

    keep, send = pl.pallas_call(
        query_kernel,
        grid=(1,),
        in_specs=[whole((1, 96, padded))] * 4 + [vmem] * 14,
        out_specs=[vmem] * 2,
        out_shape=[jax.ShapeDtypeStruct((N_Y, 112, columns), BF)] * 2,
        scratch_shapes=[pltpu.VMEM((7, tokens, 128), F32)],
        compiler_params=params(24),
        name="query_projection",
    )(
        *arrived, *others, mine, other, gain, bias, gain_out, bias_out,
        query_scale[None], query_float, query_int, pairs,
    )
    received = lax.ppermute(send, "gy", SIBLING)
    piece = jax.ShapeDtypeStruct((112, columns), BF)
    mine, to1, to2, to3 = pl.pallas_call(
        add_kernel, out_shape=[piece] * 4, compiler_params=params(8), name="add_cores"
    )(keep, received)
    from1 = lax.ppermute(to1, "gy", over_y(1))
    from3 = lax.ppermute(to3, "gy", over_y(3))
    from2 = lax.ppermute(to2, "gy", over_y(2))
    summed, pair_sums = pl.pallas_call(
        collect_kernel,
        out_shape=[
            jax.ShapeDtypeStruct((16, 6, columns), BF),
            jax.ShapeDtypeStruct((16, 512), F32),
        ],
        scratch_shapes=[pltpu.VMEM((7, 112, 128), F32)],
        compiler_params=params(8),
        name="collect",
    )(mine, from1, from2, from3)
    middle = lax.dynamic_slice(middle_outliers, (me_x * OUTL,), (OUTL,))
    chosen = jnp.arange(columns, dtype=jnp.int32)[:, None] == middle[None, :]
    plain = jnp.where(jnp.any(chosen, axis=1), 0.0, 1.0).astype(BF)[None]
    chosen = jnp.pad(chosen.astype(BF), ((0, 0), (0, 128 - OUTL)))
    factors = jnp.concatenate([output_scale[None], output_float])
    summed, chosen, plain, factors = lax.optimization_barrier((summed, chosen, plain, factors))
    queries = lax.all_to_all(summed, "gx", split_axis=0, concat_axis=0, tiled=True)

    positions = (lengths[:, None] + jnp.arange(NEW, dtype=jnp.int32)[None, :]).reshape(6, 1)
    frequency = jnp.exp(jnp.arange(32, dtype=F32) * (-2.0 * math.log(rope_base) / HEAD))
    angles = positions.astype(F32) * frequency[None, :]
    cosine = jnp.tile(jnp.cos(angles), (1, 4))
    sine = jnp.sin(angles)
    sine = jnp.concatenate([-sine, sine, -sine, sine], axis=1)
    cosine = jnp.pad(cosine, ((0, 2), (0, 0)))
    sine = jnp.pad(sine, ((0, 2), (0, 0)))

    requests, window, cached = key_cache.shape
    hbm = pl.BlockSpec(memory_space=pltpu.HBM)
    attended = pl.pallas_call(
        attend_kernel,
        in_specs=[smem, vmem, vmem, vmem, vmem, hbm, hbm],
        out_specs=vmem,
        out_shape=jax.ShapeDtypeStruct((16, 6, columns), BF),
        scratch_shapes=[
            pltpu.VMEM((7, 128, 128), F32),
            pltpu.VMEM((96, columns), F32),
            pltpu.VMEM((128, cached), F32),
            pltpu.VMEM((128, cached), F32),
            pltpu.VMEM((6, 224, 256), F32),
            pltpu.VMEM((6, 224, 256), F32),
            pltpu.VMEM((7, 96, 128), F32),
            pltpu.VMEM((requests, window, cached), BF),
            pltpu.VMEM((requests, window, cached), BF),
            pltpu.SemaphoreType.DMA((requests, window // CHUNK, 2)),
        ],
        compiler_params=params(55),
        name="attention",
    )(lengths, queries, pair_sums, cosine, sine, key_cache, value_cache)

    back = lax.all_to_all(attended, "gx", split_axis=0, concat_axis=0, tiled=True)
    mine = pl.pallas_call(
        repack_kernel,
        out_shape=jax.ShapeDtypeStruct((96, columns), BF),
        scratch_shapes=[pltpu.VMEM((7, 128, 128), F32)],
        compiler_params=params(8),
        name="repack",
    )(back)
    blocks = [mine] + [lax.ppermute(mine, "gy", over_y(d)) for d in (1, 2, 3)]
    blocks = blocks + [lax.ppermute(b, "gy", SIBLING) for b in blocks]

    half_rows = block_rows // 2

    def project(sending):
        return pl.pallas_call(
            functools.partial(output_kernel, sending),
            in_specs=[vmem] * 12,
            out_specs=vmem,
            out_shape=jax.ShapeDtypeStruct((4, 4 * half_rows, out_columns), BF),
            scratch_shapes=[
                pltpu.VMEM((tokens, columns), BF),
                pltpu.VMEM((15, tokens // 2, 128), F32),
            ],
            compiler_params=params(24),
            name="output_sent" if sending else "output_kept",
        )(*blocks, chosen, plain, factors, output_int.T)

    other = lax.ppermute(project(True), "gy", SIBLING)
    kept = project(False)
    steps = (1, 3, 2)
    got = [
        lax.ppermute(jnp.stack([kept[d], other[d]]), plane, shift_plane(False, d)) for d in steps
    ]
    quarter = jax.ShapeDtypeStruct((2, half_rows, out_columns), BF)
    sums = pl.pallas_call(
        first_sum_kernel,
        grid=(1,),
        in_specs=[whole((1, 4 * half_rows, out_columns))] * 2 + [vmem] * 3,
        out_specs=[vmem] * 4,
        out_shape=[quarter] * 4,
        compiler_params=params(16),
        name="first_sum",
    )(kept, other, *got)
    got = [lax.ppermute(sums[f], plane, shift_plane(True, f)) for f in steps]
    half = jax.ShapeDtypeStruct((half_rows, out_columns), BF)
    keep, send = pl.pallas_call(
        last_sum_kernel, out_shape=[half] * 2, compiler_params=params(8), name="last_sum"
    )(sums[0], *got)
    return pl.pallas_call(
        join_kernel,
        out_shape=jax.ShapeDtypeStruct((block_rows, out_columns), BF),
        compiler_params=params(8),
        name="join",
    )(keep, lax.ppermute(send, "gy", SIBLING))


def solution(mesh):
    placed = (
        P("gx", "gy"),
        P("gy"),
        P("gy"),
        P("gy"),
        P("gy", "gx"),
        P("gx"),
        P("gy", None),
        P(),
        P("gy", "gx"),
        P("gy", None),
        P(("gx", "gy"), None, None),
        P(("gx", "gy"), None, None),
        P(("gx", "gy")),
        P(),
        P("gx", "gy"),
        P("gy"),
        P("gx", "gy"),
    )
    return jax.shard_map(
        on_device, mesh=mesh, in_specs=placed, out_specs=P("gx", "gy"), check_vma=False
    )
```

```python
import functools
import math

import jax
import jax.numpy as jnp
from jax import lax
from jax.experimental import pallas as pl
from jax.experimental.pallas import tpu as pltpu
from jax.sharding import PartitionSpec as P

D = 14848
HEAD = 64
KV = 8
GROUP = 28
OUTL = 4
NEW = 2
N_Y = 4
LOCAL_HEADS = 14
CHUNK = 512

epsilon = 1e-05
rope_base = 10000.0
BF = jnp.bfloat16
F32 = jnp.float32
MIB = 1024 * 1024
STEPS = (0, 1, 3, 2)
NT = (((1,), (1,)), ((), ()))


def lanes_of(columns):
    return [(n, slice(128 * n, min(128 * n + 128, columns))) for n in range((columns + 127) // 128)]


def put(ref, rows, values):
    for n, lanes in lanes_of(values.shape[1]):
        ref[n, rows, 0 : lanes.stop - lanes.start] = values[:, lanes]


def whole(shape):
    return pl.BlockSpec(shape, lambda *_: (0,) * len(shape))


def here():
    i = lax.axis_index("gx")
    j = lax.axis_index("gy")
    return lax.div(j, 2), lax.rem(j, 2), lax.div(i, 4), lax.rem(i, 4)


def prepare_kernel(positions, x, own, keep, send):
    rows, features = x.shape
    place = lax.broadcasted_iota(jnp.int32, (features, 128), 0)
    column = lax.broadcasted_iota(jnp.int32, (features, 128), 1)
    picked = (place == positions[0]) & (column == 0)
    for k in range(1, OUTL):
        picked = picked | ((place == positions[k]) & (column == k))
    picked = picked.astype(F32).astype(BF)
    outlier = jnp.dot(x[...], picked, preferred_element_type=F32)
    values = x[...].astype(F32)
    own[:, 0:features] = x[...]
    own[:, features:] = outlier[:, 0:64].astype(BF)
    half = rows // 2
    first = here()[1] == 0
    for out, flag in ((keep, first), (send, jnp.logical_not(first))):
        out[:, 0:features] = jnp.where(flag, values[0:half], values[half:]).astype(BF)
        out[:, features:] = jnp.where(flag, outlier[0:half, 0:64], outlier[half:, 0:64]).astype(BF)


def diagonal(size):
    return lax.broadcasted_iota(jnp.int32, (size, size), 0) == lax.broadcasted_iota(
        jnp.int32, (size, size), 1
    )


def sums_kernel(both, out):
    features = both.shape[2] - 64
    rows = both.shape[1]
    first = jnp.zeros((rows, 1), F32)
    second = jnp.zeros((rows, 1), F32)
    for part in range(2):
        values = both[part, :, 0:features].astype(F32)
        first = first + jnp.sum(values, axis=1, keepdims=True)
        second = second + jnp.sum(values * values, axis=1, keepdims=True)
    unit = diagonal(rows)
    first = jnp.sum(jnp.where(unit, first, 0.0), axis=0, keepdims=True)
    second = jnp.sum(jnp.where(unit, second, 0.0), axis=0, keepdims=True)
    for n in range(16):
        out[n, 0:1, :] = first
        out[n, 1:2, :] = second


def moments(sums):
    unit = diagonal(sums.shape[1])
    average = jnp.sum(jnp.where(unit, sums[0:1, :], 0.0), axis=1, keepdims=True) / D
    squares = jnp.sum(jnp.where(unit, sums[1:2, :], 0.0), axis=1, keepdims=True) / D
    return average, lax.rsqrt(squares - average * average + epsilon)


def normalize(rows, average, inverse, gain, bias, gain_out, bias_out, features):
    regular = ((rows[:, 0:features].astype(F32) - average) * inverse * gain + bias).astype(BF)
    outlier = (rows[:, features : features + OUTL].astype(F32) - average) * inverse * gain_out + bias_out
    return regular, outlier.astype(BF).astype(F32)


def pair_kernel(own, mine, other, gain, bias, gain_out, bias_out, scale, extra, weight, out):
    _, c, z, x = here()
    features = weight.shape[0]
    half = own.shape[0] // 2
    first = c == 0
    mine_at = mine[jnp.where(first, z, x)]
    other_at = other[jnp.where(first, x, z)]
    average0, inverse0 = moments(jnp.where(first, mine_at, other_at))
    average1, inverse1 = moments(jnp.where(first, other_at, mine_at))
    average = jnp.concatenate([average0[0:half], average1[0:half]], axis=0)
    inverse = jnp.concatenate([inverse0[0:half], inverse1[0:half]], axis=0)
    regular, outlier = normalize(
        own[...], average, inverse, gain[...], bias[...], gain_out[...], bias_out[...], features
    )
    term = jnp.dot(regular, weight[...], preferred_element_type=F32) * scale[...]
    for k in range(OUTL):
        term = term + outlier[:, k : k + 1] * extra[k : k + 1, :]
    for j in range(2 * N_Y):
        rows = slice(6 * j, 6 * j + 6)
        out[j, 0:6, :] = term[rows, 0:512]
        out[j, 6:12, :] = term[rows, 512:1024]
        out[j, 12:16, :] = jnp.zeros((4, 512), F32)


def query_kernel(
    a0, a1, a2, a3, b0, b1, b2, b3, mine, other, gain, bias, gain_out, bias_out,
    scale, extra, weight, pairs, keep, send, acc,
):
    y, c, z, x = here()
    features = weight.shape[0]
    for d2, (near, far) in enumerate(((a0, b0), (a1, b1), (a2, b2), (a3, b3))):
        regulars = []
        outliers = []
        for side, rows in enumerate((near[0], far[...])):
            sums = (mine, other)[side][lax.rem(jnp.where((c == 0) == (side == 0), z, x) + 4 - d2, 4)]
            average, inverse = moments(sums)
            regular, outlier = normalize(
                rows, average, inverse, gain[...], bias[...], gain_out[...], bias_out[...], features
            )
            regulars.append(regular)
            outliers.append(outlier)
        rows = jnp.concatenate(regulars, axis=0)
        value = jnp.concatenate(outliers, axis=0)
        term = jnp.dot(rows, weight[...], preferred_element_type=F32) * scale[...]
        for k in range(OUTL):
            term = term + value[:, k : k + 1] * extra[k : k + 1, :]
        for side in range(2):
            half = c if side == 0 else 1 - c
            for d1 in range(4):
                along_x = lax.rem(x + 4 - jnp.where(half == 0, STEPS[d1], d2), 4)
                along_z = lax.rem(z + 4 - jnp.where(half == 0, d2, STEPS[d1]), 4)
                at = pl.multiple_of((along_z * 4 + along_x) * 48 + half * 24, 8)
                row = side * 96 + d1 * 24
                put(acc, pl.ds(at, 24), term[row : row + 24, :])
    for out, core in ((keep, c), (send, 1 - c)):
        for d in range(N_Y):
            j = 2 * lax.rem(y + d, N_Y) + core
            for k in range(6):
                for n, lanes in lanes_of(896):
                    out[d, 16 * k : 16 * k + 16, lanes] = acc[n, pl.ds(6 * j + k, 16, stride=48), :].astype(BF)
            out[d, 96:112, 0:512] = pairs[j].astype(BF)
            out[d, 96:112, 512:896] = jnp.zeros((16, 384), BF)


def add_kernel(keep, received, o0, o1, o2, o3):
    for d, out in enumerate((o0, o1, o2, o3)):
        out[...] = (keep[d].astype(F32) + received[d].astype(F32)).astype(BF)


def collect_kernel(a, b, c, d, query_out, pair_out, acc):
    total = (a[...].astype(F32) + b[...].astype(F32)) + (c[...].astype(F32) + d[...].astype(F32))
    put(acc, slice(0, 112), total)
    for i in range(16):
        for n, lanes in lanes_of(896):
            query_out[i, :, lanes] = acc[n, pl.ds(i, 6, stride=16), :].astype(BF)
    pair_out[...] = total[96:112, 0:512]


def rotate_lanes(values, cosine, sine):
    lane = lax.broadcasted_iota(jnp.int32, values.shape, 1)
    partner = jnp.where(
        lane % 64 < 32, pltpu.roll(values, 96, axis=1), pltpu.roll(values, 32, axis=1)
    )
    return values * cosine + partner * sine


def attend_kernel(
    lengths, queries, pairs, cosine, sine, keys, values, out,
    staged, rotated, fresh_key, fresh_value, blocks, mixture, result, key_buf, value_buf, sems,
):
    requests = keys.shape[0]
    window = keys.shape[1]

    def fetch(r, n, which):
        source, target = ((keys, key_buf), (values, value_buf))[which]
        rows = pl.ds(pl.multiple_of(n * CHUNK, CHUNK), CHUNK)
        return pltpu.make_async_copy(source.at[r, rows], target.at[r, rows], sems.at[r, n, which])

    for r in range(requests):
        for n in range(window // CHUNK):

            @pl.when(lengths[r] > n * CHUNK)
            def _():
                fetch(r, n, 0).start()
                fetch(r, n, 1).start()

    for i in range(16):
        put(staged, slice(8 * i, 8 * i + 6), queries[i].astype(F32))
    for k in range(6):
        for col in range(7):
            lanes = slice(128 * col, 128 * col + 128)
            part = staged[col, pl.ds(k, 16, stride=8), :]
            turned = rotate_lanes(part, cosine[k : k + 1, :], sine[k : k + 1, :])
            rotated[16 * k : 16 * k + 16, lanes] = turned.astype(BF).astype(F32) * 0.125
    fresh_key[...] = jnp.zeros_like(fresh_key)
    fresh_value[...] = jnp.zeros_like(fresh_value)
    rounded = pairs[...].astype(BF).astype(F32)
    for col in range(4):
        lanes = slice(128 * col, 128 * col + 128)
        fresh_key[0:6, lanes] = rotate_lanes(rounded[0:6, lanes], cosine[0:6, :], sine[0:6, :])
    fresh_value[0:6, :] = rounded[6:12, :]

    sub = lax.broadcasted_iota(jnp.int32, (8, 256), 0)
    lane = lax.broadcasted_iota(jnp.int32, (8, 256), 1)
    own = sub // 2 == lane // 64
    low = lax.broadcasted_iota(jnp.int32, (8, 128), 1) < 64
    rows = LOCAL_HEADS * 16
    row = lax.broadcasted_iota(jnp.int32, (rows, 128), 0)
    column = lax.broadcasted_iota(jnp.int32, (rows, 128), 1)
    causal = column % 2 <= (row // 8) % 2
    place = lax.broadcasted_iota(jnp.int32, (rows, CHUNK), 1)

    starts = []
    for r in range(requests):
        state = []
        for g in range(2):
            for t in range(NEW):
                start = (NEW * r + t) * 16 + 8 * g
                for col in range(7):
                    part = rotated[start : start + 8, 128 * col : 128 * col + 128]
                    other = pltpu.roll(part, 64, axis=1)
                    for half in range(2):
                        both = jnp.where(low, part, other) if half == 0 else jnp.where(low, other, part)
                        both = jnp.concatenate([both, both], axis=1)
                        at = (2 * col + half) * 16 + t * 8
                        blocks[2 * r + g, at : at + 8, :] = jnp.where(own, both, 0.0)
            side = slice(256 * g, 256 * g + 256)
            query = blocks[2 * r + g].astype(BF)
            scores = lax.dot_general(query, fresh_key[:, side].astype(BF), NT, preferred_element_type=F32)
            scores = jnp.where(causal & (column // 2 == r), scores, -jnp.inf)
            top = jnp.max(scores, axis=1, keepdims=True)
            prob = jnp.exp(scores - top)
            total = jnp.sum(prob, axis=1, keepdims=True)
            mixture[2 * r + g] = jnp.dot(
                prob.astype(BF), fresh_value[:, side].astype(BF), preferred_element_type=F32
            )
            state.append((top, total))
        starts.append(tuple(state))

    for r in range(requests):
        length = lengths[r]

        def body(n, state):
            at = pl.multiple_of(n * CHUNK, CHUNK)
            active = place < length - at
            fetch(r, n, 0).wait()
            fetch(r, n, 1).wait()
            new = []
            for g in range(2):
                top, total = state[g]
                side = slice(256 * g, 256 * g + 256)
                key = key_buf[r, pl.ds(at, CHUNK), side]
                value = value_buf[r, pl.ds(at, CHUNK), side]
                query = blocks[2 * r + g].astype(BF)
                scores = lax.dot_general(query, key, NT, preferred_element_type=F32)
                scores = jnp.where(active, scores, -jnp.inf)
                higher = jnp.maximum(top, jnp.max(scores, axis=1, keepdims=True))
                shrink = jnp.exp(top - higher)
                prob = jnp.exp(scores - higher)
                total = total * shrink + jnp.sum(prob, axis=1, keepdims=True)
                mixture[2 * r + g] = mixture[2 * r + g] * shrink + jnp.dot(
                    prob.astype(BF), value, preferred_element_type=F32
                )
                new.append((higher, total))
            return tuple(new)

        state = lax.fori_loop(0, (length + CHUNK - 1) // CHUNK, body, starts[r])
        for g in range(2):
            blocks[2 * r + g] = mixture[2 * r + g] / state[g][1]
            for t in range(NEW):
                start = (NEW * r + t) * 16 + 8 * g
                for col in range(7):
                    folded = []
                    for half in range(2):
                        at = (2 * col + half) * 16 + t * 8
                        part = jnp.where(own, blocks[2 * r + g, at : at + 8, :], 0.0)
                        part = part[:, 0:128] + part[:, 128:256]
                        folded.append(part + pltpu.roll(part, 64, axis=1))
                    result[col, start : start + 8, :] = jnp.where(low, folded[0], folded[1])
    for i in range(16):
        for n, lanes in lanes_of(896):
            out[i, :, lanes] = result[n, pl.ds(i, 6, stride=16), :].astype(BF)


def repack_kernel(block, out, staged):
    for i in range(16):
        put(staged, slice(8 * i, 8 * i + 6), block[i].astype(F32))
    for k in range(6):
        for n, lanes in lanes_of(896):
            out[16 * k : 16 * k + 16, lanes] = staged[n, pl.ds(k, 16, stride=8), :].astype(BF)


def output_kernel(
    sending, b0, b1, b2, b3, s0, s1, s2, s3, chosen, plain, factors, weight, out, left, acc
):
    y, c, z, x = here()
    half = 1 - c if sending else c
    for blocks, core in (((b0, b1, b2, b3), c), ((s0, s1, s2, s3), 1 - c)):
        for d, block in enumerate(blocks):
            j = 2 * lax.rem(y + N_Y - d, N_Y) + core
            left[pl.ds(pl.multiple_of(96 * j, 96), 96), :] = block[...]
    step = 192
    for n in range(384 // step):
        part = left[pl.ds(pl.multiple_of(half * 384 + n * step, step), step), :]
        picked = jnp.dot(part, chosen[...], preferred_element_type=F32)
        term = lax.dot_general(part * plain[...], weight[...], NT, preferred_element_type=F32)
        term = term * factors[0:1, :]
        for k in range(OUTL):
            term = term + picked[:, k : k + 1] * factors[k + 1 : k + 2, :]
        put(acc, slice(n * step, n * step + step), term)
    for d in range(4):
        owners = []
        for f in range(4):
            along_x = lax.rem(x + jnp.where(half == 0, f, d), 4)
            along_z = lax.rem(z + jnp.where(half == 0, d, f), 4)
            owners.append(along_z * 4 + along_x)
        for n, lanes in lanes_of(out.shape[2]):
            got = [acc[n, pl.ds(i, 24, stride=16), :] for i in owners]
            got = jnp.concatenate(got, axis=0).astype(BF)
            out[d, :, lanes] = got[:, 0 : lanes.stop - lanes.start]


def first_sum_kernel(mine, other, r1, r3, r2, o0, o1, o2, o3):
    for part, start in enumerate((mine, other)):
        total = start[0].astype(F32) + r1[part].astype(F32)
        total = total + (r3[part].astype(F32) + r2[part].astype(F32))
        for f, out in enumerate((o0, o1, o2, o3)):
            out[part] = total[24 * f : 24 * f + 24, :].astype(BF)


def last_sum_kernel(own, r1, r3, r2, keep, send):
    for part, out in enumerate((keep, send)):
        total = own[part].astype(F32) + r1[part].astype(F32)
        out[...] = (total + (r3[part].astype(F32) + r2[part].astype(F32))).astype(BF)


def join_kernel(mine, other, out):
    first = here()[1] == 0
    a = mine[...].astype(F32)
    b = other[...].astype(F32)
    joined = jnp.concatenate([jnp.where(first, a, b), jnp.where(first, b, a)], axis=0)
    out[...] = joined.astype(BF)


def params(mib=48):
    return pltpu.CompilerParams(vmem_limit_bytes=mib * MIB)


def over_y(shift):
    return [(2 * y + c, 2 * ((y + shift) % N_Y) + c) for y in range(N_Y) for c in range(2)]


def shift_plane(first, shift):
    pairs = []
    for z in range(4):
        for x in range(4):
            for j in range(2 * N_Y):
                if (j % 2 == 0) == first:
                    to = z * 4 + (x + shift) % 4
                else:
                    to = (z + shift) % 4 * 4 + x
                pairs.append(((z * 4 + x) * 2 * N_Y + j, to * 2 * N_Y + j))
    return pairs


def sheets():
    groups = []
    for first in (True, False):
        for fixed in range(4):
            group = []
            for moving in range(4):
                z, x = (moving, fixed) if first else (fixed, moving)
                for y in range(N_Y):
                    group.append((z * 4 + x) * 2 * N_Y + 2 * y + (0 if first else 1))
            groups.append(group)
    return groups


SIBLING = [(j, j ^ 1) for j in range(2 * N_Y)]


def on_device(
    activations,
    norm_gain,
    norm_bias,
    input_outliers,
    query_int,
    query_scale,
    keyvalue_int,
    keyvalue_scale,
    query_float,
    keyvalue_float,
    key_cache,
    value_cache,
    lengths,
    middle_outliers,
    output_int,
    output_scale,
    output_float,
):
    block_rows, features = activations.shape
    tokens = block_rows * 16
    columns = query_int.shape[1]
    out_columns = output_int.shape[1]
    me_x = lax.axis_index("gx")
    smem = pl.BlockSpec(memory_space=pltpu.SMEM)
    vmem = pl.BlockSpec(memory_space=pltpu.VMEM)

    picked = jnp.arange(features, dtype=jnp.int32)[:, None] == input_outliers[None, :]
    is_outlier = jnp.any(picked, axis=1)
    gain = jnp.where(is_outlier, 0.0, norm_gain)[None]
    bias = jnp.where(is_outlier, 0.0, norm_bias)[None]
    gain_out = jnp.sum(jnp.where(picked, norm_gain[:, None], 0.0), axis=0)[None]
    bias_out = jnp.sum(jnp.where(picked, norm_bias[:, None], 0.0), axis=0)[None]
    padded = features + 64
    own, kept, sent = pl.pallas_call(
        prepare_kernel,
        in_specs=[smem, vmem],
        out_specs=[vmem] * 3,
        out_shape=[
            jax.ShapeDtypeStruct((block_rows, padded), BF),
            jax.ShapeDtypeStruct((block_rows // 2, padded), BF),
            jax.ShapeDtypeStruct((block_rows // 2, padded), BF),
        ],
        compiler_params=params(8),
        name="prepare",
    )(input_outliers, activations)
    plane = ("gx", "gy")
    both = jnp.stack([kept, lax.ppermute(sent, "gy", SIBLING)])
    both = jnp.concatenate(
        [both] + [lax.ppermute(both, plane, shift_plane(True, d)) for d in (1, 3, 2)], axis=1
    )
    arrived = [both] + [lax.ppermute(both, plane, shift_plane(False, d)) for d in (1, 3, 2)]
    sums = pl.pallas_call(
        sums_kernel,
        out_shape=jax.ShapeDtypeStruct((16, 2, 96), F32),
        compiler_params=params(8),
        name="row_sums",
    )(both)
    sums = lax.all_to_all(
        sums, plane, split_axis=0, concat_axis=0, tiled=True, axis_index_groups=sheets()
    )
    mine = jnp.sum(sums.reshape(4, N_Y, 2, 96), axis=1)
    other = lax.ppermute(mine, "gy", SIBLING)
    *arrived, mine, other = lax.optimization_barrier((*arrived, mine, other))
    pairs = pl.pallas_call(
        pair_kernel,
        in_specs=[vmem] * 10,
        out_specs=vmem,
        out_shape=jax.ShapeDtypeStruct((2 * N_Y, 16, 512), F32),
        compiler_params=params(16),
        name="pair_projection",
    )(
        own, mine, other, gain, bias, gain_out, bias_out,
        keyvalue_scale[None], keyvalue_float, keyvalue_int,
    )
    others = [lax.ppermute(block[1], "gy", SIBLING) for block in arrived]
    order = (0, 1, 3, 2)
    arrived = [arrived[n] for n in order]
    others = [others[n] for n in order]

    keep, send = pl.pallas_call(
        query_kernel,
        grid=(1,),
        in_specs=[whole((1, 96, padded))] * 4 + [vmem] * 14,
        out_specs=[vmem] * 2,
        out_shape=[jax.ShapeDtypeStruct((N_Y, 112, columns), BF)] * 2,
        scratch_shapes=[pltpu.VMEM((7, tokens, 128), F32)],
        compiler_params=params(24),
        name="query_projection",
    )(
        *arrived, *others, mine, other, gain, bias, gain_out, bias_out,
        query_scale[None], query_float, query_int, pairs,
    )
    received = lax.ppermute(send, "gy", SIBLING)
    piece = jax.ShapeDtypeStruct((112, columns), BF)
    mine, to1, to2, to3 = pl.pallas_call(
        add_kernel, out_shape=[piece] * 4, compiler_params=params(8), name="add_cores"
    )(keep, received)
    from1 = lax.ppermute(to1, "gy", over_y(1))
    from3 = lax.ppermute(to3, "gy", over_y(3))
    from2 = lax.ppermute(to2, "gy", over_y(2))
    summed, pair_sums = pl.pallas_call(
        collect_kernel,
        out_shape=[
            jax.ShapeDtypeStruct((16, 6, columns), BF),
            jax.ShapeDtypeStruct((16, 512), F32),
        ],
        scratch_shapes=[pltpu.VMEM((7, 112, 128), F32)],
        compiler_params=params(8),
        name="collect",
    )(mine, from1, from2, from3)
    queries = lax.all_to_all(summed, "gx", split_axis=0, concat_axis=0, tiled=True)

    positions = (lengths[:, None] + jnp.arange(NEW, dtype=jnp.int32)[None, :]).reshape(6, 1)
    frequency = jnp.exp(jnp.arange(32, dtype=F32) * (-2.0 * math.log(rope_base) / HEAD))
    angles = positions.astype(F32) * frequency[None, :]
    cosine = jnp.tile(jnp.cos(angles), (1, 4))
    sine = jnp.sin(angles)
    sine = jnp.concatenate([-sine, sine, -sine, sine], axis=1)
    cosine = jnp.pad(cosine, ((0, 2), (0, 0)))
    sine = jnp.pad(sine, ((0, 2), (0, 0)))

    requests, window, cached = key_cache.shape
    hbm = pl.BlockSpec(memory_space=pltpu.HBM)
    attended = pl.pallas_call(
        attend_kernel,
        in_specs=[smem, vmem, vmem, vmem, vmem, hbm, hbm],
        out_specs=vmem,
        out_shape=jax.ShapeDtypeStruct((16, 6, columns), BF),
        scratch_shapes=[
            pltpu.VMEM((7, 128, 128), F32),
            pltpu.VMEM((96, columns), F32),
            pltpu.VMEM((128, cached), F32),
            pltpu.VMEM((128, cached), F32),
            pltpu.VMEM((6, 224, 256), F32),
            pltpu.VMEM((6, 224, 256), F32),
            pltpu.VMEM((7, 96, 128), F32),
            pltpu.VMEM((requests, window, cached), BF),
            pltpu.VMEM((requests, window, cached), BF),
            pltpu.SemaphoreType.DMA((requests, window // CHUNK, 2)),
        ],
        compiler_params=params(57),
        name="attention",
    )(lengths, queries, pair_sums, cosine, sine, key_cache, value_cache)

    back = lax.all_to_all(attended, "gx", split_axis=0, concat_axis=0, tiled=True)
    middle = lax.dynamic_slice(middle_outliers, (me_x * OUTL,), (OUTL,))
    chosen = jnp.arange(columns, dtype=jnp.int32)[:, None] == middle[None, :]
    plain = jnp.where(jnp.any(chosen, axis=1), 0.0, 1.0).astype(BF)[None]
    chosen = jnp.pad(chosen.astype(BF), ((0, 0), (0, 128 - OUTL)))
    factors = jnp.concatenate([output_scale[None], output_float])
    back, chosen, plain, factors = lax.optimization_barrier((back, chosen, plain, factors))
    mine = pl.pallas_call(
        repack_kernel,
        out_shape=jax.ShapeDtypeStruct((96, columns), BF),
        scratch_shapes=[pltpu.VMEM((7, 128, 128), F32)],
        compiler_params=params(8),
        name="repack",
    )(back)
    blocks = [mine] + [lax.ppermute(mine, "gy", over_y(d)) for d in (1, 2, 3)]
    blocks = blocks + [lax.ppermute(b, "gy", SIBLING) for b in blocks]

    half_rows = block_rows // 2

    def project(sending):
        return pl.pallas_call(
            functools.partial(output_kernel, sending),
            in_specs=[vmem] * 12,
            out_specs=vmem,
            out_shape=jax.ShapeDtypeStruct((4, 4 * half_rows, out_columns), BF),
            scratch_shapes=[
                pltpu.VMEM((tokens, columns), BF),
                pltpu.VMEM((15, tokens // 2, 128), F32),
            ],
            compiler_params=params(24),
            name="output_sent" if sending else "output_kept",
        )(*blocks, chosen, plain, factors, output_int.T)

    other = lax.ppermute(project(True), "gy", SIBLING)
    kept = project(False)
    steps = (1, 3, 2)
    got = [
        lax.ppermute(jnp.stack([kept[d], other[d]]), plane, shift_plane(False, d)) for d in steps
    ]
    quarter = jax.ShapeDtypeStruct((2, half_rows, out_columns), BF)
    sums = pl.pallas_call(
        first_sum_kernel,
        grid=(1,),
        in_specs=[whole((1, 4 * half_rows, out_columns))] * 2 + [vmem] * 3,
        out_specs=[vmem] * 4,
        out_shape=[quarter] * 4,
        compiler_params=params(16),
        name="first_sum",
    )(kept, other, *got)
    got = [lax.ppermute(sums[f], plane, shift_plane(True, f)) for f in steps]
    half = jax.ShapeDtypeStruct((half_rows, out_columns), BF)
    keep, send = pl.pallas_call(
        last_sum_kernel, out_shape=[half] * 2, compiler_params=params(8), name="last_sum"
    )(sums[0], *got)
    return pl.pallas_call(
        join_kernel,
        out_shape=jax.ShapeDtypeStruct((block_rows, out_columns), BF),
        compiler_params=params(8),
        name="join",
    )(keep, lax.ppermute(send, "gy", SIBLING))


def solution(mesh):
    placed = (
        P("gx", "gy"),
        P("gy"),
        P("gy"),
        P("gy"),
        P("gy", "gx"),
        P("gx"),
        P("gy", None),
        P(),
        P("gy", "gx"),
        P("gy", None),
        P(("gx", "gy"), None, None),
        P(("gx", "gy"), None, None),
        P(("gx", "gy")),
        P(),
        P("gx", "gy"),
        P("gy"),
        P("gx", "gy"),
    )
    return jax.shard_map(
        on_device, mesh=mesh, in_specs=placed, out_specs=P("gx", "gy"), check_vma=False
    )
```

```python
import functools
import math

import jax
import jax.numpy as jnp
from jax import lax
from jax.experimental import pallas as pl
from jax.experimental.pallas import tpu as pltpu
from jax.sharding import PartitionSpec as P

D = 14848
HEAD = 64
KV = 8
GROUP = 28
OUTL = 4
NEW = 2
N_Y = 4
LOCAL_HEADS = 14
CHUNK = 512

epsilon = 1e-05
rope_base = 10000.0
BF = jnp.bfloat16
F32 = jnp.float32
MIB = 1024 * 1024
STEPS = (0, 1, 3, 2)
NT = (((1,), (1,)), ((), ()))


def lanes_of(columns):
    return [(n, slice(128 * n, min(128 * n + 128, columns))) for n in range((columns + 127) // 128)]


def put(ref, rows, values):
    for n, lanes in lanes_of(values.shape[1]):
        ref[n, rows, 0 : lanes.stop - lanes.start] = values[:, lanes]


def whole(shape):
    return pl.BlockSpec(shape, lambda *_: (0,) * len(shape))


def here():
    i = lax.axis_index("gx")
    j = lax.axis_index("gy")
    return lax.div(j, 2), lax.rem(j, 2), lax.div(i, 4), lax.rem(i, 4)


def prepare_kernel(positions, x, own, keep, send):
    rows, features = x.shape
    place = lax.broadcasted_iota(jnp.int32, (features, 128), 0)
    column = lax.broadcasted_iota(jnp.int32, (features, 128), 1)
    picked = (place == positions[0]) & (column == 0)
    for k in range(1, OUTL):
        picked = picked | ((place == positions[k]) & (column == k))
    picked = picked.astype(F32).astype(BF)
    outlier = jnp.dot(x[...], picked, preferred_element_type=F32)
    values = x[...].astype(F32)
    own[:, 0:features] = x[...]
    own[:, features:] = outlier[:, 0:64].astype(BF)
    half = rows // 2
    first = here()[1] == 0
    for out, flag in ((keep, first), (send, jnp.logical_not(first))):
        out[:, 0:features] = jnp.where(flag, values[0:half], values[half:]).astype(BF)
        out[:, features:] = jnp.where(flag, outlier[0:half, 0:64], outlier[half:, 0:64]).astype(BF)


def diagonal(size):
    return lax.broadcasted_iota(jnp.int32, (size, size), 0) == lax.broadcasted_iota(
        jnp.int32, (size, size), 1
    )


def sums_kernel(both, out):
    features = both.shape[2] - 64
    rows = both.shape[1]
    first = jnp.zeros((rows, 1), F32)
    second = jnp.zeros((rows, 1), F32)
    for part in range(2):
        values = both[part, :, 0:features].astype(F32)
        first = first + jnp.sum(values, axis=1, keepdims=True)
        second = second + jnp.sum(values * values, axis=1, keepdims=True)
    unit = diagonal(rows)
    first = jnp.sum(jnp.where(unit, first, 0.0), axis=0, keepdims=True)
    second = jnp.sum(jnp.where(unit, second, 0.0), axis=0, keepdims=True)
    for n in range(16):
        out[n, 0:1, :] = first
        out[n, 1:2, :] = second


def moments(sums):
    unit = diagonal(sums.shape[1])
    average = jnp.sum(jnp.where(unit, sums[0:1, :], 0.0), axis=1, keepdims=True) / D
    squares = jnp.sum(jnp.where(unit, sums[1:2, :], 0.0), axis=1, keepdims=True) / D
    return average, lax.rsqrt(squares - average * average + epsilon)


def normalize(rows, average, inverse, gain, bias, gain_out, bias_out, features):
    regular = ((rows[:, 0:features].astype(F32) - average) * inverse * gain + bias).astype(BF)
    outlier = (rows[:, features : features + OUTL].astype(F32) - average) * inverse * gain_out + bias_out
    return regular, outlier.astype(BF).astype(F32)


def pair_kernel(own, mine, other, gain, bias, gain_out, bias_out, scale, extra, weight, out):
    _, c, z, x = here()
    features = weight.shape[0]
    half = own.shape[0] // 2
    first = c == 0
    mine_at = mine[jnp.where(first, z, x)]
    other_at = other[jnp.where(first, x, z)]
    average0, inverse0 = moments(jnp.where(first, mine_at, other_at))
    average1, inverse1 = moments(jnp.where(first, other_at, mine_at))
    average = jnp.concatenate([average0[0:half], average1[0:half]], axis=0)
    inverse = jnp.concatenate([inverse0[0:half], inverse1[0:half]], axis=0)
    regular, outlier = normalize(
        own[...], average, inverse, gain[...], bias[...], gain_out[...], bias_out[...], features
    )
    term = jnp.dot(regular, weight[...], preferred_element_type=F32) * scale[...]
    for k in range(OUTL):
        term = term + outlier[:, k : k + 1] * extra[k : k + 1, :]
    for j in range(2 * N_Y):
        rows = slice(6 * j, 6 * j + 6)
        out[j, 0:6, :] = term[rows, 0:896]
        out[j, 6:8, :] = jnp.zeros((2, 896), F32)
        for t in range(6):
            out[j, 6:7, 128 * t : 128 * t + 128] = term[6 * j + t : 6 * j + t + 1, 896:1024]


def query_kernel(
    a0, a1, a2, a3, b0, b1, b2, b3, mine, other, gain, bias, gain_out, bias_out,
    scale, extra, weight, pairs, keep, send, acc,
):
    y, c, z, x = here()
    features = weight.shape[0]
    for d2, (near, far) in enumerate(((a0, b0), (a1, b1), (a2, b2), (a3, b3))):
        regulars = []
        outliers = []
        for side, rows in enumerate((near[0], far[...])):
            sums = (mine, other)[side][lax.rem(jnp.where((c == 0) == (side == 0), z, x) + 4 - d2, 4)]
            average, inverse = moments(sums)
            regular, outlier = normalize(
                rows, average, inverse, gain[...], bias[...], gain_out[...], bias_out[...], features
            )
            regulars.append(regular)
            outliers.append(outlier)
        rows = jnp.concatenate(regulars, axis=0)
        value = jnp.concatenate(outliers, axis=0)
        term = jnp.dot(rows, weight[...], preferred_element_type=F32) * scale[...]
        for k in range(OUTL):
            term = term + value[:, k : k + 1] * extra[k : k + 1, :]
        for side in range(2):
            half = c if side == 0 else 1 - c
            for d1 in range(4):
                along_x = lax.rem(x + 4 - jnp.where(half == 0, STEPS[d1], d2), 4)
                along_z = lax.rem(z + 4 - jnp.where(half == 0, d2, STEPS[d1]), 4)
                at = pl.multiple_of((along_z * 4 + along_x) * 48 + half * 24, 8)
                row = side * 96 + d1 * 24
                put(acc, pl.ds(at, 24), term[row : row + 24, :])
    for out, core in ((keep, c), (send, 1 - c)):
        for d in range(N_Y):
            j = 2 * lax.rem(y + d, N_Y) + core
            for k in range(6):
                for n, lanes in lanes_of(896):
                    out[d, 16 * k : 16 * k + 16, lanes] = acc[n, pl.ds(6 * j + k, 16, stride=48), :].astype(BF)
            out[d, 96:104, :] = pairs[j].astype(BF)


def add_kernel(keep, received, o0, o1, o2, o3):
    for d, out in enumerate((o0, o1, o2, o3)):
        out[...] = (keep[d].astype(F32) + received[d].astype(F32)).astype(BF)


def collect_kernel(a, b, c, d, query_out, pair_out, acc):
    total = (a[...].astype(F32) + b[...].astype(F32)) + (c[...].astype(F32) + d[...].astype(F32))
    put(acc, slice(0, 104), total)
    for i in range(16):
        for n, lanes in lanes_of(896):
            query_out[i, :, lanes] = acc[n, pl.ds(i, 6, stride=16), :].astype(BF)
    pair_out[0:6, :] = total[96:102, 0:512]
    pair_out[6:12, 0:384] = total[96:102, 512:896]
    for t in range(6):
        pair_out[6 + t : 7 + t, 384:512] = total[102:103, 128 * t : 128 * t + 128]
    pair_out[12:16, :] = jnp.zeros((4, 512), F32)


def rotate_lanes(values, cosine, sine):
    lane = lax.broadcasted_iota(jnp.int32, values.shape, 1)
    partner = jnp.where(
        lane % 64 < 32, pltpu.roll(values, 96, axis=1), pltpu.roll(values, 32, axis=1)
    )
    return values * cosine + partner * sine


def attend_kernel(
    lengths, queries, pairs, cosine, sine, keys, values, out,
    staged, rotated, fresh_key, fresh_value, blocks, mixture, result, key_buf, value_buf, sems,
):
    requests = keys.shape[0]
    window = keys.shape[1]

    def fetch(r, n, which):
        source, target = ((keys, key_buf), (values, value_buf))[which]
        rows = pl.ds(pl.multiple_of(n * CHUNK, CHUNK), CHUNK)
        return pltpu.make_async_copy(source.at[r, rows], target.at[r, rows], sems.at[r, n, which])

    for r in range(requests):
        for n in range(window // CHUNK):

            @pl.when(lengths[r] > n * CHUNK)
            def _():
                fetch(r, n, 0).start()
                fetch(r, n, 1).start()

    for i in range(16):
        put(staged, slice(8 * i, 8 * i + 6), queries[i].astype(F32))
    for k in range(6):
        for col in range(7):
            lanes = slice(128 * col, 128 * col + 128)
            part = staged[col, pl.ds(k, 16, stride=8), :]
            turned = rotate_lanes(part, cosine[k : k + 1, :], sine[k : k + 1, :])
            rotated[16 * k : 16 * k + 16, lanes] = turned.astype(BF).astype(F32) * 0.125
    fresh_key[...] = jnp.zeros_like(fresh_key)
    fresh_value[...] = jnp.zeros_like(fresh_value)
    rounded = pairs[...].astype(BF).astype(F32)
    for col in range(4):
        lanes = slice(128 * col, 128 * col + 128)
        fresh_key[0:6, lanes] = rotate_lanes(rounded[0:6, lanes], cosine[0:6, :], sine[0:6, :])
    fresh_value[0:6, :] = rounded[6:12, :]

    sub = lax.broadcasted_iota(jnp.int32, (8, 256), 0)
    lane = lax.broadcasted_iota(jnp.int32, (8, 256), 1)
    own = sub // 2 == lane // 64
    low = lax.broadcasted_iota(jnp.int32, (8, 128), 1) < 64
    rows = LOCAL_HEADS * 16
    row = lax.broadcasted_iota(jnp.int32, (rows, 128), 0)
    column = lax.broadcasted_iota(jnp.int32, (rows, 128), 1)
    causal = column % 2 <= (row // 8) % 2
    place = lax.broadcasted_iota(jnp.int32, (rows, CHUNK), 1)

    starts = []
    for r in range(requests):
        state = []
        for g in range(2):
            for t in range(NEW):
                start = (NEW * r + t) * 16 + 8 * g
                for col in range(7):
                    part = rotated[start : start + 8, 128 * col : 128 * col + 128]
                    other = pltpu.roll(part, 64, axis=1)
                    for half in range(2):
                        both = jnp.where(low, part, other) if half == 0 else jnp.where(low, other, part)
                        both = jnp.concatenate([both, both], axis=1)
                        at = (2 * col + half) * 16 + t * 8
                        blocks[2 * r + g, at : at + 8, :] = jnp.where(own, both, 0.0)
            side = slice(256 * g, 256 * g + 256)
            query = blocks[2 * r + g].astype(BF)
            scores = lax.dot_general(query, fresh_key[:, side].astype(BF), NT, preferred_element_type=F32)
            scores = jnp.where(causal & (column // 2 == r), scores, -jnp.inf)
            top = jnp.max(scores, axis=1, keepdims=True)
            prob = jnp.exp(scores - top)
            total = jnp.sum(prob, axis=1, keepdims=True)
            mixture[2 * r + g] = jnp.dot(
                prob.astype(BF), fresh_value[:, side].astype(BF), preferred_element_type=F32
            )
            state.append((top, total))
        starts.append(tuple(state))

    for r in range(requests):
        length = lengths[r]

        def body(n, state):
            at = pl.multiple_of(n * CHUNK, CHUNK)
            active = place < length - at
            fetch(r, n, 0).wait()
            fetch(r, n, 1).wait()
            new = []
            for g in range(2):
                top, total = state[g]
                side = slice(256 * g, 256 * g + 256)
                key = key_buf[r, pl.ds(at, CHUNK), side]
                value = value_buf[r, pl.ds(at, CHUNK), side]
                query = blocks[2 * r + g].astype(BF)
                scores = lax.dot_general(query, key, NT, preferred_element_type=F32)
                scores = jnp.where(active, scores, -jnp.inf)
                higher = jnp.maximum(top, jnp.max(scores, axis=1, keepdims=True))
                shrink = jnp.exp(top - higher)
                prob = jnp.exp(scores - higher)
                total = total * shrink + jnp.sum(prob, axis=1, keepdims=True)
                mixture[2 * r + g] = mixture[2 * r + g] * shrink + jnp.dot(
                    prob.astype(BF), value, preferred_element_type=F32
                )
                new.append((higher, total))
            return tuple(new)

        state = lax.fori_loop(0, (length + CHUNK - 1) // CHUNK, body, starts[r])
        for g in range(2):
            blocks[2 * r + g] = mixture[2 * r + g] / state[g][1]
            for t in range(NEW):
                start = (NEW * r + t) * 16 + 8 * g
                for col in range(7):
                    folded = []
                    for half in range(2):
                        at = (2 * col + half) * 16 + t * 8
                        part = jnp.where(own, blocks[2 * r + g, at : at + 8, :], 0.0)
                        part = part[:, 0:128] + part[:, 128:256]
                        folded.append(part + pltpu.roll(part, 64, axis=1))
                    result[col, start : start + 8, :] = jnp.where(low, folded[0], folded[1])
    for i in range(16):
        for n, lanes in lanes_of(896):
            out[i, :, lanes] = result[n, pl.ds(i, 6, stride=16), :].astype(BF)


def repack_kernel(block, out, staged):
    for i in range(16):
        put(staged, slice(8 * i, 8 * i + 6), block[i].astype(F32))
    for k in range(6):
        for n, lanes in lanes_of(896):
            out[16 * k : 16 * k + 16, lanes] = staged[n, pl.ds(k, 16, stride=8), :].astype(BF)


def output_kernel(
    sending, b0, b1, b2, b3, s0, s1, s2, s3, chosen, plain, scale, extra, weight, out, left, acc
):
    y, c, z, x = here()
    half = 1 - c if sending else c
    for blocks, core in (((b0, b1, b2, b3), c), ((s0, s1, s2, s3), 1 - c)):
        for d, block in enumerate(blocks):
            j = 2 * lax.rem(y + N_Y - d, N_Y) + core
            left[pl.ds(pl.multiple_of(96 * j, 96), 96), :] = block[...]
    step = 192
    for n in range(384 // step):
        part = left[pl.ds(pl.multiple_of(half * 384 + n * step, step), step), :]
        picked = jnp.dot(part, chosen[...], preferred_element_type=F32)
        term = lax.dot_general(part * plain[...], weight[...], NT, preferred_element_type=F32) * scale[...]
        for k in range(OUTL):
            term = term + picked[:, k : k + 1] * extra[k : k + 1, :]
        put(acc, slice(n * step, n * step + step), term)
    for d in range(4):
        owners = []
        for f in range(4):
            along_x = lax.rem(x + jnp.where(half == 0, f, d), 4)
            along_z = lax.rem(z + jnp.where(half == 0, d, f), 4)
            owners.append(along_z * 4 + along_x)
        for n, lanes in lanes_of(out.shape[2]):
            got = [acc[n, pl.ds(i, 24, stride=16), :] for i in owners]
            got = jnp.concatenate(got, axis=0).astype(BF)
            out[d, :, lanes] = got[:, 0 : lanes.stop - lanes.start]


def first_sum_kernel(mine, other, r1, r3, r2, o0, o1, o2, o3):
    for part, start in enumerate((mine, other)):
        total = start[0].astype(F32) + r1[part].astype(F32)
        total = total + (r3[part].astype(F32) + r2[part].astype(F32))
        for f, out in enumerate((o0, o1, o2, o3)):
            out[part] = total[24 * f : 24 * f + 24, :].astype(BF)


def last_sum_kernel(own, r1, r3, r2, keep, send):
    for part, out in enumerate((keep, send)):
        total = own[part].astype(F32) + r1[part].astype(F32)
        out[...] = (total + (r3[part].astype(F32) + r2[part].astype(F32))).astype(BF)


def join_kernel(mine, other, out):
    first = here()[1] == 0
    a = mine[...].astype(F32)
    b = other[...].astype(F32)
    joined = jnp.concatenate([jnp.where(first, a, b), jnp.where(first, b, a)], axis=0)
    out[...] = joined.astype(BF)


def params(mib=48):
    return pltpu.CompilerParams(vmem_limit_bytes=mib * MIB)


def over_y(shift):
    return [(2 * y + c, 2 * ((y + shift) % N_Y) + c) for y in range(N_Y) for c in range(2)]


def shift_plane(first, shift):
    pairs = []
    for z in range(4):
        for x in range(4):
            for j in range(2 * N_Y):
                if (j % 2 == 0) == first:
                    to = z * 4 + (x + shift) % 4
                else:
                    to = (z + shift) % 4 * 4 + x
                pairs.append(((z * 4 + x) * 2 * N_Y + j, to * 2 * N_Y + j))
    return pairs


def sheets():
    groups = []
    for first in (True, False):
        for fixed in range(4):
            group = []
            for moving in range(4):
                z, x = (moving, fixed) if first else (fixed, moving)
                for y in range(N_Y):
                    group.append((z * 4 + x) * 2 * N_Y + 2 * y + (0 if first else 1))
            groups.append(group)
    return groups


SIBLING = [(j, j ^ 1) for j in range(2 * N_Y)]


def on_device(
    activations,
    norm_gain,
    norm_bias,
    input_outliers,
    query_int,
    query_scale,
    keyvalue_int,
    keyvalue_scale,
    query_float,
    keyvalue_float,
    key_cache,
    value_cache,
    lengths,
    middle_outliers,
    output_int,
    output_scale,
    output_float,
):
    block_rows, features = activations.shape
    tokens = block_rows * 16
    columns = query_int.shape[1]
    out_columns = output_int.shape[1]
    me_x = lax.axis_index("gx")
    smem = pl.BlockSpec(memory_space=pltpu.SMEM)
    vmem = pl.BlockSpec(memory_space=pltpu.VMEM)

    picked = jnp.arange(features, dtype=jnp.int32)[:, None] == input_outliers[None, :]
    is_outlier = jnp.any(picked, axis=1)
    gain = jnp.where(is_outlier, 0.0, norm_gain)[None]
    bias = jnp.where(is_outlier, 0.0, norm_bias)[None]
    gain_out = jnp.sum(jnp.where(picked, norm_gain[:, None], 0.0), axis=0)[None]
    bias_out = jnp.sum(jnp.where(picked, norm_bias[:, None], 0.0), axis=0)[None]
    padded = features + 64
    own, kept, sent = pl.pallas_call(
        prepare_kernel,
        in_specs=[smem, vmem],
        out_specs=[vmem] * 3,
        out_shape=[
            jax.ShapeDtypeStruct((block_rows, padded), BF),
            jax.ShapeDtypeStruct((block_rows // 2, padded), BF),
            jax.ShapeDtypeStruct((block_rows // 2, padded), BF),
        ],
        compiler_params=params(8),
        name="prepare",
    )(input_outliers, activations)
    plane = ("gx", "gy")
    both = jnp.stack([kept, lax.ppermute(sent, "gy", SIBLING)])
    both = jnp.concatenate(
        [both] + [lax.ppermute(both, plane, shift_plane(True, d)) for d in (1, 3, 2)], axis=1
    )
    arrived = [both] + [lax.ppermute(both, plane, shift_plane(False, d)) for d in (1, 3, 2)]
    sums = pl.pallas_call(
        sums_kernel,
        out_shape=jax.ShapeDtypeStruct((16, 2, 96), F32),
        compiler_params=params(8),
        name="row_sums",
    )(both)
    sums = lax.all_to_all(
        sums, plane, split_axis=0, concat_axis=0, tiled=True, axis_index_groups=sheets()
    )
    mine = jnp.sum(sums.reshape(4, N_Y, 2, 96), axis=1)
    other = lax.ppermute(mine, "gy", SIBLING)
    *arrived, mine, other = lax.optimization_barrier((*arrived, mine, other))
    pairs = pl.pallas_call(
        pair_kernel,
        in_specs=[vmem] * 10,
        out_specs=vmem,
        out_shape=jax.ShapeDtypeStruct((2 * N_Y, 8, columns), F32),
        compiler_params=params(16),
        name="pair_projection",
    )(
        own, mine, other, gain, bias, gain_out, bias_out,
        keyvalue_scale[None], keyvalue_float, keyvalue_int,
    )
    others = [lax.ppermute(block[1], "gy", SIBLING) for block in arrived]
    order = (0, 1, 3, 2)
    arrived = [arrived[n] for n in order]
    others = [others[n] for n in order]

    keep, send = pl.pallas_call(
        query_kernel,
        grid=(1,),
        in_specs=[whole((1, 96, padded))] * 4 + [vmem] * 14,
        out_specs=[vmem] * 2,
        out_shape=[jax.ShapeDtypeStruct((N_Y, 104, columns), BF)] * 2,
        scratch_shapes=[pltpu.VMEM((7, tokens, 128), F32)],
        compiler_params=params(24),
        name="query_projection",
    )(
        *arrived, *others, mine, other, gain, bias, gain_out, bias_out,
        query_scale[None], query_float, query_int, pairs,
    )
    received = lax.ppermute(send, "gy", SIBLING)
    piece = jax.ShapeDtypeStruct((104, columns), BF)
    mine, to1, to2, to3 = pl.pallas_call(
        add_kernel, out_shape=[piece] * 4, compiler_params=params(8), name="add_cores"
    )(keep, received)
    from1 = lax.ppermute(to1, "gy", over_y(1))
    from3 = lax.ppermute(to3, "gy", over_y(3))
    from2 = lax.ppermute(to2, "gy", over_y(2))
    summed, pair_sums = pl.pallas_call(
        collect_kernel,
        out_shape=[
            jax.ShapeDtypeStruct((16, 6, columns), BF),
            jax.ShapeDtypeStruct((16, 512), F32),
        ],
        scratch_shapes=[pltpu.VMEM((7, 104, 128), F32)],
        compiler_params=params(8),
        name="collect",
    )(mine, from1, from2, from3)
    queries = lax.all_to_all(summed, "gx", split_axis=0, concat_axis=0, tiled=True)

    positions = (lengths[:, None] + jnp.arange(NEW, dtype=jnp.int32)[None, :]).reshape(6, 1)
    frequency = jnp.exp(jnp.arange(32, dtype=F32) * (-2.0 * math.log(rope_base) / HEAD))
    angles = positions.astype(F32) * frequency[None, :]
    cosine = jnp.tile(jnp.cos(angles), (1, 4))
    sine = jnp.sin(angles)
    sine = jnp.concatenate([-sine, sine, -sine, sine], axis=1)
    cosine = jnp.pad(cosine, ((0, 2), (0, 0)))
    sine = jnp.pad(sine, ((0, 2), (0, 0)))

    requests, window, cached = key_cache.shape
    hbm = pl.BlockSpec(memory_space=pltpu.HBM)
    attended = pl.pallas_call(
        attend_kernel,
        in_specs=[smem, vmem, vmem, vmem, vmem, hbm, hbm],
        out_specs=vmem,
        out_shape=jax.ShapeDtypeStruct((16, 6, columns), BF),
        scratch_shapes=[
            pltpu.VMEM((7, 128, 128), F32),
            pltpu.VMEM((96, columns), F32),
            pltpu.VMEM((128, cached), F32),
            pltpu.VMEM((128, cached), F32),
            pltpu.VMEM((6, 224, 256), F32),
            pltpu.VMEM((6, 224, 256), F32),
            pltpu.VMEM((7, 96, 128), F32),
            pltpu.VMEM((requests, window, cached), BF),
            pltpu.VMEM((requests, window, cached), BF),
            pltpu.SemaphoreType.DMA((requests, window // CHUNK, 2)),
        ],
        compiler_params=params(57),
        name="attention",
    )(lengths, queries, pair_sums, cosine, sine, key_cache, value_cache)

    back = lax.all_to_all(attended, "gx", split_axis=0, concat_axis=0, tiled=True)
    mine = pl.pallas_call(
        repack_kernel,
        out_shape=jax.ShapeDtypeStruct((96, columns), BF),
        scratch_shapes=[pltpu.VMEM((7, 128, 128), F32)],
        compiler_params=params(8),
        name="repack",
    )(back)
    blocks = [mine] + [lax.ppermute(mine, "gy", over_y(d)) for d in (1, 2, 3)]
    blocks = blocks + [lax.ppermute(b, "gy", SIBLING) for b in blocks]

    middle = lax.dynamic_slice(middle_outliers, (me_x * OUTL,), (OUTL,))
    chosen = jnp.arange(columns, dtype=jnp.int32)[:, None] == middle[None, :]
    plain = jnp.where(jnp.any(chosen, axis=1), 0.0, 1.0).astype(BF)[None]
    chosen = jnp.pad(chosen.astype(BF), ((0, 0), (0, 128 - OUTL)))
    half_rows = block_rows // 2

    def project(sending):
        return pl.pallas_call(
            functools.partial(output_kernel, sending),
            in_specs=[vmem] * 13,
            out_specs=vmem,
            out_shape=jax.ShapeDtypeStruct((4, 4 * half_rows, out_columns), BF),
            scratch_shapes=[
                pltpu.VMEM((tokens, columns), BF),
                pltpu.VMEM((15, tokens // 2, 128), F32),
            ],
            compiler_params=params(24),
            name="output_sent" if sending else "output_kept",
        )(*blocks, chosen, plain, output_scale[None], output_float, output_int.T)

    other = lax.ppermute(project(True), "gy", SIBLING)
    kept = project(False)
    steps = (1, 3, 2)
    got = [
        lax.ppermute(jnp.stack([kept[d], other[d]]), plane, shift_plane(False, d)) for d in steps
    ]
    quarter = jax.ShapeDtypeStruct((2, half_rows, out_columns), BF)
    sums = pl.pallas_call(
        first_sum_kernel,
        grid=(1,),
        in_specs=[whole((1, 4 * half_rows, out_columns))] * 2 + [vmem] * 3,
        out_specs=[vmem] * 4,
        out_shape=[quarter] * 4,
        compiler_params=params(16),
        name="first_sum",
    )(kept, other, *got)
    got = [lax.ppermute(sums[f], plane, shift_plane(True, f)) for f in steps]
    half = jax.ShapeDtypeStruct((half_rows, out_columns), BF)
    keep, send = pl.pallas_call(
        last_sum_kernel, out_shape=[half] * 2, compiler_params=params(8), name="last_sum"
    )(sums[0], *got)
    return pl.pallas_call(
        join_kernel,
        out_shape=jax.ShapeDtypeStruct((block_rows, out_columns), BF),
        compiler_params=params(8),
        name="join",
    )(keep, lax.ppermute(send, "gy", SIBLING))


def solution(mesh):
    placed = (
        P("gx", "gy"),
        P("gy"),
        P("gy"),
        P("gy"),
        P("gy", "gx"),
        P("gx"),
        P("gy", None),
        P(),
        P("gy", "gx"),
        P("gy", None),
        P(("gx", "gy"), None, None),
        P(("gx", "gy"), None, None),
        P(("gx", "gy")),
        P(),
        P("gx", "gy"),
        P("gy"),
        P("gx", "gy"),
    )
    return jax.shard_map(
        on_device, mesh=mesh, in_specs=placed, out_specs=P("gx", "gy"), check_vma=False
    )
```

```python
import functools
import math

import jax
import jax.numpy as jnp
from jax import lax
from jax.experimental import pallas as pl
from jax.experimental.pallas import tpu as pltpu
from jax.sharding import PartitionSpec as P

D = 14848
HEAD = 64
KV = 8
GROUP = 28
OUTL = 4
NEW = 2
N_Y = 4
LOCAL_HEADS = 14
CHUNK = 512

epsilon = 1e-05
rope_base = 10000.0
BF = jnp.bfloat16
F32 = jnp.float32
MIB = 1024 * 1024
STEPS = (0, 1, 3, 2)
NT = (((1,), (1,)), ((), ()))


def lanes_of(columns):
    return [(n, slice(128 * n, min(128 * n + 128, columns))) for n in range((columns + 127) // 128)]


def put(ref, rows, values):
    for n, lanes in lanes_of(values.shape[1]):
        ref[n, rows, 0 : lanes.stop - lanes.start] = values[:, lanes]


def whole(shape):
    return pl.BlockSpec(shape, lambda *_: (0,) * len(shape))


def here():
    i = lax.axis_index("gx")
    j = lax.axis_index("gy")
    return lax.div(j, 2), lax.rem(j, 2), lax.div(i, 4), lax.rem(i, 4)


def prepare_kernel(positions, x, own, keep, send):
    rows, features = x.shape
    place = lax.broadcasted_iota(jnp.int32, (features, 128), 0)
    column = lax.broadcasted_iota(jnp.int32, (features, 128), 1)
    picked = (place == positions[0]) & (column == 0)
    for k in range(1, OUTL):
        picked = picked | ((place == positions[k]) & (column == k))
    picked = picked.astype(F32).astype(BF)
    outlier = jnp.dot(x[...], picked, preferred_element_type=F32)
    values = x[...].astype(F32)
    own[:, 0:features] = x[...]
    own[:, features:] = outlier[:, 0:64].astype(BF)
    half = rows // 2
    first = here()[1] == 0
    for out, flag in ((keep, first), (send, jnp.logical_not(first))):
        out[:, 0:features] = jnp.where(flag, values[0:half], values[half:]).astype(BF)
        out[:, features:] = jnp.where(flag, outlier[0:half, 0:64], outlier[half:, 0:64]).astype(BF)


def diagonal(size):
    return lax.broadcasted_iota(jnp.int32, (size, size), 0) == lax.broadcasted_iota(
        jnp.int32, (size, size), 1
    )


def sums_kernel(both, out):
    features = both.shape[2] - 64
    rows = both.shape[1]
    first = jnp.zeros((rows, 1), F32)
    second = jnp.zeros((rows, 1), F32)
    for part in range(2):
        values = both[part, :, 0:features].astype(F32)
        first = first + jnp.sum(values, axis=1, keepdims=True)
        second = second + jnp.sum(values * values, axis=1, keepdims=True)
    unit = diagonal(rows)
    first = jnp.sum(jnp.where(unit, first, 0.0), axis=0, keepdims=True)
    second = jnp.sum(jnp.where(unit, second, 0.0), axis=0, keepdims=True)
    for n in range(16):
        out[n, 0:1, :] = first
        out[n, 1:2, :] = second


def moments(sums):
    unit = diagonal(sums.shape[1])
    average = jnp.sum(jnp.where(unit, sums[0:1, :], 0.0), axis=1, keepdims=True) / D
    squares = jnp.sum(jnp.where(unit, sums[1:2, :], 0.0), axis=1, keepdims=True) / D
    return average, lax.rsqrt(squares - average * average + epsilon)


def normalize(rows, average, inverse, gain, bias, gain_out, bias_out, features):
    regular = ((rows[:, 0:features].astype(F32) - average) * inverse * gain + bias).astype(BF)
    outlier = (rows[:, features : features + OUTL].astype(F32) - average) * inverse * gain_out + bias_out
    return regular, outlier.astype(BF).astype(F32)


def pair_kernel(own, mine, other, gain, bias, gain_out, bias_out, scale, extra, weight, out):
    _, c, z, x = here()
    features = weight.shape[0]
    half = own.shape[0] // 2
    first = c == 0
    mine_at = mine[jnp.where(first, z, x)]
    other_at = other[jnp.where(first, x, z)]
    average0, inverse0 = moments(jnp.where(first, mine_at, other_at))
    average1, inverse1 = moments(jnp.where(first, other_at, mine_at))
    average = jnp.concatenate([average0[0:half], average1[0:half]], axis=0)
    inverse = jnp.concatenate([inverse0[0:half], inverse1[0:half]], axis=0)
    regular, outlier = normalize(
        own[...], average, inverse, gain[...], bias[...], gain_out[...], bias_out[...], features
    )
    term = jnp.dot(regular, weight[...], preferred_element_type=F32) * scale[...]
    for k in range(OUTL):
        term = term + outlier[:, k : k + 1] * extra[k : k + 1, :]
    for j in range(2 * N_Y):
        rows = slice(6 * j, 6 * j + 6)
        out[j, 0:6, :] = term[rows, 0:896]
        out[j, 6:8, :] = jnp.zeros((2, 896), F32)
        for t in range(6):
            out[j, 6:7, 128 * t : 128 * t + 128] = term[6 * j + t : 6 * j + t + 1, 896:1024]


def query_kernel(
    a0, a1, a2, a3, b0, b1, b2, b3, mine, other, gain, bias, gain_out, bias_out,
    scale, extra, weight, pairs, keep, send, acc,
):
    y, c, z, x = here()
    features = weight.shape[0]
    for d2, (near, far) in enumerate(((a0, b0), (a1, b1), (a2, b2), (a3, b3))):
        regulars = []
        outliers = []
        for side, rows in enumerate((near[0], far[...])):
            sums = (mine, other)[side][lax.rem(jnp.where((c == 0) == (side == 0), z, x) + 4 - d2, 4)]
            average, inverse = moments(sums)
            regular, outlier = normalize(
                rows, average, inverse, gain[...], bias[...], gain_out[...], bias_out[...], features
            )
            regulars.append(regular)
            outliers.append(outlier)
        rows = jnp.concatenate(regulars, axis=0)
        value = jnp.concatenate(outliers, axis=0)
        term = jnp.dot(rows, weight[...], preferred_element_type=F32) * scale[...]
        for k in range(OUTL):
            term = term + value[:, k : k + 1] * extra[k : k + 1, :]
        for side in range(2):
            half = c if side == 0 else 1 - c
            for d1 in range(4):
                along_x = lax.rem(x + 4 - jnp.where(half == 0, STEPS[d1], d2), 4)
                along_z = lax.rem(z + 4 - jnp.where(half == 0, d2, STEPS[d1]), 4)
                at = pl.multiple_of((along_z * 4 + along_x) * 48 + half * 24, 8)
                row = side * 96 + d1 * 24
                put(acc, pl.ds(at, 24), term[row : row + 24, :])
    for out, core in ((keep, c), (send, 1 - c)):
        for d in range(N_Y):
            j = 2 * lax.rem(y + d, N_Y) + core
            for k in range(6):
                for n, lanes in lanes_of(896):
                    out[d, 16 * k : 16 * k + 16, lanes] = acc[n, pl.ds(6 * j + k, 16, stride=48), :].astype(BF)
            out[d, 96:104, :] = pairs[j].astype(BF)


def add_kernel(keep, received, o0, o1, o2, o3):
    for d, out in enumerate((o0, o1, o2, o3)):
        out[...] = (keep[d].astype(F32) + received[d].astype(F32)).astype(BF)


def collect_kernel(a, b, c, d, query_out, pair_out, acc):
    total = (a[...].astype(F32) + b[...].astype(F32)) + (c[...].astype(F32) + d[...].astype(F32))
    put(acc, slice(0, 104), total)
    for i in range(16):
        for n, lanes in lanes_of(896):
            query_out[i, :, lanes] = acc[n, pl.ds(i, 6, stride=16), :].astype(BF)
    pair_out[0:6, :] = total[96:102, 0:512]
    pair_out[6:12, 0:384] = total[96:102, 512:896]
    for t in range(6):
        pair_out[6 + t : 7 + t, 384:512] = total[102:103, 128 * t : 128 * t + 128]
    pair_out[12:16, :] = jnp.zeros((4, 512), F32)


def rotate_lanes(values, cosine, sine):
    lane = lax.broadcasted_iota(jnp.int32, values.shape, 1)
    partner = jnp.where(
        lane % 64 < 32, pltpu.roll(values, 96, axis=1), pltpu.roll(values, 32, axis=1)
    )
    return values * cosine + partner * sine


def attend_kernel(
    lengths, queries, pairs, cosine, sine, keys, values, out,
    staged, rotated, fresh_key, fresh_value, blocks, mixture, result, key_buf, value_buf, sems,
):
    requests = keys.shape[0]
    window = keys.shape[1]

    def fetch(r, n, which):
        source, target = ((keys, key_buf), (values, value_buf))[which]
        rows = pl.ds(pl.multiple_of(n * CHUNK, CHUNK), CHUNK)
        return pltpu.make_async_copy(source.at[r, rows], target.at[r, rows], sems.at[r, n, which])

    for r in range(requests):
        for n in range(window // CHUNK):

            @pl.when(lengths[r] > n * CHUNK)
            def _():
                fetch(r, n, 0).start()
                fetch(r, n, 1).start()

    for i in range(16):
        put(staged, slice(8 * i, 8 * i + 6), queries[i].astype(F32))
    for k in range(6):
        for col in range(7):
            lanes = slice(128 * col, 128 * col + 128)
            part = staged[col, pl.ds(k, 16, stride=8), :]
            turned = rotate_lanes(part, cosine[k : k + 1, :], sine[k : k + 1, :])
            rotated[16 * k : 16 * k + 16, lanes] = turned.astype(BF).astype(F32) * 0.125
    fresh_key[...] = jnp.zeros_like(fresh_key)
    fresh_value[...] = jnp.zeros_like(fresh_value)
    rounded = pairs[...].astype(BF).astype(F32)
    for col in range(4):
        lanes = slice(128 * col, 128 * col + 128)
        fresh_key[0:6, lanes] = rotate_lanes(rounded[0:6, lanes], cosine[0:6, :], sine[0:6, :])
    fresh_value[0:6, :] = rounded[6:12, :]

    sub = lax.broadcasted_iota(jnp.int32, (8, 256), 0)
    lane = lax.broadcasted_iota(jnp.int32, (8, 256), 1)
    own = sub // 2 == lane // 64
    low = lax.broadcasted_iota(jnp.int32, (8, 128), 1) < 64
    rows = LOCAL_HEADS * 16
    row = lax.broadcasted_iota(jnp.int32, (rows, 128), 0)
    column = lax.broadcasted_iota(jnp.int32, (rows, 128), 1)
    causal = column % 2 <= (row // 8) % 2
    place = lax.broadcasted_iota(jnp.int32, (rows, CHUNK), 1)

    starts = []
    for r in range(requests):
        state = []
        for g in range(2):
            for t in range(NEW):
                start = (NEW * r + t) * 16 + 8 * g
                for col in range(7):
                    part = rotated[start : start + 8, 128 * col : 128 * col + 128]
                    other = pltpu.roll(part, 64, axis=1)
                    for half in range(2):
                        both = jnp.where(low, part, other) if half == 0 else jnp.where(low, other, part)
                        both = jnp.concatenate([both, both], axis=1)
                        at = (2 * col + half) * 16 + t * 8
                        blocks[2 * r + g, at : at + 8, :] = jnp.where(own, both, 0.0)
            side = slice(256 * g, 256 * g + 256)
            query = blocks[2 * r + g].astype(BF)
            scores = lax.dot_general(query, fresh_key[:, side].astype(BF), NT, preferred_element_type=F32)
            scores = jnp.where(causal & (column // 2 == r), scores, -jnp.inf)
            top = jnp.max(scores, axis=1, keepdims=True)
            prob = jnp.exp(scores - top)
            total = jnp.sum(prob, axis=1, keepdims=True)
            mixture[2 * r + g] = jnp.dot(
                prob.astype(BF), fresh_value[:, side].astype(BF), preferred_element_type=F32
            )
            state.append((top, total))
        starts.append(tuple(state))

    for r in range(requests):
        length = lengths[r]

        def body(n, state):
            at = pl.multiple_of(n * CHUNK, CHUNK)
            active = place < length - at
            fetch(r, n, 0).wait()
            fetch(r, n, 1).wait()
            new = []
            for g in range(2):
                top, total = state[g]
                side = slice(256 * g, 256 * g + 256)
                key = key_buf[r, pl.ds(at, CHUNK), side]
                value = value_buf[r, pl.ds(at, CHUNK), side]
                query = blocks[2 * r + g].astype(BF)
                scores = lax.dot_general(query, key, NT, preferred_element_type=F32)
                scores = jnp.where(active, scores, -jnp.inf)
                higher = jnp.maximum(top, jnp.max(scores, axis=1, keepdims=True))
                shrink = jnp.exp(top - higher)
                prob = jnp.exp(scores - higher)
                total = total * shrink + jnp.sum(prob, axis=1, keepdims=True)
                mixture[2 * r + g] = mixture[2 * r + g] * shrink + jnp.dot(
                    prob.astype(BF), value, preferred_element_type=F32
                )
                new.append((higher, total))
            return tuple(new)

        state = lax.fori_loop(0, (length + CHUNK - 1) // CHUNK, body, starts[r])
        for g in range(2):
            blocks[2 * r + g] = mixture[2 * r + g] / state[g][1]
            for t in range(NEW):
                start = (NEW * r + t) * 16 + 8 * g
                for col in range(7):
                    folded = []
                    for half in range(2):
                        at = (2 * col + half) * 16 + t * 8
                        part = jnp.where(own, blocks[2 * r + g, at : at + 8, :], 0.0)
                        part = part[:, 0:128] + part[:, 128:256]
                        folded.append(part + pltpu.roll(part, 64, axis=1))
                    result[col, start : start + 8, :] = jnp.where(low, folded[0], folded[1])
    for i in range(16):
        for n, lanes in lanes_of(896):
            out[i, :, lanes] = result[n, pl.ds(i, 6, stride=16), :].astype(BF)


def repack_kernel(block, out, staged):
    for i in range(16):
        put(staged, slice(8 * i, 8 * i + 6), block[i].astype(F32))
    for k in range(6):
        for n, lanes in lanes_of(896):
            out[16 * k : 16 * k + 16, lanes] = staged[n, pl.ds(k, 16, stride=8), :].astype(BF)


def output_kernel(
    sending, b0, b1, b2, b3, s0, s1, s2, s3, chosen, plain, scale, extra, weight, out, left, acc
):
    y, c, z, x = here()
    half = 1 - c if sending else c
    for blocks, core in (((b0, b1, b2, b3), c), ((s0, s1, s2, s3), 1 - c)):
        for d, block in enumerate(blocks):
            j = 2 * lax.rem(y + N_Y - d, N_Y) + core
            left[pl.ds(pl.multiple_of(96 * j, 96), 96), :] = block[...]
    step = 192
    for n in range(384 // step):
        part = left[pl.ds(pl.multiple_of(half * 384 + n * step, step), step), :]
        picked = jnp.dot(part, chosen[...], preferred_element_type=F32)
        term = lax.dot_general(part * plain[...], weight[...], NT, preferred_element_type=F32) * scale[...]
        for k in range(OUTL):
            term = term + picked[:, k : k + 1] * extra[k : k + 1, :]
        put(acc, slice(n * step, n * step + step), term)
    for d in range(4):
        owners = []
        for f in range(4):
            along_x = lax.rem(x + jnp.where(half == 0, f, d), 4)
            along_z = lax.rem(z + jnp.where(half == 0, d, f), 4)
            owners.append(along_z * 4 + along_x)
        for n, lanes in lanes_of(out.shape[2]):
            got = [acc[n, pl.ds(i, 24, stride=16), :] for i in owners]
            got = jnp.concatenate(got, axis=0).astype(BF)
            out[d, :, lanes] = got[:, 0 : lanes.stop - lanes.start]


def first_sum_kernel(mine, other, r1, r3, r2, o0, o1, o2, o3):
    for part, start in enumerate((mine, other)):
        total = start[0].astype(F32) + r1[part].astype(F32)
        total = total + (r3[part].astype(F32) + r2[part].astype(F32))
        for f, out in enumerate((o0, o1, o2, o3)):
            out[part] = total[24 * f : 24 * f + 24, :].astype(BF)


def last_sum_kernel(own, r1, r3, r2, keep, send):
    for part, out in enumerate((keep, send)):
        total = own[part].astype(F32) + r1[part].astype(F32)
        out[...] = (total + (r3[part].astype(F32) + r2[part].astype(F32))).astype(BF)


def join_kernel(mine, other, out):
    first = here()[1] == 0
    a = mine[...].astype(F32)
    b = other[...].astype(F32)
    joined = jnp.concatenate([jnp.where(first, a, b), jnp.where(first, b, a)], axis=0)
    out[...] = joined.astype(BF)


def params(mib=48):
    return pltpu.CompilerParams(vmem_limit_bytes=mib * MIB)


def over_y(shift):
    return [(2 * y + c, 2 * ((y + shift) % N_Y) + c) for y in range(N_Y) for c in range(2)]


def shift_plane(first, shift):
    pairs = []
    for z in range(4):
        for x in range(4):
            for j in range(2 * N_Y):
                if (j % 2 == 0) == first:
                    to = z * 4 + (x + shift) % 4
                else:
                    to = (z + shift) % 4 * 4 + x
                pairs.append(((z * 4 + x) * 2 * N_Y + j, to * 2 * N_Y + j))
    return pairs


def sheets():
    groups = []
    for first in (True, False):
        for fixed in range(4):
            group = []
            for moving in range(4):
                z, x = (moving, fixed) if first else (fixed, moving)
                for y in range(N_Y):
                    group.append((z * 4 + x) * 2 * N_Y + 2 * y + (0 if first else 1))
            groups.append(group)
    return groups


SIBLING = [(j, j ^ 1) for j in range(2 * N_Y)]


def on_device(
    activations,
    norm_gain,
    norm_bias,
    input_outliers,
    query_int,
    query_scale,
    keyvalue_int,
    keyvalue_scale,
    query_float,
    keyvalue_float,
    key_cache,
    value_cache,
    lengths,
    middle_outliers,
    output_int,
    output_scale,
    output_float,
):
    block_rows, features = activations.shape
    tokens = block_rows * 16
    columns = query_int.shape[1]
    out_columns = output_int.shape[1]
    me_x = lax.axis_index("gx")
    smem = pl.BlockSpec(memory_space=pltpu.SMEM)
    vmem = pl.BlockSpec(memory_space=pltpu.VMEM)

    picked = jnp.arange(features, dtype=jnp.int32)[:, None] == input_outliers[None, :]
    is_outlier = jnp.any(picked, axis=1)
    gain = jnp.where(is_outlier, 0.0, norm_gain)[None]
    bias = jnp.where(is_outlier, 0.0, norm_bias)[None]
    gain_out = jnp.sum(jnp.where(picked, norm_gain[:, None], 0.0), axis=0)[None]
    bias_out = jnp.sum(jnp.where(picked, norm_bias[:, None], 0.0), axis=0)[None]
    padded = features + 64
    own, kept, sent = pl.pallas_call(
        prepare_kernel,
        in_specs=[smem, vmem],
        out_specs=[vmem] * 3,
        out_shape=[
            jax.ShapeDtypeStruct((block_rows, padded), BF),
            jax.ShapeDtypeStruct((block_rows // 2, padded), BF),
            jax.ShapeDtypeStruct((block_rows // 2, padded), BF),
        ],
        compiler_params=params(60),
        name="prepare",
    )(input_outliers, activations)
    plane = ("gx", "gy")
    both = jnp.stack([kept, lax.ppermute(sent, "gy", SIBLING)])
    both = jnp.concatenate(
        [both] + [lax.ppermute(both, plane, shift_plane(True, d)) for d in (1, 3, 2)], axis=1
    )
    arrived = [both] + [lax.ppermute(both, plane, shift_plane(False, d)) for d in (1, 3, 2)]
    sums = pl.pallas_call(
        sums_kernel,
        out_shape=jax.ShapeDtypeStruct((16, 2, 96), F32),
        compiler_params=params(8),
        name="row_sums",
    )(both)
    sums = lax.all_to_all(
        sums, plane, split_axis=0, concat_axis=0, tiled=True, axis_index_groups=sheets()
    )
    mine = jnp.sum(sums.reshape(4, N_Y, 2, 96), axis=1)
    other = lax.ppermute(mine, "gy", SIBLING)
    *arrived, mine, other = lax.optimization_barrier((*arrived, mine, other))
    pairs = pl.pallas_call(
        pair_kernel,
        in_specs=[vmem] * 10,
        out_specs=vmem,
        out_shape=jax.ShapeDtypeStruct((2 * N_Y, 8, columns), F32),
        compiler_params=params(16),
        name="pair_projection",
    )(
        own, mine, other, gain, bias, gain_out, bias_out,
        keyvalue_scale[None], keyvalue_float, keyvalue_int,
    )
    others = [lax.ppermute(block[1], "gy", SIBLING) for block in arrived]
    order = (0, 1, 3, 2)
    arrived = [arrived[n] for n in order]
    others = [others[n] for n in order]

    keep, send = pl.pallas_call(
        query_kernel,
        grid=(1,),
        in_specs=[whole((1, 96, padded))] * 4 + [vmem] * 14,
        out_specs=[vmem] * 2,
        out_shape=[jax.ShapeDtypeStruct((N_Y, 104, columns), BF)] * 2,
        scratch_shapes=[pltpu.VMEM((7, tokens, 128), F32)],
        compiler_params=params(24),
        name="query_projection",
    )(
        *arrived, *others, mine, other, gain, bias, gain_out, bias_out,
        query_scale[None], query_float, query_int, pairs,
    )
    received = lax.ppermute(send, "gy", SIBLING)
    piece = jax.ShapeDtypeStruct((104, columns), BF)
    mine, to1, to2, to3 = pl.pallas_call(
        add_kernel, out_shape=[piece] * 4, compiler_params=params(8), name="add_cores"
    )(keep, received)
    from1 = lax.ppermute(to1, "gy", over_y(1))
    from3 = lax.ppermute(to3, "gy", over_y(3))
    from2 = lax.ppermute(to2, "gy", over_y(2))
    summed, pair_sums = pl.pallas_call(
        collect_kernel,
        out_shape=[
            jax.ShapeDtypeStruct((16, 6, columns), BF),
            jax.ShapeDtypeStruct((16, 512), F32),
        ],
        scratch_shapes=[pltpu.VMEM((7, 104, 128), F32)],
        compiler_params=params(8),
        name="collect",
    )(mine, from1, from2, from3)
    queries = lax.all_to_all(summed, "gx", split_axis=0, concat_axis=0, tiled=True)

    positions = (lengths[:, None] + jnp.arange(NEW, dtype=jnp.int32)[None, :]).reshape(6, 1)
    frequency = jnp.exp(jnp.arange(32, dtype=F32) * (-2.0 * math.log(rope_base) / HEAD))
    angles = positions.astype(F32) * frequency[None, :]
    cosine = jnp.tile(jnp.cos(angles), (1, 4))
    sine = jnp.sin(angles)
    sine = jnp.concatenate([-sine, sine, -sine, sine], axis=1)
    cosine = jnp.pad(cosine, ((0, 2), (0, 0)))
    sine = jnp.pad(sine, ((0, 2), (0, 0)))

    requests, window, cached = key_cache.shape
    hbm = pl.BlockSpec(memory_space=pltpu.HBM)
    attended = pl.pallas_call(
        attend_kernel,
        in_specs=[smem, vmem, vmem, vmem, vmem, hbm, hbm],
        out_specs=vmem,
        out_shape=jax.ShapeDtypeStruct((16, 6, columns), BF),
        scratch_shapes=[
            pltpu.VMEM((7, 128, 128), F32),
            pltpu.VMEM((96, columns), F32),
            pltpu.VMEM((128, cached), F32),
            pltpu.VMEM((128, cached), F32),
            pltpu.VMEM((6, 224, 256), F32),
            pltpu.VMEM((6, 224, 256), F32),
            pltpu.VMEM((7, 96, 128), F32),
            pltpu.VMEM((requests, window, cached), BF),
            pltpu.VMEM((requests, window, cached), BF),
            pltpu.SemaphoreType.DMA((requests, window // CHUNK, 2)),
        ],
        compiler_params=params(57),
        name="attention",
    )(lengths, queries, pair_sums, cosine, sine, key_cache, value_cache)

    back = lax.all_to_all(attended, "gx", split_axis=0, concat_axis=0, tiled=True)
    mine = pl.pallas_call(
        repack_kernel,
        out_shape=jax.ShapeDtypeStruct((96, columns), BF),
        scratch_shapes=[pltpu.VMEM((7, 128, 128), F32)],
        compiler_params=params(8),
        name="repack",
    )(back)
    blocks = [mine] + [lax.ppermute(mine, "gy", over_y(d)) for d in (1, 2, 3)]
    blocks = blocks + [lax.ppermute(b, "gy", SIBLING) for b in blocks]

    middle = lax.dynamic_slice(middle_outliers, (me_x * OUTL,), (OUTL,))
    chosen = jnp.arange(columns, dtype=jnp.int32)[:, None] == middle[None, :]
    plain = jnp.where(jnp.any(chosen, axis=1), 0.0, 1.0).astype(BF)[None]
    chosen = jnp.pad(chosen.astype(BF), ((0, 0), (0, 128 - OUTL)))
    half_rows = block_rows // 2

    def project(sending):
        return pl.pallas_call(
            functools.partial(output_kernel, sending),
            in_specs=[vmem] * 13,
            out_specs=vmem,
            out_shape=jax.ShapeDtypeStruct((4, 4 * half_rows, out_columns), BF),
            scratch_shapes=[
                pltpu.VMEM((tokens, columns), BF),
                pltpu.VMEM((15, tokens // 2, 128), F32),
            ],
            compiler_params=params(24),
            name="output_sent" if sending else "output_kept",
        )(*blocks, chosen, plain, output_scale[None], output_float, output_int.T)

    other = lax.ppermute(project(True), "gy", SIBLING)
    kept = project(False)
    steps = (1, 3, 2)
    got = [
        lax.ppermute(jnp.stack([kept[d], other[d]]), plane, shift_plane(False, d)) for d in steps
    ]
    quarter = jax.ShapeDtypeStruct((2, half_rows, out_columns), BF)
    sums = pl.pallas_call(
        first_sum_kernel,
        grid=(1,),
        in_specs=[whole((1, 4 * half_rows, out_columns))] * 2 + [vmem] * 3,
        out_specs=[vmem] * 4,
        out_shape=[quarter] * 4,
        compiler_params=params(16),
        name="first_sum",
    )(kept, other, *got)
    got = [lax.ppermute(sums[f], plane, shift_plane(True, f)) for f in steps]
    half = jax.ShapeDtypeStruct((half_rows, out_columns), BF)
    keep, send = pl.pallas_call(
        last_sum_kernel, out_shape=[half] * 2, compiler_params=params(8), name="last_sum"
    )(sums[0], *got)
    return pl.pallas_call(
        join_kernel,
        out_shape=jax.ShapeDtypeStruct((block_rows, out_columns), BF),
        compiler_params=params(8),
        name="join",
    )(keep, lax.ppermute(send, "gy", SIBLING))


def solution(mesh):
    placed = (
        P("gx", "gy"),
        P("gy"),
        P("gy"),
        P("gy"),
        P("gy", "gx"),
        P("gx"),
        P("gy", None),
        P(),
        P("gy", "gx"),
        P("gy", None),
        P(("gx", "gy"), None, None),
        P(("gx", "gy"), None, None),
        P(("gx", "gy")),
        P(),
        P("gx", "gy"),
        P("gy"),
        P("gx", "gy"),
    )
    return jax.shard_map(
        on_device, mesh=mesh, in_specs=placed, out_specs=P("gx", "gy"), check_vma=False
    )
```
